32 devices in a mesh: gx: 4 (over y, x), gy: 8 (over z, core).
Axes of the slice: x: 2, y: 2, z: 4, core: 2. Of those that a mesh axis runs over, the one named last changes fastest.
Arguments:
- permeability: float32 [1, 16, 32, 1024], P(None, None, 'gx', 'gy'), may hold values from 0.2 to 5
- saturation: float32 [1, 16, 32, 1024], P(None, None, 'gx', 'gy'), may hold values from 0.1 to 0.9
- pressure_old: float32 [1, 16, 32, 1024], P(None, None, 'gx', 'gy'), may hold values from -6 to 6
- source: float32 [16, 32, 1024], P(None, 'gx', 'gy'), may hold values from -25 to 25
Outputs:
- pressure: float32 [1, 16, 32, 1024], P(None, None, 'gx', 'gy')
- saturation_new: float32 [1, 16, 32, 1024], P(None, None, 'gx', 'gy')
The draws below stay inside these ranges and needn't reach their ends.
All inputs are finite; a program needn't handle non-finite values.
Results may differ from the reference program's by a relative error of at most 0.0003.
Values sent between devices are 32-bit elements; how exact they have to be, the bound alone decides.
A program may use at most 64 MiB of HBM per device.

```python
import math
import jax
import jax.numpy as jnp
from jax import lax

SAMPLES = 1
NZ = 16
ITERS = 2
NX = 32
NY = 1024


def draw_source(key, part):
    across = jnp.arange(NX, dtype=jnp.float32) / max(NX - 1, 1)
    along = jnp.arange(NY, dtype=jnp.float32) / max(NY - 1, 1)
    growth = 3.0
    noise_field = jnp.clip(jax.random.normal(key, (NZ, NX, NY), jnp.float32), -5.0, 5.0)
    slope_factor = jnp.power(growth, across)[:, None] * jnp.power(growth, along)[None, :]
    return 0.5 * slope_factor[None] * noise_field


def levels(key, shape, shards, least, largest):
    def one(axis_at, shards_of):
        heights = jax.random.uniform(jax.random.fold_in(jax.random.fold_in(key, 6), axis_at), (shards_of,), jnp.float32, least / len(shards), largest / len(shards))
        return jnp.repeat(jnp.exp(heights), shape[axis_at] // shards_of).reshape((-1,) + (1,) * (len(shape) - axis_at - 1))

    loudness = one(*shards[0])
    for cut in shards[1:]:
        loudness = loudness * one(*cut)
    return loudness


def scatter_about(key, extent, deviation, reach, shards=(), kind=jnp.bfloat16):
    result = deviation * jax.random.normal(key, extent, jnp.float32)
    if shards:
        result = result * levels(key, extent, shards, -0.22, 0.18)
    return jnp.clip(result, -reach, reach).astype(kind)


def setup_inputs(seed: int = 0) -> dict:
    arg_keys = jax.random.split(jax.random.key(seed), 5)
    permeability = jnp.clip(jnp.exp(math.log(5.0) - 3.218876 * jax.random.uniform(arg_keys[0], (SAMPLES, NZ, NX, NY), jnp.float32) ** levels(arg_keys[0], (SAMPLES, NZ, NX, NY), ((2, 4), (3, 8)), -0.2, 0.2)), 0.2, 5.0)
    saturation = jnp.clip(0.1 + 0.79999997 * jax.random.uniform(arg_keys[1], (SAMPLES, NZ, NX, NY), jnp.float32) ** levels(arg_keys[1], (SAMPLES, NZ, NX, NY), ((2, 4), (3, 8)), -0.2, 0.2), 0.1, 0.9)
    pressure_old = scatter_about(arg_keys[2], (SAMPLES, NZ, NX, NY), 1.0, 6.0, ((2, 4), (3, 8)), jnp.float32)
    source = draw_source(jax.random.fold_in(arg_keys[4], 71), 0)
    return dict(permeability=permeability, saturation=saturation, pressure_old=pressure_old, source=source)


storage_term = 0.5
vertical_ratio = 0.1
step_ratio = 0.05
water_viscosity = 1.0
oil_viscosity = 2.0


def total_mobility(values):
    return values * values / water_viscosity + (1.0 - values) * (1.0 - values) / oil_viscosity


def water_fraction(values):
    return (values * values / water_viscosity) / total_mobility(values)


def neighbours(values, layout_axis):
    widths = [(0, 0)] * values.ndim
    widths[layout_axis] = (1, 1)
    padded = jnp.pad(values, widths)
    length = padded.shape[layout_axis]
    return lax.slice_in_dim(padded, 0, length - 1, axis=layout_axis), lax.slice_in_dim(padded, 1, length, axis=layout_axis)


def upper_part(values, layout_axis):
    length = values.shape[layout_axis]
    return lax.slice_in_dim(values, 1, length, axis=layout_axis)


def lower_part(values, layout_axis):
    length = values.shape[layout_axis]
    return lax.slice_in_dim(values, 0, length - 1, axis=layout_axis)


def coefficient(perm_left, perm_right, mobile_left, mobile_right, scaling):
    return scaling * (2.0 * perm_left * perm_right / (perm_left + perm_right)) * (0.5 * (mobile_left + mobile_right))


def face_terms(permeability, saturation):
    terms = []
    for layout_axis in (1, 2, 3):
        perm_left, perm_right = neighbours(permeability, layout_axis)
        sat_left, sat_right = neighbours(saturation, layout_axis)
        scaling = vertical_ratio if layout_axis == 1 else 1.0
        terms.append(coefficient(perm_left, perm_right, total_mobility(sat_left), total_mobility(sat_right), scaling))
    return terms


def divergence(flows):
    summed = None
    for layout_axis, flow in zip((1, 2, 3), flows):
        change = upper_part(flow, layout_axis) - lower_part(flow, layout_axis)
        summed = change if summed is None else summed + change
    return summed


def diagonal_of(terms):
    summed = storage_term
    for layout_axis, term in zip((1, 2, 3), terms):
        summed = summed + (upper_part(term, layout_axis) + lower_part(term, layout_axis))
    return summed


def fluxes(terms, values):
    flows = []
    for layout_axis, term in zip((1, 2, 3), terms):
        left_side, right_side = neighbours(values, layout_axis)
        flows.append(term * (left_side - right_side))
    return flows


def apply_operator(terms, values):
    return storage_term * values + divergence(fluxes(terms, values))


def sample_dot(former, latter):
    return jnp.sum(former * latter, axis=(1, 2, 3), keepdims=True)


def transport(flows, current, inflow_rate):
    fraction = water_fraction(current)
    water = []
    for layout_axis, flow in zip((1, 2, 3), flows):
        frac_left, frac_right = neighbours(fraction, layout_axis)
        water.append(flow * jnp.where(flow > 0.0, frac_left, frac_right))
    gained = jnp.maximum(inflow_rate, 0.0) + jnp.minimum(inflow_rate, 0.0) * fraction
    return current + step_ratio * (gained - divergence(water))


def reference(permeability, saturation, pressure_old, source):
    terms = face_terms(permeability, saturation)
    diagonal = diagonal_of(terms)
    inflow_rate = source[None]
    right_side = inflow_rate + storage_term * pressure_old
    solution = pressure_old
    residual = right_side - apply_operator(terms, solution)
    precond = residual / diagonal
    direction = precond
    energy_now = sample_dot(residual, precond)
    for sweep in range(ITERS):
        image_field = apply_operator(terms, direction)
        step_size = energy_now / sample_dot(direction, image_field)
        solution = solution + step_size * direction
        residual = residual - step_size * image_field
        precond = residual / diagonal
        energy_next = sample_dot(residual, precond)
        direction = precond + (energy_next / energy_now) * direction
        energy_now = energy_next
    flows = fluxes(terms, solution)
    current = saturation
    for sweep in range(2):
        current = transport(flows, current, inflow_rate)
    return solution, current
```

```python
import functools

import jax
import jax.numpy as jnp
from jax import lax
from jax.experimental import pallas as pl
from jax.experimental.pallas import tpu as pltpu
from jax.sharding import PartitionSpec as P

HALO = 4
STORAGE = 0.5
VERTICAL = 0.1
STEP = 0.05
WATER = 1.0
OIL = 2.0
MESH = pl.DeviceIdType.MESH


def iota(shape, dim):
    return lax.broadcasted_iota(jnp.int32, shape, dim)


class Field:
    def __init__(self, main, side):
        self.main, self.side = main, side

    def map(self, fn, *others):
        return Field(fn(self.main, *[o.main for o in others]), fn(self.side, *[o.side for o in others]))


def fmap(fn, first, *others):
    return first.map(fn, *others)


def row_roll(v, shift):
    axis = v.ndim - 2
    return pltpu.roll(v, shift % v.shape[axis], axis)


def lane_roll(v, shift):
    axis = v.ndim - 1
    shift = shift % v.shape[axis]
    return v if shift == 0 else pltpu.roll(v, shift, axis)


def x_next(f):
    return f.map(lambda v: row_roll(v, -1))


def x_prev(f):
    return f.map(lambda v: row_roll(v, 1))


def z_next(f):
    main = jnp.concatenate([f.main[1:], jnp.zeros_like(f.main[:1])], axis=0)
    width = 2 * HALO
    lanes = f.side.shape[1]
    side = jnp.where(iota(f.side.shape, 1) < lanes - width, lane_roll(f.side, -width), 0.0)
    return Field(main, side)


def z_prev(f):
    main = jnp.concatenate([jnp.zeros_like(f.main[:1]), f.main[:-1]], axis=0)
    width = 2 * HALO
    side = jnp.where(iota(f.side.shape, 1) >= width, lane_roll(f.side, width), 0.0)
    return Field(main, side)


def inserted(side, depth, lane_from, lane_to):
    return jnp.stack([lane_roll(side, lane_to - (2 * HALO * z + lane_from)) for z in range(depth)], axis=0)


def gathered(main, lane_from, lane_to, base):
    width = 2 * HALO
    lane = iota(base.shape, 1)
    for z in range(main.shape[0]):
        base = jnp.where(lane == width * z + lane_to, lane_roll(main[z], width * z + lane_to - lane_from), base)
    return base


def y_next_main(main, side):
    lanes = main.shape[2]
    return jnp.where(
        iota(main.shape, 2) == lanes - 1, inserted(side, main.shape[0], 0, lanes - 1), lane_roll(main, -1)
    )


def y_prev_main(main, side):
    return jnp.where(
        iota(main.shape, 2) == 0, inserted(side, main.shape[0], 2 * HALO - 1, 0), lane_roll(main, 1)
    )


def y_next(f):
    return Field(y_next_main(f.main, f.side), gathered(f.main, 0, 2 * HALO - 1, lane_roll(f.side, -1)))


def y_prev(f):
    return Field(
        y_prev_main(f.main, f.side), gathered(f.main, f.main.shape[2] - 1, 0, lane_roll(f.side, 1))
    )


def mobility(s):
    return s * s / WATER + (1.0 - s) * (1.0 - s) / OIL


def fraction(s):
    water = s * s / WATER
    return water / (water + (1.0 - s) * (1.0 - s) / OIL)


def coefficient(scaling):
    def fn(ka, kb, ma, mb):
        return (scaling * ka * kb / jnp.maximum(ka + kb, 1e-30)) * (ma + mb)

    return fn


NEXT = (z_next, x_next, y_next)
PREV = (z_prev, x_prev, y_prev)


def add(*terms):
    total = terms[0]
    for t in terms[1:]:
        total = total + t
    return total


def packed(own):
    depth, rows, lanes = own.shape
    width = 2 * HALO
    edge = jnp.where(iota(own.shape, 2) < HALO, own, lane_roll(own, width))
    block = iota((rows, lanes), 1) // width
    out = edge[0]
    for z in range(1, depth):
        out = jnp.where(block == z, lane_roll(edge[z], width * z), out)
    return out


def kernel(nx, ny, k_in, s_in, x_in, q_in, p_out, s_out, main_ref, pack_ref, side_ref, part_x, part_y,
           load_sem, xsend, xrecv, psend, precv, rxsend, rxrecv, rysend, ryrecv):
    gx, gy = lax.axis_index("gx"), lax.axis_index("gy")
    ins = (k_in, s_in, x_in, q_in)
    rows = k_in.shape[1]
    wide = rows + 2 * HALO

    def has(dx, dy):
        ok = None
        for d, at, n in ((dx, gx, nx), (dy, gy, ny)):
            if d:
                one = at + d >= 0 if d < 0 else at + d < n
                ok = one if ok is None else ok & one
        return ok

    def at(dx, dy):
        return {"gx": gx + dx, "gy": gy + dy}

    diagonals = [(dx, dy) for dx in (-1, 1) for dy in (-1, 1)]

    loads = [pltpu.make_async_copy(ref, main_ref.at[i, :, pl.ds(0, rows)], load_sem.at[i]) for i, ref in enumerate(ins)]
    for copy in loads:
        copy.start()

    barrier = pltpu.get_barrier_semaphore()
    expected = jnp.int32(nx - 1 + ny - 1)
    for off in range(1, nx):
        pl.semaphore_signal(barrier, inc=1, device_id={"gx": lax.rem(gx + off, nx), "gy": gy}, device_id_type=MESH)
    for off in range(1, ny):
        pl.semaphore_signal(barrier, inc=1, device_id={"gx": gx, "gy": lax.rem(gy + off, ny)}, device_id_type=MESH)
    for dx, dy in diagonals:
        @pl.when(has(dx, dy))
        def _():
            pl.semaphore_signal(barrier, inc=1, device_id=at(dx, dy), device_id_type=MESH)

        expected = expected + has(dx, dy).astype(jnp.int32)

    def edge_rows(dx):
        return pl.ds(0, HALO) if dx < 0 else pl.ds(rows - HALO, HALO)

    def halo_rows(dx):
        return pl.ds(rows, HALO) if dx < 0 else pl.ds(rows + HALO, HALO)

    def x_copies(dx):
        d = (dx + 1) // 2
        return [
            pltpu.make_async_remote_copy(
                src_ref=ref.at[:, edge_rows(dx)],
                dst_ref=main_ref.at[i, :, halo_rows(dx)],
                send_sem=xsend.at[d * len(ins) + i],
                recv_sem=xrecv.at[d * len(ins) + i],
                device_id=at(dx, 0),
                device_id_type=MESH,
            )
            for i, ref in enumerate(ins)
        ]

    def y_copy(dx, dy):
        number = (dx + 1) * 2 + (dy + 1) // 2
        from_rows, to_rows = (edge_rows(dx), halo_rows(dx)) if dx else (pl.ds(0, rows), pl.ds(0, rows))
        return pltpu.make_async_remote_copy(
            src_ref=pack_ref.at[:, from_rows],
            dst_ref=side_ref.at[(1 - dy) // 2, :, to_rows],
            send_sem=psend.at[number],
            recv_sem=precv.at[number],
            device_id=at(dx, dy),
            device_id_type=MESH,
        )

    y_moves = [(0, 1), (0, -1)] + diagonals

    pl.semaphore_wait(barrier, expected)
    for dx in (-1, 1):
        @pl.when(has(dx, 0))
        def _():
            for copy in x_copies(dx):
                copy.start()

    for copy in loads:
        copy.wait()
    for i in range(len(ins)):
        pack_ref[i] = packed(main_ref[i, :, 0:rows, :])
    for dx, dy in y_moves:
        @pl.when(has(dx, dy))
        def _():
            y_copy(dx, dy).start()

    for dx in (-1, 1):
        @pl.when(has(-dx, 0))
        def _():
            for copy in x_copies(dx):
                copy.wait_recv()

    for dx, dy in y_moves:
        @pl.when(has(-dx, -dy))
        def _():
            y_copy(dx, dy).wait_recv()

    lanes = k_in.shape[2]
    depth = k_in.shape[0]
    row = iota((wide, lanes), 0)
    lane = iota((wide, lanes), 1)
    inside = (
        (row < rows)
        | ((row < rows + HALO) & (gx + 1 < nx))
        | ((row >= rows + HALO) & (gx > 0))
    )
    right = lane % (2 * HALO) < HALO
    inside_right = right & inside & (gy + 1 < ny)
    inside_left = jnp.logical_not(right) & inside & (gy > 0)

    def field(i):
        main = jnp.where(inside[None], main_ref[i], 0.0)
        side = jnp.where(inside_right, side_ref[1, i], jnp.where(inside_left, side_ref[0, i], 0.0))
        return Field(main, side)

    k, s, x0, q = (field(i) for i in range(4))
    mob = fmap(mobility, s)
    coefs = []
    for nxt, scaling in zip(NEXT, (VERTICAL, 1.0, 1.0)):
        coefs.append(fmap(coefficient(scaling), k, nxt(k), mob, nxt(mob)))
    before = [prv(c) for prv, c in zip(PREV, coefs)]
    diag = fmap(lambda *c: add(STORAGE, *c), *coefs, *before)
    inverse = fmap(lambda d: 1.0 / d, diag)

    def around(v):
        total = None
        for nxt, prv, c, b in zip(NEXT, PREV, coefs, before):
            term = fmap(lambda c, n, b, p: c * n + b * p, c, nxt(v), b, prv(v))
            total = term if total is None else fmap(jnp.add, total, term)
        return total

    def around_own(v):
        main, side = v.main, v.side[:rows]
        own = main[:, :rows]
        below = jnp.concatenate([own[1:], jnp.zeros_like(own[:1])], axis=0)
        above = jnp.concatenate([jnp.zeros_like(own[:1]), own[:-1]], axis=0)
        moved = (
            (below, above),
            (row_roll(main, -1)[:, :rows], row_roll(main, 1)[:, :rows]),
            (y_next_main(own, side), y_prev_main(own, side)),
        )
        return add(*[c.main[:, :rows] * n + b.main[:, :rows] * p for c, b, (n, p) in zip(coefs, before, moved)])

    r0 = fmap(lambda q, x, d, a: q + STORAGE * x - (d * x - a), q, x0, diag, around(x0))
    u0 = fmap(jnp.multiply, r0, inverse)
    v0 = fmap(lambda d, u, a: d * u - a, diag, u0, around(u0))
    u1 = fmap(jnp.multiply, v0, inverse)
    own_v1 = diag.main[:, :rows] * u1.main[:, :rows] - around_own(u1)

    def own(f):
        return f.main[:, :rows]

    pairs = ((own(r0), own(u0)), (own(u0), own(v0)), (own(v0), own(u1)), (own(u1), own_v1))
    tile_row = iota((rows, lanes), 0)
    part = jnp.zeros((rows, lanes), jnp.float32)
    for i, (left, other) in enumerate(pairs):
        part = jnp.where(tile_row == i, jnp.sum(jnp.sum(left * other, axis=0), axis=0, keepdims=True), part)

    def total_over(value, slots, name, me, n, send, recv):
        def copy(off, slot):
            target = lax.rem(me + off, n)
            return pltpu.make_async_remote_copy(
                src_ref=slots.at[slot], dst_ref=slots.at[slot], send_sem=send.at[off], recv_sem=recv.at[slot],
                device_id={"gx": gx, "gy": gy, name: target}, device_id_type=MESH,
            )

        slots[me] = value
        for off in range(1, n):
            copy(off, me).start()
        for off in range(1, n):
            copy(off, lax.rem(me + off, n)).wait_recv()
        for off in range(1, n):
            copy(off, me).wait_send()
        return add(*[slots[i] for i in range(n)])

    part = total_over(part, part_x, "gx", gx, nx, rxsend, rxrecv)
    part = total_over(part, part_y, "gy", gy, ny, rysend, ryrecv)
    sums = jnp.sum(part, axis=1, keepdims=True)
    sa, sb, sc, sd = (sums[i : i + 1, :] for i in range(4))
    step0 = sa / sb
    next_energy = step0 * step0 * sc - sa
    conjugacy = next_energy / sa
    curvature = sb - 2.0 * step0 * sc + step0 * step0 * sd
    step1 = next_energy / (curvature - conjugacy * next_energy / step0)
    weight0 = step0 + step1 * (1.0 + conjugacy)
    weight1 = -step1 * step0

    pressure = fmap(lambda x, a, b: x + weight0 * a + weight1 * b, x0, u0, u1)
    p_out[...] = own(pressure)
    flows = [fmap(lambda c, a, b: c * (a - b), c, pressure, nxt(pressure)) for nxt, c in zip(NEXT, coefs)]
    inject = fmap(lambda v: jnp.maximum(v, 0.0), q)
    produce = fmap(lambda v: jnp.minimum(v, 0.0), q)

    def transport(current):
        frac = fmap(fraction, current)
        total = fmap(lambda i, o, f: i + o * f, inject, produce, frac)
        for nxt, prv, flow in zip(NEXT, PREV, flows):
            water = fmap(lambda w, a, b: w * jnp.where(w > 0.0, a, b), flow, frac, nxt(frac))
            total = fmap(lambda t, w, p: t - (w - p), total, water, prv(water))
        return fmap(lambda c, t: c + STEP * t, current, total)

    s_out[...] = own(transport(transport(s)))

    for dx in (-1, 1):
        @pl.when(has(dx, 0))
        def _():
            for copy in x_copies(dx):
                copy.wait_send()

    for dx, dy in y_moves:
        @pl.when(has(dx, dy))
        def _():
            y_copy(dx, dy).wait_send()


def local(nx, ny, permeability, saturation, pressure_old, source):
    shape = source.shape
    depth, rows, lanes = shape
    assert permeability.shape[0] == 1 and depth * 2 * HALO == lanes and rows == 2 * HALO
    wide = rows + 2 * HALO
    f32 = jnp.float32
    dma = pltpu.SemaphoreType.DMA
    outs = pl.pallas_call(
        functools.partial(kernel, nx, ny),
        out_shape=[jax.ShapeDtypeStruct(shape, f32)] * 2,
        in_specs=[pl.BlockSpec(memory_space=pl.ANY)] * 4,
        out_specs=[pl.BlockSpec(memory_space=pltpu.VMEM)] * 2,
        scratch_shapes=[
            pltpu.VMEM((4, depth, wide, lanes), f32),
            pltpu.VMEM((4, rows, lanes), f32),
            pltpu.VMEM((2, 4, wide, lanes), f32),
            pltpu.VMEM((nx, rows, lanes), f32),
            pltpu.VMEM((ny, rows, lanes), f32),
            dma((4,)),
            dma((8,)),
            dma((8,)),
            dma((6,)),
            dma((6,)),
            dma((nx,)),
            dma((nx,)),
            dma((ny,)),
            dma((ny,)),
        ],
        compiler_params=pltpu.CompilerParams(
            collective_id=0, has_side_effects=True, vmem_limit_bytes=32 * 1024 * 1024
        ),
    )(permeability[0], saturation[0], pressure_old[0], source)
    return outs[0][None], outs[1][None]


def solution(mesh):
    wide = P(None, None, "gx", "gy")
    return jax.shard_map(
        functools.partial(local, mesh.shape["gx"], mesh.shape["gy"]),
        mesh=mesh,
        in_specs=(wide, wide, wide, P(None, "gx", "gy")),
        out_specs=(wide, wide),
        check_vma=False,
    )
```

```python
import functools

import jax
import jax.numpy as jnp
from jax import lax
from jax.experimental import pallas as pl
from jax.experimental.pallas import tpu as pltpu
from jax.sharding import PartitionSpec as P

HALO = 4
STORAGE = 0.5
VERTICAL = 0.1
STEP = 0.05
WATER = 1.0
OIL = 2.0
MESH = pl.DeviceIdType.MESH


def iota(shape, dim):
    return lax.broadcasted_iota(jnp.int32, shape, dim)


class Field:
    def __init__(self, main, side):
        self.main, self.side = main, side

    def map(self, fn, *others):
        return Field(fn(self.main, *[o.main for o in others]), fn(self.side, *[o.side for o in others]))


def fmap(fn, first, *others):
    return first.map(fn, *others)


def row_roll(v, shift):
    axis = v.ndim - 2
    return pltpu.roll(v, shift % v.shape[axis], axis)


def lane_roll(v, shift):
    axis = v.ndim - 1
    shift = shift % v.shape[axis]
    return v if shift == 0 else pltpu.roll(v, shift, axis)


def x_next(f):
    return f.map(lambda v: row_roll(v, -1))


def x_prev(f):
    return f.map(lambda v: row_roll(v, 1))


def z_next(f):
    main = jnp.concatenate([f.main[1:], jnp.zeros_like(f.main[:1])], axis=0)
    width = 2 * HALO
    lanes = f.side.shape[1]
    side = jnp.where(iota(f.side.shape, 1) < lanes - width, lane_roll(f.side, -width), 0.0)
    return Field(main, side)


def z_prev(f):
    main = jnp.concatenate([jnp.zeros_like(f.main[:1]), f.main[:-1]], axis=0)
    width = 2 * HALO
    side = jnp.where(iota(f.side.shape, 1) >= width, lane_roll(f.side, width), 0.0)
    return Field(main, side)


def inserted(side, depth, lane_from, lane_to):
    return jnp.stack([lane_roll(side, lane_to - (2 * HALO * z + lane_from)) for z in range(depth)], axis=0)


def gathered(main, lane_from, lane_to, base):
    width = 2 * HALO
    lane = iota(base.shape, 1)
    for z in range(main.shape[0]):
        base = jnp.where(lane == width * z + lane_to, lane_roll(main[z], width * z + lane_to - lane_from), base)
    return base


def y_next_main(main, side):
    lanes = main.shape[2]
    return jnp.where(
        iota(main.shape, 2) == lanes - 1, inserted(side, main.shape[0], 0, lanes - 1), lane_roll(main, -1)
    )


def y_prev_main(main, side):
    return jnp.where(
        iota(main.shape, 2) == 0, inserted(side, main.shape[0], 2 * HALO - 1, 0), lane_roll(main, 1)
    )


def y_next(f):
    return Field(y_next_main(f.main, f.side), gathered(f.main, 0, 2 * HALO - 1, lane_roll(f.side, -1)))


def y_prev(f):
    return Field(
        y_prev_main(f.main, f.side), gathered(f.main, f.main.shape[2] - 1, 0, lane_roll(f.side, 1))
    )


def inverted(v):
    r = pl.reciprocal(v, approx=True)
    r = r * (2.0 - v * r)
    return r * (2.0 - v * r)


def mobility(s):
    return s * s / WATER + (1.0 - s) * (1.0 - s) / OIL


def fraction(s):
    water = s * s / WATER
    return water * inverted(water + (1.0 - s) * (1.0 - s) / OIL)


def coefficient(scaling):
    def fn(ka, kb, ma, mb):
        return (scaling * ka * kb) * inverted(jnp.maximum(ka + kb, 1e-20)) * (ma + mb)

    return fn


NEXT = (z_next, x_next, y_next)
PREV = (z_prev, x_prev, y_prev)


def add(*terms):
    total = terms[0]
    for t in terms[1:]:
        total = total + t
    return total


def packed(own):
    depth, rows, lanes = own.shape
    width = 2 * HALO
    edge = jnp.where(iota(own.shape, 2) < HALO, own, lane_roll(own, width))
    block = iota((rows, lanes), 1) // width
    out = edge[0]
    for z in range(1, depth):
        out = jnp.where(block == z, lane_roll(edge[z], width * z), out)
    return out


def kernel(nx, ny, k_in, s_in, x_in, q_in, p_out, s_out, main_ref, pack_ref, side_ref, part_x, part_y,
           load_sem, xsend, xrecv, psend, precv, rxsend, rxrecv, rysend, ryrecv):
    gx, gy = lax.axis_index("gx"), lax.axis_index("gy")
    ins = (k_in, s_in, x_in, q_in)
    rows = k_in.shape[1]
    wide = rows + 2 * HALO

    def has(dx, dy):
        ok = None
        for d, at, n in ((dx, gx, nx), (dy, gy, ny)):
            if d:
                one = at + d >= 0 if d < 0 else at + d < n
                ok = one if ok is None else ok & one
        return ok

    def at(dx, dy):
        return {"gx": gx + dx, "gy": gy + dy}

    diagonals = [(dx, dy) for dx in (-1, 1) for dy in (-1, 1)]

    loads = [pltpu.make_async_copy(ref, main_ref.at[i, :, pl.ds(0, rows)], load_sem.at[i]) for i, ref in enumerate(ins)]
    for copy in loads:
        copy.start()

    barrier = pltpu.get_barrier_semaphore()
    expected = jnp.int32(nx - 1 + ny - 1)
    for off in range(1, nx):
        pl.semaphore_signal(barrier, inc=1, device_id={"gx": lax.rem(gx + off, nx), "gy": gy}, device_id_type=MESH)
    for off in range(1, ny):
        pl.semaphore_signal(barrier, inc=1, device_id={"gx": gx, "gy": lax.rem(gy + off, ny)}, device_id_type=MESH)
    for dx, dy in diagonals:
        @pl.when(has(dx, dy))
        def _():
            pl.semaphore_signal(barrier, inc=1, device_id=at(dx, dy), device_id_type=MESH)

        expected = expected + has(dx, dy).astype(jnp.int32)

    def edge_rows(dx):
        return pl.ds(0, HALO) if dx < 0 else pl.ds(rows - HALO, HALO)

    def halo_rows(dx):
        return pl.ds(rows, HALO) if dx < 0 else pl.ds(rows + HALO, HALO)

    def x_copies(dx):
        d = (dx + 1) // 2
        return [
            pltpu.make_async_remote_copy(
                src_ref=ref.at[:, edge_rows(dx)],
                dst_ref=main_ref.at[i, :, halo_rows(dx)],
                send_sem=xsend.at[d * len(ins) + i],
                recv_sem=xrecv.at[d * len(ins) + i],
                device_id=at(dx, 0),
                device_id_type=MESH,
            )
            for i, ref in enumerate(ins)
        ]

    def y_copy(dx, dy):
        number = (dx + 1) * 2 + (dy + 1) // 2
        from_rows, to_rows = (edge_rows(dx), halo_rows(dx)) if dx else (pl.ds(0, rows), pl.ds(0, rows))
        return pltpu.make_async_remote_copy(
            src_ref=pack_ref.at[:, from_rows],
            dst_ref=side_ref.at[(1 - dy) // 2, :, to_rows],
            send_sem=psend.at[number],
            recv_sem=precv.at[number],
            device_id=at(dx, dy),
            device_id_type=MESH,
        )

    y_moves = [(0, 1), (0, -1)] + diagonals

    pl.semaphore_wait(barrier, expected)
    for dx in (-1, 1):
        @pl.when(has(dx, 0))
        def _():
            for copy in x_copies(dx):
                copy.start()

    for copy in loads:
        copy.wait()
    for i in range(len(ins)):
        pack_ref[i] = packed(main_ref[i, :, 0:rows, :])
    for dx, dy in y_moves:
        @pl.when(has(dx, dy))
        def _():
            y_copy(dx, dy).start()

    for dx in (-1, 1):
        @pl.when(has(-dx, 0))
        def _():
            for copy in x_copies(dx):
                copy.wait_recv()

    for dx, dy in y_moves:
        @pl.when(has(-dx, -dy))
        def _():
            y_copy(dx, dy).wait_recv()

    lanes = k_in.shape[2]
    depth = k_in.shape[0]
    row = iota((wide, lanes), 0)
    lane = iota((wide, lanes), 1)
    inside = (
        (row < rows)
        | ((row < rows + HALO) & (gx + 1 < nx))
        | ((row >= rows + HALO) & (gx > 0))
    )
    right = lane % (2 * HALO) < HALO
    inside_right = right & inside & (gy + 1 < ny)
    inside_left = jnp.logical_not(right) & inside & (gy > 0)

    def field(i):
        main = jnp.where(inside[None], main_ref[i], 0.0)
        side = jnp.where(inside_right, side_ref[1, i], jnp.where(inside_left, side_ref[0, i], 0.0))
        return Field(main, side)

    k, s, x0, q = (field(i) for i in range(4))
    mob = fmap(mobility, s)
    coefs = []
    for nxt, scaling in zip(NEXT, (VERTICAL, 1.0, 1.0)):
        coefs.append(fmap(coefficient(scaling), k, nxt(k), mob, nxt(mob)))
    before = [prv(c) for prv, c in zip(PREV, coefs)]
    diag = fmap(lambda *c: add(STORAGE, *c), *coefs, *before)
    inverse = fmap(inverted, diag)

    def around(v):
        total = None
        for nxt, prv, c, b in zip(NEXT, PREV, coefs, before):
            term = fmap(lambda c, n, b, p: c * n + b * p, c, nxt(v), b, prv(v))
            total = term if total is None else fmap(jnp.add, total, term)
        return total

    def around_own(v):
        main, side = v.main, v.side[:rows]
        own = main[:, :rows]
        below = jnp.concatenate([own[1:], jnp.zeros_like(own[:1])], axis=0)
        above = jnp.concatenate([jnp.zeros_like(own[:1]), own[:-1]], axis=0)
        moved = (
            (below, above),
            (row_roll(main, -1)[:, :rows], row_roll(main, 1)[:, :rows]),
            (y_next_main(own, side), y_prev_main(own, side)),
        )
        return add(*[c.main[:, :rows] * n + b.main[:, :rows] * p for c, b, (n, p) in zip(coefs, before, moved)])

    r0 = fmap(lambda q, x, d, a: q + STORAGE * x - (d * x - a), q, x0, diag, around(x0))
    u0 = fmap(jnp.multiply, r0, inverse)
    v0 = fmap(lambda d, u, a: d * u - a, diag, u0, around(u0))
    u1 = fmap(jnp.multiply, v0, inverse)
    own_v1 = diag.main[:, :rows] * u1.main[:, :rows] - around_own(u1)

    def own(f):
        return f.main[:, :rows]

    pairs = ((own(r0), own(u0)), (own(u0), own(v0)), (own(v0), own(u1)), (own(u1), own_v1))
    tile_row = iota((rows, lanes), 0)
    part = jnp.zeros((rows, lanes), jnp.float32)
    for i, (left, other) in enumerate(pairs):
        part = jnp.where(tile_row == i, jnp.sum(jnp.sum(left * other, axis=0), axis=0, keepdims=True), part)

    def total_over(value, slots, name, me, n, send, recv):
        def copy(off, slot):
            target = lax.rem(me + off, n)
            return pltpu.make_async_remote_copy(
                src_ref=slots.at[slot], dst_ref=slots.at[slot], send_sem=send.at[off], recv_sem=recv.at[slot],
                device_id={"gx": gx, "gy": gy, name: target}, device_id_type=MESH,
            )

        slots[me] = value
        for off in range(1, n):
            copy(off, me).start()
        for off in range(1, n):
            copy(off, lax.rem(me + off, n)).wait_recv()
        for off in range(1, n):
            copy(off, me).wait_send()
        return add(*[slots[i] for i in range(n)])

    part = total_over(part, part_x, "gx", gx, nx, rxsend, rxrecv)
    part = total_over(part, part_y, "gy", gy, ny, rysend, ryrecv)
    sums = jnp.sum(part, axis=1, keepdims=True)
    sa, sb, sc, sd = (sums[i : i + 1, :] for i in range(4))
    step0 = sa / sb
    next_energy = step0 * step0 * sc - sa
    conjugacy = next_energy / sa
    curvature = sb - 2.0 * step0 * sc + step0 * step0 * sd
    step1 = next_energy / (curvature - conjugacy * next_energy / step0)
    weight0 = step0 + step1 * (1.0 + conjugacy)
    weight1 = -step1 * step0

    pressure = fmap(lambda x, a, b: x + weight0 * a + weight1 * b, x0, u0, u1)
    p_out[...] = own(pressure)
    flows = [fmap(lambda c, a, b: c * (a - b), c, pressure, nxt(pressure)) for nxt, c in zip(NEXT, coefs)]
    inject = fmap(lambda v: jnp.maximum(v, 0.0), q)
    produce = fmap(lambda v: jnp.minimum(v, 0.0), q)

    def transport(current):
        frac = fmap(fraction, current)
        total = fmap(lambda i, o, f: i + o * f, inject, produce, frac)
        for nxt, prv, flow in zip(NEXT, PREV, flows):
            water = fmap(lambda w, a, b: w * jnp.where(w > 0.0, a, b), flow, frac, nxt(frac))
            total = fmap(lambda t, w, p: t - (w - p), total, water, prv(water))
        return fmap(lambda c, t: c + STEP * t, current, total)

    s_out[...] = own(transport(transport(s)))

    for dx in (-1, 1):
        @pl.when(has(dx, 0))
        def _():
            for copy in x_copies(dx):
                copy.wait_send()

    for dx, dy in y_moves:
        @pl.when(has(dx, dy))
        def _():
            y_copy(dx, dy).wait_send()


def local(nx, ny, permeability, saturation, pressure_old, source):
    shape = source.shape
    depth, rows, lanes = shape
    assert permeability.shape[0] == 1 and depth * 2 * HALO == lanes and rows == 2 * HALO
    wide = rows + 2 * HALO
    f32 = jnp.float32
    dma = pltpu.SemaphoreType.DMA
    outs = pl.pallas_call(
        functools.partial(kernel, nx, ny),
        out_shape=[jax.ShapeDtypeStruct(shape, f32)] * 2,
        in_specs=[pl.BlockSpec(memory_space=pltpu.HBM)] * 4,
        out_specs=[pl.BlockSpec(memory_space=pltpu.VMEM)] * 2,
        scratch_shapes=[
            pltpu.VMEM((4, depth, wide, lanes), f32),
            pltpu.VMEM((4, rows, lanes), f32),
            pltpu.VMEM((2, 4, wide, lanes), f32),
            pltpu.VMEM((nx, rows, lanes), f32),
            pltpu.VMEM((ny, rows, lanes), f32),
            dma((4,)),
            dma((8,)),
            dma((8,)),
            dma((6,)),
            dma((6,)),
            dma((nx,)),
            dma((nx,)),
            dma((ny,)),
            dma((ny,)),
        ],
        compiler_params=pltpu.CompilerParams(
            collective_id=0, has_side_effects=True, vmem_limit_bytes=32 * 1024 * 1024
        ),
    )(*[pltpu.with_memory_space_constraint(v, pltpu.HBM) for v in (permeability[0], saturation[0], pressure_old[0], source)])
    return outs[0][None], outs[1][None]


def solution(mesh):
    wide = P(None, None, "gx", "gy")
    return jax.shard_map(
        functools.partial(local, mesh.shape["gx"], mesh.shape["gy"]),
        mesh=mesh,
        in_specs=(wide, wide, wide, P(None, "gx", "gy")),
        out_specs=(wide, wide),
        check_vma=False,
    )
```

```python
import functools

import jax
import jax.numpy as jnp
from jax import lax
from jax.experimental import pallas as pl
from jax.experimental.pallas import tpu as pltpu
from jax.sharding import PartitionSpec as P

HALO = 4
STORAGE = 0.5
VERTICAL = 0.1
STEP = 0.05
WATER = 1.0
OIL = 2.0
MESH = pl.DeviceIdType.MESH


def iota(shape, dim):
    return lax.broadcasted_iota(jnp.int32, shape, dim)


class Field:
    def __init__(self, main, side):
        self.main, self.side = main, side

    def map(self, fn, *others):
        return Field(fn(self.main, *[o.main for o in others]), fn(self.side, *[o.side for o in others]))


def fmap(fn, first, *others):
    return first.map(fn, *others)


def row_roll(v, shift):
    axis = v.ndim - 2
    return pltpu.roll(v, shift % v.shape[axis], axis)


def lane_roll(v, shift):
    axis = v.ndim - 1
    shift = shift % v.shape[axis]
    return v if shift == 0 else pltpu.roll(v, shift, axis)


def x_next(f):
    return f.map(lambda v: row_roll(v, -1))


def x_prev(f):
    return f.map(lambda v: row_roll(v, 1))


def z_next(f):
    main = jnp.concatenate([f.main[1:], jnp.zeros_like(f.main[:1])], axis=0)
    width = 2 * HALO
    lanes = f.side.shape[1]
    side = jnp.where(iota(f.side.shape, 1) < lanes - width, lane_roll(f.side, -width), 0.0)
    return Field(main, side)


def z_prev(f):
    main = jnp.concatenate([jnp.zeros_like(f.main[:1]), f.main[:-1]], axis=0)
    width = 2 * HALO
    side = jnp.where(iota(f.side.shape, 1) >= width, lane_roll(f.side, width), 0.0)
    return Field(main, side)


def inserted(side, depth, lane_from, lane_to):
    return jnp.stack([lane_roll(side, lane_to - (2 * HALO * z + lane_from)) for z in range(depth)], axis=0)


def gathered(main, lane_from, lane_to, base):
    width = 2 * HALO
    lane = iota(base.shape, 1)
    for z in range(main.shape[0]):
        base = jnp.where(lane == width * z + lane_to, lane_roll(main[z], width * z + lane_to - lane_from), base)
    return base


def y_next_main(main, side):
    lanes = main.shape[2]
    return jnp.where(
        iota(main.shape, 2) == lanes - 1, inserted(side, main.shape[0], 0, lanes - 1), lane_roll(main, -1)
    )


def y_prev_main(main, side):
    return jnp.where(
        iota(main.shape, 2) == 0, inserted(side, main.shape[0], 2 * HALO - 1, 0), lane_roll(main, 1)
    )


def y_next(f):
    return Field(y_next_main(f.main, f.side), gathered(f.main, 0, 2 * HALO - 1, lane_roll(f.side, -1)))


def y_prev(f):
    return Field(
        y_prev_main(f.main, f.side), gathered(f.main, f.main.shape[2] - 1, 0, lane_roll(f.side, 1))
    )


def inverted(v):
    r = pl.reciprocal(v, approx=True)
    r = r * (2.0 - v * r)
    return r * (2.0 - v * r)


def mobility(s):
    return s * s / WATER + (1.0 - s) * (1.0 - s) / OIL


def fraction(s):
    water = s * s / WATER
    return water * inverted(water + (1.0 - s) * (1.0 - s) / OIL)


def coefficient(scaling):
    def fn(ka, kb, ma, mb):
        return (scaling * ka * kb) * inverted(jnp.maximum(ka + kb, 1e-20)) * (ma + mb)

    return fn


NEXT = (z_next, x_next, y_next)
PREV = (z_prev, x_prev, y_prev)


def add(*terms):
    total = terms[0]
    for t in terms[1:]:
        total = total + t
    return total


def packed(own):
    depth, rows, lanes = own.shape
    width = 2 * HALO
    edge = jnp.where(iota(own.shape, 2) < HALO, own, lane_roll(own, width))
    block = iota((rows, lanes), 1) // width
    out = edge[0]
    for z in range(1, depth):
        out = jnp.where(block == z, lane_roll(edge[z], width * z), out)
    return out


def kernel(nx, ny, k_in, s_in, x_in, q_in, p_out, s_out, main_ref, pack_ref, side_ref, part_x, part_y,
           late_send, late_recv, load_sem, xsend, xrecv, psend, precv, rxsend, rxrecv, rysend, ryrecv, lsem, lrecv):
    gx, gy = lax.axis_index("gx"), lax.axis_index("gy")
    ins = (k_in, s_in, x_in, q_in)
    rows = k_in.shape[1]
    wide = rows + 2 * HALO

    def has(dx, dy):
        ok = None
        for d, at, n in ((dx, gx, nx), (dy, gy, ny)):
            if d:
                one = at + d >= 0 if d < 0 else at + d < n
                ok = one if ok is None else ok & one
        return ok

    def at(dx, dy):
        return {"gx": gx + dx, "gy": gy + dy}

    diagonals = [(dx, dy) for dx in (-1, 1) for dy in (-1, 1)]

    loads = [pltpu.make_async_copy(ref, main_ref.at[i, :, pl.ds(0, rows)], load_sem.at[i]) for i, ref in enumerate(ins)]
    for copy in loads:
        copy.start()

    barrier = pltpu.get_barrier_semaphore()
    expected = jnp.int32(nx - 1 + ny - 1)
    for off in range(1, nx):
        pl.semaphore_signal(barrier, inc=1, device_id={"gx": lax.rem(gx + off, nx), "gy": gy}, device_id_type=MESH)
    for off in range(1, ny):
        pl.semaphore_signal(barrier, inc=1, device_id={"gx": gx, "gy": lax.rem(gy + off, ny)}, device_id_type=MESH)
    for dx, dy in diagonals:
        @pl.when(has(dx, dy))
        def _():
            pl.semaphore_signal(barrier, inc=1, device_id=at(dx, dy), device_id_type=MESH)

        expected = expected + has(dx, dy).astype(jnp.int32)

    reach = (HALO - 1, HALO - 1, HALO - 1, HALO - 2)

    def edge_rows(dx, width):
        return pl.ds(0, width) if dx < 0 else pl.ds(rows - width, width)

    def halo_rows(dx, width):
        return pl.ds(rows, width) if dx < 0 else pl.ds(wide - width, width)

    def x_copies(dx, halves=(0, 1)):
        d = (dx + 1) // 2
        return [
            pltpu.make_async_remote_copy(
                src_ref=ref.at[:, edge_rows(dx, reach[i])],
                dst_ref=main_ref.at[i, :, halo_rows(dx, reach[i])],
                send_sem=xsend.at[d * len(ins) + i],
                recv_sem=xrecv.at[d * len(ins) + i],
                device_id=at(dx, 0),
                device_id_type=MESH,
            )
            for i, ref in enumerate(ins)
            if i // 2 in halves
        ]

    def y_copy(half, dx, dy):
        number = half * 6 + (dx + 1) * 2 + (dy + 1) // 2
        from_rows = to_rows = pl.ds(0, rows)
        if dx:
            from_rows, to_rows = edge_rows(dx, HALO - 1), halo_rows(dx, HALO - 1)
        arrays = pl.ds(2 * half, 2)
        return pltpu.make_async_remote_copy(
            src_ref=pack_ref.at[arrays, from_rows],
            dst_ref=side_ref.at[(1 - dy) // 2, arrays, to_rows],
            send_sem=psend.at[number],
            recv_sem=precv.at[number],
            device_id=at(dx, dy),
            device_id_type=MESH,
        )

    def late_copy(dx):
        line = pl.ds(1, 1) if dx < 0 else pl.ds(rows - 2, 1)
        d = (dx + 1) // 2
        return pltpu.make_async_remote_copy(
            src_ref=late_send.at[:, line],
            dst_ref=late_recv.at[:, line],
            send_sem=lsem.at[d],
            recv_sem=lrecv.at[d],
            device_id=at(dx, 0),
            device_id_type=MESH,
        )

    y_moves = [(0, 1), (0, -1)] + diagonals

    pl.semaphore_wait(barrier, expected)
    for dx in (-1, 1):
        @pl.when(has(dx, 0))
        def _():
            for copy in x_copies(dx):
                copy.start()

    for half in range(2):
        for i in (2 * half, 2 * half + 1):
            loads[i].wait()
            pack_ref[i] = packed(main_ref[i, :, 0:rows, :])
        for dx, dy in y_moves:
            @pl.when(has(dx, dy))
            def _():
                y_copy(half, dx, dy).start()

    def arrive(half):
        for dx in (-1, 1):
            @pl.when(has(-dx, 0))
            def _():
                for copy in x_copies(dx, (half,)):
                    copy.wait_recv()

        for dx, dy in y_moves:
            @pl.when(has(-dx, -dy))
            def _():
                y_copy(half, dx, dy).wait_recv()

    lanes = k_in.shape[2]
    depth = k_in.shape[0]
    row = iota((wide, lanes), 0)
    lane = iota((wide, lanes), 1)
    right = lane % (2 * HALO) < HALO

    def field(i):
        inside = (
            (row < rows)
            | ((row < rows + reach[i]) & (gx + 1 < nx))
            | ((row >= wide - reach[i]) & (gx > 0))
        )
        inside_right = right & inside & (gy + 1 < ny)
        inside_left = jnp.logical_not(right) & inside & (gy > 0)
        main = jnp.where(inside[None], main_ref[i], 0.0)
        side = jnp.where(inside_right, side_ref[1, i], jnp.where(inside_left, side_ref[0, i], 0.0))
        return Field(main, side)

    arrive(0)
    k, s = field(0), field(1)
    mob = fmap(mobility, s)
    coefs = []
    for nxt, scaling in zip(NEXT, (VERTICAL, 1.0, 1.0)):
        coefs.append(fmap(coefficient(scaling), k, nxt(k), mob, nxt(mob)))
    before = [prv(c) for prv, c in zip(PREV, coefs)]
    diag = fmap(lambda *c: add(STORAGE, *c), *coefs, *before)
    inverse = fmap(inverted, diag)

    def around(v):
        total = None
        for nxt, prv, c, b in zip(NEXT, PREV, coefs, before):
            term = fmap(lambda c, n, b, p: c * n + b * p, c, nxt(v), b, prv(v))
            total = term if total is None else fmap(jnp.add, total, term)
        return total

    def around_own(v):
        main, side = v.main, v.side[:rows]
        own = main[:, :rows]
        below = jnp.concatenate([own[1:], jnp.zeros_like(own[:1])], axis=0)
        above = jnp.concatenate([jnp.zeros_like(own[:1]), own[:-1]], axis=0)
        moved = (
            (below, above),
            (row_roll(main, -1)[:, :rows], row_roll(main, 1)[:, :rows]),
            (y_next_main(own, side), y_prev_main(own, side)),
        )
        return add(*[c.main[:, :rows] * n + b.main[:, :rows] * p for c, b, (n, p) in zip(coefs, before, moved)])

    arrive(1)
    x0, q = field(2), field(3)
    r0 = fmap(lambda q, x, d, a: q + STORAGE * x - (d * x - a), q, x0, diag, around(x0))
    u0 = fmap(jnp.multiply, r0, inverse)
    v0 = fmap(lambda d, u, a: d * u - a, diag, u0, around(u0))
    u1 = fmap(jnp.multiply, v0, inverse)
    own_v1 = diag.main[:, :rows] * u1.main[:, :rows] - around_own(u1)

    def own(f):
        return f.main[:, :rows]

    pairs = ((own(r0), own(u0)), (own(u0), own(v0)), (own(v0), own(u1)), (own(u1), own_v1))
    tile_row = iota((rows, lanes), 0)
    part = jnp.zeros((rows, lanes), jnp.float32)
    for i, (left, other) in enumerate(pairs):
        part = jnp.where(tile_row == i, jnp.sum(jnp.sum(left * other, axis=0), axis=0, keepdims=True), part)

    late_send[...] = own(u1)

    def total_over(value, slots, name, me, n, send, recv):
        def copy(off, slot):
            target = lax.rem(me + off, n)
            return pltpu.make_async_remote_copy(
                src_ref=slots.at[slot], dst_ref=slots.at[slot], send_sem=send.at[off], recv_sem=recv.at[slot],
                device_id={"gx": gx, "gy": gy, name: target}, device_id_type=MESH,
            )

        def begin():
            slots[me] = value
            for off in range(1, n):
                copy(off, me).start()

        def end():
            for off in range(1, n):
                copy(off, lax.rem(me + off, n)).wait_recv()
            for off in range(1, n):
                copy(off, me).wait_send()
            return add(*[slots[i] for i in range(n)])

        return begin, end

    inject = fmap(lambda v: jnp.maximum(v, 0.0), q)
    produce = fmap(lambda v: jnp.minimum(v, 0.0), q)

    def shares(current):
        frac = fmap(fraction, current)
        gained = fmap(lambda i, o, f: i + o * f, inject, produce, frac)
        return frac, gained, [nxt(frac) for nxt in NEXT]

    begin, end = total_over(part, part_x, "gx", gx, nx, rxsend, rxrecv)
    begin()
    for dx in (-1, 1):
        @pl.when(has(dx, 0))
        def _():
            late_copy(dx).start()

    part = end()
    begin, end = total_over(part, part_y, "gy", gy, ny, rysend, ryrecv)
    begin()
    first_shares = shares(s)
    for dx in (-1, 1):
        @pl.when(has(-dx, 0))
        def _():
            late_copy(dx).wait_recv()

    late = late_recv[...]
    late_row = iota(late.shape, 1)
    taken = ((late_row == 1) & (gx + 1 < nx)) | ((late_row == rows - 2) & (gx > 0))
    u1 = Field(
        jnp.concatenate([own(u1), jnp.where(taken, late, u1.main[:, rows:])], axis=1), u1.side
    )
    part = end()
    sums = jnp.sum(part, axis=1, keepdims=True)
    sa, sb, sc, sd = (sums[i : i + 1, :] for i in range(4))
    step0 = sa / sb
    next_energy = step0 * step0 * sc - sa
    conjugacy = next_energy / sa
    curvature = sb - 2.0 * step0 * sc + step0 * step0 * sd
    step1 = next_energy / (curvature - conjugacy * next_energy / step0)
    weight0 = step0 + step1 * (1.0 + conjugacy)
    weight1 = -step1 * step0

    pressure = fmap(lambda x, a, b: x + weight0 * a + weight1 * b, x0, u0, u1)
    p_out[...] = own(pressure)
    flows = [fmap(lambda c, a, b: c * (a - b), c, pressure, nxt(pressure)) for nxt, c in zip(NEXT, coefs)]
    def transport(current, share):
        frac, total, after = share
        for prv, flow, nf in zip(PREV, flows, after):
            water = fmap(lambda w, a, b: w * jnp.where(w > 0.0, a, b), flow, frac, nf)
            total = fmap(lambda t, w, p: t - (w - p), total, water, prv(water))
        return fmap(lambda c, t: c + STEP * t, current, total)

    first = transport(s, first_shares)
    s_out[...] = own(transport(first, shares(first)))

    for dx in (-1, 1):
        @pl.when(has(dx, 0))
        def _():
            for copy in x_copies(dx):
                copy.wait_send()
            late_copy(dx).wait_send()

    for dx, dy in y_moves:
        @pl.when(has(dx, dy))
        def _():
            for half in range(2):
                y_copy(half, dx, dy).wait_send()


def local(nx, ny, permeability, saturation, pressure_old, source):
    shape = source.shape
    depth, rows, lanes = shape
    assert permeability.shape[0] == 1 and depth * 2 * HALO == lanes and rows == 2 * HALO
    wide = rows + 2 * HALO
    f32 = jnp.float32
    dma = pltpu.SemaphoreType.DMA
    outs = pl.pallas_call(
        functools.partial(kernel, nx, ny),
        out_shape=[jax.ShapeDtypeStruct(shape, f32)] * 2,
        in_specs=[pl.BlockSpec(memory_space=pltpu.HBM)] * 4,
        out_specs=[pl.BlockSpec(memory_space=pltpu.VMEM)] * 2,
        scratch_shapes=[
            pltpu.VMEM((4, depth, wide, lanes), f32),
            pltpu.VMEM((4, rows, lanes), f32),
            pltpu.VMEM((2, 4, wide, lanes), f32),
            pltpu.VMEM((nx, rows, lanes), f32),
            pltpu.VMEM((ny, rows, lanes), f32),
            pltpu.VMEM(shape, f32),
            pltpu.VMEM(shape, f32),
            dma((4,)),
            dma((8,)),
            dma((8,)),
            dma((12,)),
            dma((12,)),
            dma((nx,)),
            dma((nx,)),
            dma((ny,)),
            dma((ny,)),
            dma((2,)),
            dma((2,)),
        ],
        compiler_params=pltpu.CompilerParams(
            collective_id=0, has_side_effects=True, vmem_limit_bytes=32 * 1024 * 1024
        ),
    )(*[pltpu.with_memory_space_constraint(v, pltpu.HBM) for v in (permeability[0], saturation[0], pressure_old[0], source)])
    return outs[0][None], outs[1][None]


def solution(mesh):
    wide = P(None, None, "gx", "gy")
    return jax.shard_map(
        functools.partial(local, mesh.shape["gx"], mesh.shape["gy"]),
        mesh=mesh,
        in_specs=(wide, wide, wide, P(None, "gx", "gy")),
        out_specs=(wide, wide),
        check_vma=False,
    )
```

```python
import functools

import jax
import jax.numpy as jnp
from jax import lax
from jax.experimental import pallas as pl
from jax.experimental.pallas import tpu as pltpu
from jax.sharding import PartitionSpec as P

HALO = 4
STORAGE = 0.5
VERTICAL = 0.1
STEP = 0.05
WATER = 1.0
OIL = 2.0
MESH = pl.DeviceIdType.MESH


def iota(shape, dim):
    return lax.broadcasted_iota(jnp.int32, shape, dim)


class Field:
    def __init__(self, main, side):
        self.main, self.side = main, side

    def map(self, fn, *others):
        return Field(fn(self.main, *[o.main for o in others]), fn(self.side, *[o.side for o in others]))


def fmap(fn, first, *others):
    return first.map(fn, *others)


def row_roll(v, shift):
    axis = v.ndim - 2
    return pltpu.roll(v, shift % v.shape[axis], axis)


def lane_roll(v, shift):
    axis = v.ndim - 1
    shift = shift % v.shape[axis]
    return v if shift == 0 else pltpu.roll(v, shift, axis)


def x_next(f):
    return f.map(lambda v: row_roll(v, -1))


def x_prev(f):
    return f.map(lambda v: row_roll(v, 1))


def z_next(f):
    main = jnp.concatenate([f.main[1:], jnp.zeros_like(f.main[:1])], axis=0)
    width = 2 * HALO
    lanes = f.side.shape[1]
    side = jnp.where(iota(f.side.shape, 1) < lanes - width, lane_roll(f.side, -width), 0.0)
    return Field(main, side)


def z_prev(f):
    main = jnp.concatenate([jnp.zeros_like(f.main[:1]), f.main[:-1]], axis=0)
    width = 2 * HALO
    side = jnp.where(iota(f.side.shape, 1) >= width, lane_roll(f.side, width), 0.0)
    return Field(main, side)


def inserted(side, depth, lane_from, lane_to):
    return jnp.stack([lane_roll(side, lane_to - (2 * HALO * z + lane_from)) for z in range(depth)], axis=0)


def gathered(main, lane_from, lane_to, base):
    width = 2 * HALO
    lane = iota(base.shape, 1)
    for z in range(main.shape[0]):
        base = jnp.where(lane == width * z + lane_to, lane_roll(main[z], width * z + lane_to - lane_from), base)
    return base


def y_next_main(main, side):
    lanes = main.shape[2]
    return jnp.where(
        iota(main.shape, 2) == lanes - 1, inserted(side, main.shape[0], 0, lanes - 1), lane_roll(main, -1)
    )


def y_prev_main(main, side):
    return jnp.where(
        iota(main.shape, 2) == 0, inserted(side, main.shape[0], 2 * HALO - 1, 0), lane_roll(main, 1)
    )


def y_next(f):
    return Field(y_next_main(f.main, f.side), gathered(f.main, 0, 2 * HALO - 1, lane_roll(f.side, -1)))


def y_prev(f):
    return Field(
        y_prev_main(f.main, f.side), gathered(f.main, f.main.shape[2] - 1, 0, lane_roll(f.side, 1))
    )


def inverted(v):
    r = pl.reciprocal(v, approx=True)
    r = r * (2.0 - v * r)
    return r * (2.0 - v * r)


def mobility(s):
    return s * s / WATER + (1.0 - s) * (1.0 - s) / OIL


def fraction(s):
    water = s * s / WATER
    return water * inverted(water + (1.0 - s) * (1.0 - s) / OIL)


def coefficient(scaling):
    def fn(ka, kb, ma, mb):
        return (scaling * ka * kb) * inverted(jnp.maximum(ka + kb, 1e-20)) * (ma + mb)

    return fn


NEXT = (z_next, x_next, y_next)
PREV = (z_prev, x_prev, y_prev)


def add(*terms):
    total = terms[0]
    for t in terms[1:]:
        total = total + t
    return total


def packed(own):
    depth, rows, lanes = own.shape
    width = 2 * HALO
    edge = jnp.where(iota(own.shape, 2) < HALO, own, lane_roll(own, width))
    block = iota((rows, lanes), 1) // width
    out = edge[0]
    for z in range(1, depth):
        out = jnp.where(block == z, lane_roll(edge[z], width * z), out)
    return out


def kernel(nx, ny, k_in, s_in, x_in, q_in, p_out, s_out, main_ref, pack_ref, side_ref, slots,
           late_send, late_recv, load_sem, xsend, xrecv, psend, precv, rsend, rrecv, ready, lsem, lrecv):
    gx, gy = lax.axis_index("gx"), lax.axis_index("gy")
    ins = (k_in, s_in, x_in, q_in)
    rows = k_in.shape[1]
    wide = rows + 2 * HALO

    def has(dx, dy):
        ok = None
        for d, at, n in ((dx, gx, nx), (dy, gy, ny)):
            if d:
                one = at + d >= 0 if d < 0 else at + d < n
                ok = one if ok is None else ok & one
        return ok

    def at(dx, dy):
        return {"gx": gx + dx, "gy": gy + dy}

    diagonals = [(dx, dy) for dx in (-1, 1) for dy in (-1, 1)]

    loads = [pltpu.make_async_copy(ref, main_ref.at[i, :, pl.ds(0, rows)], load_sem.at[i]) for i, ref in enumerate(ins)]
    for copy in loads:
        copy.start()

    barrier = pltpu.get_barrier_semaphore()
    expected = jnp.int32(nx - 1 + ny - 1)
    for off in range(1, nx):
        pl.semaphore_signal(barrier, inc=1, device_id={"gx": lax.rem(gx + off, nx), "gy": gy}, device_id_type=MESH)
    for off in range(1, ny):
        pl.semaphore_signal(barrier, inc=1, device_id={"gx": gx, "gy": lax.rem(gy + off, ny)}, device_id_type=MESH)
    for dx, dy in diagonals:
        @pl.when(has(dx, dy))
        def _():
            pl.semaphore_signal(barrier, inc=1, device_id=at(dx, dy), device_id_type=MESH)

        expected = expected + has(dx, dy).astype(jnp.int32)

    reach = (HALO - 1, HALO - 1, HALO - 1, HALO - 2)

    def edge_rows(dx, width):
        return pl.ds(0, width) if dx < 0 else pl.ds(rows - width, width)

    def halo_rows(dx, width):
        return pl.ds(rows, width) if dx < 0 else pl.ds(wide - width, width)

    def x_copies(dx, halves=(0, 1)):
        d = (dx + 1) // 2
        return [
            pltpu.make_async_remote_copy(
                src_ref=ref.at[:, edge_rows(dx, reach[i])],
                dst_ref=main_ref.at[i, :, halo_rows(dx, reach[i])],
                send_sem=xsend.at[d * len(ins) + i],
                recv_sem=xrecv.at[d * len(ins) + i],
                device_id=at(dx, 0),
                device_id_type=MESH,
            )
            for i, ref in enumerate(ins)
            if i // 2 in halves
        ]

    def y_copy(half, dx, dy):
        number = half * 6 + (dx + 1) * 2 + (dy + 1) // 2
        from_rows = to_rows = pl.ds(0, rows)
        if dx:
            from_rows, to_rows = edge_rows(dx, HALO - 1), halo_rows(dx, HALO - 1)
        arrays = pl.ds(2 * half, 2)
        return pltpu.make_async_remote_copy(
            src_ref=pack_ref.at[arrays, from_rows],
            dst_ref=side_ref.at[(1 - dy) // 2, arrays, to_rows],
            send_sem=psend.at[number],
            recv_sem=precv.at[number],
            device_id=at(dx, dy),
            device_id_type=MESH,
        )

    def late_copy(dx):
        line = pl.ds(1, 1) if dx < 0 else pl.ds(rows - 2, 1)
        d = (dx + 1) // 2
        return pltpu.make_async_remote_copy(
            src_ref=late_send.at[:, line],
            dst_ref=late_recv.at[:, line],
            send_sem=lsem.at[d],
            recv_sem=lrecv.at[d],
            device_id=at(dx, 0),
            device_id_type=MESH,
        )

    y_moves = [(0, 1), (0, -1)] + diagonals

    pl.semaphore_wait(barrier, expected)
    for dx in (-1, 1):
        @pl.when(has(dx, 0))
        def _():
            for copy in x_copies(dx):
                copy.start()

    for off in range(1, nx):
        pl.semaphore_signal(ready, inc=1, device_id={"gx": lax.rem(gx + off, nx), "gy": gy}, device_id_type=MESH)

    for half in range(2):
        for i in (2 * half, 2 * half + 1):
            loads[i].wait()
            pack_ref[i] = packed(main_ref[i, :, 0:rows, :])
        for dx, dy in y_moves:
            @pl.when(has(dx, dy))
            def _():
                y_copy(half, dx, dy).start()

    def arrive(half):
        for dx in (-1, 1):
            @pl.when(has(-dx, 0))
            def _():
                for copy in x_copies(dx, (half,)):
                    copy.wait_recv()

        for dx, dy in y_moves:
            @pl.when(has(-dx, -dy))
            def _():
                y_copy(half, dx, dy).wait_recv()

    lanes = k_in.shape[2]
    depth = k_in.shape[0]
    row = iota((wide, lanes), 0)
    lane = iota((wide, lanes), 1)
    right = lane % (2 * HALO) < HALO

    def field(i):
        inside = (
            (row < rows)
            | ((row < rows + reach[i]) & (gx + 1 < nx))
            | ((row >= wide - reach[i]) & (gx > 0))
        )
        inside_right = right & inside & (gy + 1 < ny)
        inside_left = jnp.logical_not(right) & inside & (gy > 0)
        main = jnp.where(inside[None], main_ref[i], 0.0)
        side = jnp.where(inside_right, side_ref[1, i], jnp.where(inside_left, side_ref[0, i], 0.0))
        return Field(main, side)

    arrive(0)
    k, s = field(0), field(1)
    mob = fmap(mobility, s)
    coefs = []
    for nxt, scaling in zip(NEXT, (VERTICAL, 1.0, 1.0)):
        coefs.append(fmap(coefficient(scaling), k, nxt(k), mob, nxt(mob)))
    before = [prv(c) for prv, c in zip(PREV, coefs)]
    diag = fmap(lambda *c: add(STORAGE, *c), *coefs, *before)
    inverse = fmap(inverted, diag)

    def around(v):
        total = None
        for nxt, prv, c, b in zip(NEXT, PREV, coefs, before):
            term = fmap(lambda c, n, b, p: c * n + b * p, c, nxt(v), b, prv(v))
            total = term if total is None else fmap(jnp.add, total, term)
        return total

    def around_own(v):
        main, side = v.main, v.side[:rows]
        own = main[:, :rows]
        below = jnp.concatenate([own[1:], jnp.zeros_like(own[:1])], axis=0)
        above = jnp.concatenate([jnp.zeros_like(own[:1]), own[:-1]], axis=0)
        moved = (
            (below, above),
            (row_roll(main, -1)[:, :rows], row_roll(main, 1)[:, :rows]),
            (y_next_main(own, side), y_prev_main(own, side)),
        )
        return add(*[c.main[:, :rows] * n + b.main[:, :rows] * p for c, b, (n, p) in zip(coefs, before, moved)])

    arrive(1)
    x0, q = field(2), field(3)
    r0 = fmap(lambda q, x, d, a: q + STORAGE * x - (d * x - a), q, x0, diag, around(x0))
    u0 = fmap(jnp.multiply, r0, inverse)
    v0 = fmap(lambda d, u, a: d * u - a, diag, u0, around(u0))
    u1 = fmap(jnp.multiply, v0, inverse)
    own_v1 = diag.main[:, :rows] * u1.main[:, :rows] - around_own(u1)

    def own(f):
        return f.main[:, :rows]

    pairs = ((own(r0), own(u0)), (own(u0), own(v0)), (own(v0), own(u1)), (own(u1), own_v1))
    tile_row = iota((rows, lanes), 0)
    part = jnp.zeros((rows, lanes), jnp.float32)
    for i, (left, other) in enumerate(pairs):
        part = jnp.where(tile_row == i, jnp.sum(jnp.sum(left * other, axis=0), axis=0, keepdims=True), part)

    late_send[...] = own(u1)

    count = nx * ny
    group = lanes // 4
    folded = part + lane_roll(part, lanes // 2)
    folded = folded + lane_roll(folded, lanes // 4)
    mine = iota((rows, lanes), 1) // group == iota((rows, lanes), 0)
    slots[0:1, :] = jnp.sum(jnp.where(mine, folded, 0.0), axis=0, keepdims=True)
    me = gx * ny + gy

    def share_copy(off, first, size):
        target = lax.rem(me + off, count)
        return pltpu.make_async_remote_copy(
            src_ref=slots.at[pl.ds(0 if size == 1 else first, size)],
            dst_ref=slots.at[pl.ds(first, size)],
            send_sem=rsend,
            recv_sem=rrecv,
            device_id={"gx": target // ny, "gy": target % ny},
            device_id_type=MESH,
        )

    pl.semaphore_wait(ready, nx - 1)
    for off in range(1, count):
        share_copy(off, off, 1).start()

    inject = fmap(lambda v: jnp.maximum(v, 0.0), q)
    produce = fmap(lambda v: jnp.minimum(v, 0.0), q)

    def shares(current):
        frac = fmap(fraction, current)
        gained = fmap(lambda i, o, f: i + o * f, inject, produce, frac)
        return frac, gained, [nxt(frac) for nxt in NEXT]

    for dx in (-1, 1):
        @pl.when(has(dx, 0))
        def _():
            late_copy(dx).start()

    first_shares = shares(s)
    for dx in (-1, 1):
        @pl.when(has(-dx, 0))
        def _():
            late_copy(dx).wait_recv()

    late = late_recv[...]
    late_row = iota(late.shape, 1)
    taken = ((late_row == 1) & (gx + 1 < nx)) | ((late_row == rows - 2) & (gx > 0))
    u1 = Field(
        jnp.concatenate([own(u1), jnp.where(taken, late, u1.main[:, rows:])], axis=1), u1.side
    )
    share_copy(1, 1, count - 1).wait_recv()
    total = jnp.sum(slots[...], axis=0, keepdims=True)
    sums = jnp.sum(jnp.where(mine, total, 0.0), axis=1, keepdims=True)
    sa, sb, sc, sd = (sums[i : i + 1, :] for i in range(4))
    step0 = sa / sb
    next_energy = step0 * step0 * sc - sa
    conjugacy = next_energy / sa
    curvature = sb - 2.0 * step0 * sc + step0 * step0 * sd
    step1 = next_energy / (curvature - conjugacy * next_energy / step0)
    weight0 = step0 + step1 * (1.0 + conjugacy)
    weight1 = -step1 * step0

    pressure = fmap(lambda x, a, b: x + weight0 * a + weight1 * b, x0, u0, u1)
    p_out[...] = own(pressure)
    flows = [fmap(lambda c, a, b: c * (a - b), c, pressure, nxt(pressure)) for nxt, c in zip(NEXT, coefs)]
    def transport(current, share):
        frac, total, after = share
        for prv, flow, nf in zip(PREV, flows, after):
            water = fmap(lambda w, a, b: w * jnp.where(w > 0.0, a, b), flow, frac, nf)
            total = fmap(lambda t, w, p: t - (w - p), total, water, prv(water))
        return fmap(lambda c, t: c + STEP * t, current, total)

    first = transport(s, first_shares)
    s_out[...] = own(transport(first, shares(first)))

    for dx in (-1, 1):
        @pl.when(has(dx, 0))
        def _():
            for copy in x_copies(dx):
                copy.wait_send()
            late_copy(dx).wait_send()

    for dx, dy in y_moves:
        @pl.when(has(dx, dy))
        def _():
            for half in range(2):
                y_copy(half, dx, dy).wait_send()

    share_copy(1, 1, count - 1).wait_send()


def local(nx, ny, permeability, saturation, pressure_old, source):
    shape = source.shape
    depth, rows, lanes = shape
    assert permeability.shape[0] == 1 and depth * 2 * HALO == lanes and rows == 2 * HALO
    wide = rows + 2 * HALO
    f32 = jnp.float32
    dma = pltpu.SemaphoreType.DMA
    outs = pl.pallas_call(
        functools.partial(kernel, nx, ny),
        out_shape=[jax.ShapeDtypeStruct(shape, f32)] * 2,
        in_specs=[pl.BlockSpec(memory_space=pltpu.HBM)] * 4,
        out_specs=[pl.BlockSpec(memory_space=pltpu.VMEM)] * 2,
        scratch_shapes=[
            pltpu.VMEM((4, depth, wide, lanes), f32),
            pltpu.VMEM((4, rows, lanes), f32),
            pltpu.VMEM((2, 4, wide, lanes), f32),
            pltpu.VMEM((nx * ny, lanes), f32),
            pltpu.VMEM(shape, f32),
            pltpu.VMEM(shape, f32),
            dma((4,)),
            dma((8,)),
            dma((8,)),
            dma((12,)),
            dma((12,)),
            dma,
            dma,
            pltpu.SemaphoreType.REGULAR,
            dma((2,)),
            dma((2,)),
        ],
        compiler_params=pltpu.CompilerParams(
            collective_id=0, has_side_effects=True, vmem_limit_bytes=32 * 1024 * 1024
        ),
    )(*[pltpu.with_memory_space_constraint(v, pltpu.HBM) for v in (permeability[0], saturation[0], pressure_old[0], source)])
    return outs[0][None], outs[1][None]


def solution(mesh):
    wide = P(None, None, "gx", "gy")
    return jax.shard_map(
        functools.partial(local, mesh.shape["gx"], mesh.shape["gy"]),
        mesh=mesh,
        in_specs=(wide, wide, wide, P(None, "gx", "gy")),
        out_specs=(wide, wide),
        check_vma=False,
    )
```

```python
import functools

import jax
import jax.numpy as jnp
from jax import lax
from jax.experimental import pallas as pl
from jax.experimental.pallas import tpu as pltpu
from jax.sharding import PartitionSpec as P

HALO = 4
BLOCK = 4
STORAGE = 0.5
VERTICAL = 0.1
STEP = 0.05
WATER = 1.0
OIL = 2.0
MESH = pl.DeviceIdType.MESH


def iota(shape, dim):
    return lax.broadcasted_iota(jnp.int32, shape, dim)


class Field:
    def __init__(self, blocks, side):
        self.blocks, self.side = blocks, side

    def at(self, i):
        return self.side if i is None else self.blocks[i]


def row_roll(v, shift):
    axis = v.ndim - 2
    return pltpu.roll(v, shift % v.shape[axis], axis)


def lane_roll(v, shift):
    axis = v.ndim - 1
    shift = shift % v.shape[axis]
    return v if shift == 0 else pltpu.roll(v, shift, axis)


def x_next(f, i):
    return row_roll(f.at(i), -1)


def x_prev(f, i):
    return row_roll(f.at(i), 1)


def z_next(f, i):
    width = 2 * HALO
    if i is None:
        lanes = f.side.shape[1]
        return jnp.where(iota(f.side.shape, 1) < lanes - width, lane_roll(f.side, -width), 0.0)
    b = f.blocks[i]
    last = f.blocks[i + 1][:1] if i + 1 < len(f.blocks) else jnp.zeros_like(b[:1])
    return jnp.concatenate([b[1:], last], axis=0)


def z_prev(f, i):
    width = 2 * HALO
    if i is None:
        return jnp.where(iota(f.side.shape, 1) >= width, lane_roll(f.side, width), 0.0)
    b = f.blocks[i]
    first = f.blocks[i - 1][-1:] if i else jnp.zeros_like(b[:1])
    return jnp.concatenate([first, b[:-1]], axis=0)


def inserted(side, i, lane_from, lane_to):
    planes = range(i * BLOCK, (i + 1) * BLOCK)
    return jnp.stack([lane_roll(side, lane_to - (2 * HALO * z + lane_from)) for z in planes], axis=0)


def gathered(blocks, lane_from, lane_to, base):
    width = 2 * HALO
    lane = iota(base.shape, 1)
    for i, b in enumerate(blocks):
        for j in range(BLOCK):
            to = width * (i * BLOCK + j) + lane_to
            base = jnp.where(lane == to, lane_roll(b[j], to - lane_from), base)
    return base


def y_next(f, i):
    if i is None:
        return gathered(f.blocks, 0, 2 * HALO - 1, lane_roll(f.side, -1))
    b = f.blocks[i]
    lanes = b.shape[2]
    return jnp.where(iota(b.shape, 2) == lanes - 1, inserted(f.side, i, 0, lanes - 1), lane_roll(b, -1))


def y_prev(f, i):
    if i is None:
        return gathered(f.blocks, f.blocks[0].shape[2] - 1, 0, lane_roll(f.side, 1))
    b = f.blocks[i]
    return jnp.where(iota(b.shape, 2) == 0, inserted(f.side, i, 2 * HALO - 1, 0), lane_roll(b, 1))


def inverted(v):
    r = pl.reciprocal(v, approx=True)
    r = r * (2.0 - v * r)
    return r * (2.0 - v * r)


def mobility(s):
    return s * s / WATER + (1.0 - s) * (1.0 - s) / OIL


def fraction(s):
    water = s * s / WATER
    return water * inverted(water + (1.0 - s) * (1.0 - s) / OIL)


def coefficient(scaling):
    def fn(ka, kb, ma, mb):
        return (scaling * ka * kb) * inverted(jnp.maximum(ka + kb, 1e-20)) * (ma + mb)

    return fn


NEXT = (z_next, x_next, y_next)
PREV = (z_prev, x_prev, y_prev)


def build(fn, count):
    side = fn(None)
    blocks = [fn(i) for i in range(count)]
    return [Field([b[n] for b in blocks], side[n]) for n in range(len(side))]


def add(*terms):
    total = terms[0]
    for t in terms[1:]:
        total = total + t
    return total


def packed(own):
    depth, rows, lanes = own.shape
    width = 2 * HALO
    edge = jnp.where(iota(own.shape, 2) < HALO, own, lane_roll(own, width))
    block = iota((rows, lanes), 1) // width
    out = edge[0]
    for z in range(1, depth):
        out = jnp.where(block == z, lane_roll(edge[z], width * z), out)
    return out


def kernel(nx, ny, k_in, s_in, x_in, q_in, p_out, s_out, main_ref, pack_ref, side_ref, slots,
           late_send, late_recv, load_sem, xsend, xrecv, psend, precv, rsend, rrecv, ready, lsem, lrecv):
    gx, gy = lax.axis_index("gx"), lax.axis_index("gy")
    ins = (k_in, s_in, x_in, q_in)
    rows = k_in.shape[1]
    wide = rows + 2 * HALO

    def has(dx, dy):
        ok = None
        for d, at, n in ((dx, gx, nx), (dy, gy, ny)):
            if d:
                one = at + d >= 0 if d < 0 else at + d < n
                ok = one if ok is None else ok & one
        return ok

    def at(dx, dy):
        return {"gx": gx + dx, "gy": gy + dy}

    diagonals = [(dx, dy) for dx in (-1, 1) for dy in (-1, 1)]

    loads = [pltpu.make_async_copy(ref, main_ref.at[i, :, pl.ds(0, rows)], load_sem.at[i]) for i, ref in enumerate(ins)]
    for copy in loads:
        copy.start()

    barrier = pltpu.get_barrier_semaphore()
    expected = jnp.int32(nx - 1 + ny - 1)
    for off in range(1, nx):
        pl.semaphore_signal(barrier, inc=1, device_id={"gx": lax.rem(gx + off, nx), "gy": gy}, device_id_type=MESH)
    for off in range(1, ny):
        pl.semaphore_signal(barrier, inc=1, device_id={"gx": gx, "gy": lax.rem(gy + off, ny)}, device_id_type=MESH)
    for dx, dy in diagonals:
        @pl.when(has(dx, dy))
        def _():
            pl.semaphore_signal(barrier, inc=1, device_id=at(dx, dy), device_id_type=MESH)

        expected = expected + has(dx, dy).astype(jnp.int32)

    reach = (HALO - 1, HALO - 1, HALO - 1, HALO - 2)

    def edge_rows(dx, width):
        return pl.ds(0, width) if dx < 0 else pl.ds(rows - width, width)

    def halo_rows(dx, width):
        return pl.ds(rows, width) if dx < 0 else pl.ds(wide - width, width)

    def x_copies(dx, halves=(0, 1)):
        d = (dx + 1) // 2
        return [
            pltpu.make_async_remote_copy(
                src_ref=ref.at[:, edge_rows(dx, reach[i])],
                dst_ref=main_ref.at[i, :, halo_rows(dx, reach[i])],
                send_sem=xsend.at[d * len(ins) + i],
                recv_sem=xrecv.at[d * len(ins) + i],
                device_id=at(dx, 0),
                device_id_type=MESH,
            )
            for i, ref in enumerate(ins)
            if i // 2 in halves
        ]

    def y_copy(half, dx, dy):
        number = half * 6 + (dx + 1) * 2 + (dy + 1) // 2
        from_rows = to_rows = pl.ds(0, rows)
        if dx:
            from_rows, to_rows = edge_rows(dx, HALO - 1), halo_rows(dx, HALO - 1)
        arrays = pl.ds(2 * half, 2)
        return pltpu.make_async_remote_copy(
            src_ref=pack_ref.at[arrays, from_rows],
            dst_ref=side_ref.at[(1 - dy) // 2, arrays, to_rows],
            send_sem=psend.at[number],
            recv_sem=precv.at[number],
            device_id=at(dx, dy),
            device_id_type=MESH,
        )

    def late_copy(dx):
        line = pl.ds(1, 1) if dx < 0 else pl.ds(rows - 2, 1)
        d = (dx + 1) // 2
        return pltpu.make_async_remote_copy(
            src_ref=late_send.at[:, line],
            dst_ref=late_recv.at[:, line],
            send_sem=lsem.at[d],
            recv_sem=lrecv.at[d],
            device_id=at(dx, 0),
            device_id_type=MESH,
        )

    y_moves = [(0, 1), (0, -1)] + diagonals

    pl.semaphore_wait(barrier, expected)
    for dx in (-1, 1):
        @pl.when(has(dx, 0))
        def _():
            for copy in x_copies(dx):
                copy.start()

    for off in range(1, nx):
        pl.semaphore_signal(ready, inc=1, device_id={"gx": lax.rem(gx + off, nx), "gy": gy}, device_id_type=MESH)

    for half in range(2):
        for i in (2 * half, 2 * half + 1):
            loads[i].wait()
            pack_ref[i] = packed(main_ref[i, :, 0:rows, :])
        for dx, dy in y_moves:
            @pl.when(has(dx, dy))
            def _():
                y_copy(half, dx, dy).start()

    def arrive(half):
        for dx in (-1, 1):
            @pl.when(has(-dx, 0))
            def _():
                for copy in x_copies(dx, (half,)):
                    copy.wait_recv()

        for dx, dy in y_moves:
            @pl.when(has(-dx, -dy))
            def _():
                y_copy(half, dx, dy).wait_recv()

    lanes = k_in.shape[2]
    depth = k_in.shape[0]
    row = iota((wide, lanes), 0)
    lane = iota((wide, lanes), 1)
    right = lane % (2 * HALO) < HALO

    nb = depth // BLOCK

    def field(i):
        inside = (
            (row < rows)
            | ((row < rows + reach[i]) & (gx + 1 < nx))
            | ((row >= wide - reach[i]) & (gx > 0))
        )
        inside_right = right & inside & (gy + 1 < ny)
        inside_left = jnp.logical_not(right) & inside & (gy > 0)
        blocks = [jnp.where(inside[None], main_ref[i, n * BLOCK : (n + 1) * BLOCK], 0.0) for n in range(nb)]
        side = jnp.where(inside_right, side_ref[1, i], jnp.where(inside_left, side_ref[0, i], 0.0))
        return Field(blocks, side)

    def own(f):
        return jnp.concatenate([b[:, :rows] for b in f.blocks], axis=0)

    arrive(0)
    k, s = field(0), field(1)
    (mob,) = build(lambda i: [mobility(s.at(i))], nb)
    scalings = (VERTICAL, 1.0, 1.0)
    coefs = [Field([], None) for _ in NEXT]
    before = [Field([], None) for _ in NEXT]
    diag, inverse = Field([], None), Field([], None)

    def face(i):
        return [
            coefficient(sc)(k.at(i), nxt(k, i), mob.at(i), nxt(mob, i)) for nxt, sc in zip(NEXT, scalings)
        ]

    def centre(i):
        sides = [prv(c, i) for prv, c in zip(PREV, coefs)]
        d = add(STORAGE, *[c.at(i) for c in coefs], *sides)
        return sides, d, inverted(d)

    for c, value in zip(coefs, face(None)):
        c.side = value
    for i in range(nb):
        for c, value in zip(coefs, face(i)):
            c.blocks.append(value)
        sides, d, r = centre(i)
        for c, value in zip(before, sides):
            c.blocks.append(value)
        diag.blocks.append(d)
        inverse.blocks.append(r)
    sides, diag.side, inverse.side = centre(None)
    for c, value in zip(before, sides):
        c.side = value

    def around(v, i):
        return add(*[
            c.at(i) * nxt(v, i) + b.at(i) * prv(v, i) for nxt, prv, c, b in zip(NEXT, PREV, coefs, before)
        ])

    arrive(1)
    x0, q = field(2), field(3)
    (u0,) = build(
        lambda i: [(q.at(i) + STORAGE * x0.at(i) - (diag.at(i) * x0.at(i) - around(x0, i))) * inverse.at(i)], nb
    )
    (u1,) = build(lambda i: [u0.at(i) - around(u0, i) * inverse.at(i)], nb)
    sums = [0.0] * 4
    for i in range(nb):
        d, a, b = [f.blocks[i][:, :rows] for f in (diag, u0, u1)]
        da, db = d * a, d * b
        image = db - around(u1, i)[:, :rows]
        for n, value in enumerate((da * a, da * b, db * b, b * image)):
            sums[n] = sums[n] + jnp.sum(value, axis=0)

    tile_row = iota((rows, lanes), 0)
    part = jnp.zeros((rows, lanes), jnp.float32)
    for i, value in enumerate(sums):
        part = jnp.where(tile_row == i, jnp.sum(value, axis=0, keepdims=True), part)

    late_send[...] = own(u1)

    count = nx * ny
    group = lanes // 4
    folded = part + lane_roll(part, lanes // 2)
    folded = folded + lane_roll(folded, lanes // 4)
    mine = iota((rows, lanes), 1) // group == iota((rows, lanes), 0)
    slots[0:1, :] = jnp.sum(jnp.where(mine, folded, 0.0), axis=0, keepdims=True)
    me = gx * ny + gy

    def share_copy(off, first, size):
        target = lax.rem(me + off, count)
        return pltpu.make_async_remote_copy(
            src_ref=slots.at[pl.ds(0 if size == 1 else first, size)],
            dst_ref=slots.at[pl.ds(first, size)],
            send_sem=rsend,
            recv_sem=rrecv,
            device_id={"gx": target // ny, "gy": target % ny},
            device_id_type=MESH,
        )

    pl.semaphore_wait(ready, nx - 1)
    for off in range(1, count):
        share_copy(off, off, 1).start()

    def gained(i, frac):
        return jnp.maximum(q.at(i), 0.0) + jnp.minimum(q.at(i), 0.0) * frac

    for dx in (-1, 1):
        @pl.when(has(dx, 0))
        def _():
            late_copy(dx).start()

    (frac,) = build(lambda i: [fraction(s.at(i))], nb)
    (gain,) = build(lambda i: [gained(i, frac.at(i))], nb)
    after = build(lambda i: [nxt(frac, i) for nxt in NEXT], nb)
    for dx in (-1, 1):
        @pl.when(has(-dx, 0))
        def _():
            late_copy(dx).wait_recv()

    late = late_recv[...]
    late_row = iota(late.shape, 1)
    taken = ((late_row == 1) & (gx + 1 < nx)) | ((late_row == rows - 2) & (gx > 0))
    u1 = Field(
        [
            jnp.concatenate(
                [
                    b[:, :rows],
                    jnp.where(taken[i * BLOCK : (i + 1) * BLOCK], late[i * BLOCK : (i + 1) * BLOCK], b[:, rows:]),
                ],
                axis=1,
            )
            for i, b in enumerate(u1.blocks)
        ],
        u1.side,
    )
    share_copy(1, 1, count - 1).wait_recv()
    total = jnp.sum(slots[...], axis=0, keepdims=True)
    sums = jnp.sum(jnp.where(mine, total, 0.0), axis=1, keepdims=True)
    sa, sb, sc, sd = (sums[i : i + 1, :] for i in range(4))
    step0 = sa / sb
    next_energy = step0 * step0 * sc - sa
    conjugacy = next_energy / sa
    curvature = sb - 2.0 * step0 * sc + step0 * step0 * sd
    step1 = next_energy / (curvature - conjugacy * next_energy / step0)
    weight0 = step0 + step1 * (1.0 + conjugacy)
    weight1 = -step1 * step0

    (pressure,) = build(lambda i: [x0.at(i) + weight0 * u0.at(i) + weight1 * u1.at(i)], nb)
    flows = [Field([], None) for _ in NEXT]

    def flux(i):
        return [c.at(i) * (pressure.at(i) - nxt(pressure, i)) for nxt, c in zip(NEXT, coefs)]

    def water_at(i, frac, nexts):
        return [
            f.at(i) * jnp.where(f.at(i) > 0.0, frac.at(i), n) for f, n in zip(flows, nexts)
        ]

    def moved(i, current, gain, water):
        return current + STEP * add(gain, *[prv(w, i) - w.at(i) for prv, w in zip(PREV, water)])

    water = [Field([], None) for _ in NEXT]
    first = Field([], None)
    for f, value in zip(flows, flux(None)):
        f.side = value
    for w, value in zip(water, water_at(None, frac, [n.side for n in after])):
        w.side = value
    for i in range(nb):
        p_out[i * BLOCK : (i + 1) * BLOCK] = pressure.blocks[i][:, :rows]
        for f, value in zip(flows, flux(i)):
            f.blocks.append(value)
        for w, value in zip(water, water_at(i, frac, [n.blocks[i] for n in after])):
            w.blocks.append(value)
        first.blocks.append(moved(i, s.blocks[i], gain.blocks[i], water))
    first.side = moved(None, s.side, gain.side, water)

    (frac,) = build(lambda i: [fraction(first.at(i))], nb)
    water = [Field([], None) for _ in NEXT]
    for w, value in zip(water, water_at(None, frac, [nxt(frac, None) for nxt in NEXT])):
        w.side = value
    for i in range(nb):
        for w, value in zip(water, water_at(i, frac, [nxt(frac, i) for nxt in NEXT])):
            w.blocks.append(value)
        second = moved(i, first.blocks[i], gained(i, frac.blocks[i]), water)
        s_out[i * BLOCK : (i + 1) * BLOCK] = second[:, :rows]

    for dx in (-1, 1):
        @pl.when(has(dx, 0))
        def _():
            for copy in x_copies(dx):
                copy.wait_send()
            late_copy(dx).wait_send()

    for dx, dy in y_moves:
        @pl.when(has(dx, dy))
        def _():
            for half in range(2):
                y_copy(half, dx, dy).wait_send()

    share_copy(1, 1, count - 1).wait_send()


def local(nx, ny, permeability, saturation, pressure_old, source):
    shape = source.shape
    depth, rows, lanes = shape
    assert permeability.shape[0] == 1 and depth % BLOCK == 0 and depth * 2 * HALO == lanes and rows == 2 * HALO
    wide = rows + 2 * HALO
    f32 = jnp.float32
    dma = pltpu.SemaphoreType.DMA
    outs = pl.pallas_call(
        functools.partial(kernel, nx, ny),
        out_shape=[jax.ShapeDtypeStruct(shape, f32)] * 2,
        in_specs=[pl.BlockSpec(memory_space=pltpu.HBM)] * 4,
        out_specs=[pl.BlockSpec(memory_space=pltpu.VMEM)] * 2,
        scratch_shapes=[
            pltpu.VMEM((4, depth, wide, lanes), f32),
            pltpu.VMEM((4, rows, lanes), f32),
            pltpu.VMEM((2, 4, wide, lanes), f32),
            pltpu.VMEM((nx * ny, lanes), f32),
            pltpu.VMEM(shape, f32),
            pltpu.VMEM(shape, f32),
            dma((4,)),
            dma((8,)),
            dma((8,)),
            dma((12,)),
            dma((12,)),
            dma,
            dma,
            pltpu.SemaphoreType.REGULAR,
            dma((2,)),
            dma((2,)),
        ],
        compiler_params=pltpu.CompilerParams(
            collective_id=0, has_side_effects=True, vmem_limit_bytes=32 * 1024 * 1024
        ),
    )(*[pltpu.with_memory_space_constraint(v, pltpu.HBM) for v in (permeability[0], saturation[0], pressure_old[0], source)])
    return outs[0][None], outs[1][None]


def solution(mesh):
    wide = P(None, None, "gx", "gy")
    return jax.shard_map(
        functools.partial(local, mesh.shape["gx"], mesh.shape["gy"]),
        mesh=mesh,
        in_specs=(wide, wide, wide, P(None, "gx", "gy")),
        out_specs=(wide, wide),
        check_vma=False,
    )
```

```python
import functools

import jax
import jax.numpy as jnp
from jax import lax
from jax.experimental import pallas as pl
from jax.experimental.pallas import tpu as pltpu
from jax.sharding import PartitionSpec as P

HALO = 4
BLOCK = 4
STORAGE = 0.5
VERTICAL = 0.1
STEP = 0.05
WATER = 1.0
OIL = 2.0
MESH = pl.DeviceIdType.MESH


def iota(shape, dim):
    return lax.broadcasted_iota(jnp.int32, shape, dim)


class Field:
    def __init__(self, blocks, side):
        self.blocks, self.side = blocks, side

    def at(self, i):
        return self.side if i is None else self.blocks[i]


def row_roll(v, shift):
    axis = v.ndim - 2
    return pltpu.roll(v, shift % v.shape[axis], axis)


def lane_roll(v, shift):
    axis = v.ndim - 1
    shift = shift % v.shape[axis]
    return v if shift == 0 else pltpu.roll(v, shift, axis)


def x_next(f, i):
    return row_roll(f.at(i), -1)


def x_prev(f, i):
    return row_roll(f.at(i), 1)


def z_next(f, i):
    width = 2 * HALO
    if i is None:
        lanes = f.side.shape[1]
        return jnp.where(iota(f.side.shape, 1) < lanes - width, lane_roll(f.side, -width), 0.0)
    b = f.blocks[i]
    last = f.blocks[i + 1][:1] if i + 1 < len(f.blocks) else jnp.zeros_like(b[:1])
    return jnp.concatenate([b[1:], last], axis=0)


def z_prev(f, i):
    width = 2 * HALO
    if i is None:
        return jnp.where(iota(f.side.shape, 1) >= width, lane_roll(f.side, width), 0.0)
    b = f.blocks[i]
    first = f.blocks[i - 1][-1:] if i else jnp.zeros_like(b[:1])
    return jnp.concatenate([first, b[:-1]], axis=0)


def inserted(side, i, lane_from, lane_to):
    planes = range(i * BLOCK, (i + 1) * BLOCK)
    return jnp.stack([lane_roll(side, lane_to - (2 * HALO * z + lane_from)) for z in planes], axis=0)


def gathered(blocks, lane_from, lane_to, base):
    width = 2 * HALO
    lane = iota(base.shape, 1)
    for i, b in enumerate(blocks):
        for j in range(BLOCK):
            to = width * (i * BLOCK + j) + lane_to
            base = jnp.where(lane == to, lane_roll(b[j], to - lane_from), base)
    return base


def y_next(f, i):
    if i is None:
        return gathered(f.blocks, 0, 2 * HALO - 1, lane_roll(f.side, -1))
    b = f.blocks[i]
    lanes = b.shape[2]
    return jnp.where(iota(b.shape, 2) == lanes - 1, inserted(f.side, i, 0, lanes - 1), lane_roll(b, -1))


def y_prev(f, i):
    if i is None:
        return gathered(f.blocks, f.blocks[0].shape[2] - 1, 0, lane_roll(f.side, 1))
    b = f.blocks[i]
    return jnp.where(iota(b.shape, 2) == 0, inserted(f.side, i, 2 * HALO - 1, 0), lane_roll(b, 1))


def inverted(v):
    r = pl.reciprocal(v, approx=True)
    r = r * (2.0 - v * r)
    return r * (2.0 - v * r)


def mobility(s):
    return s * s / WATER + (1.0 - s) * (1.0 - s) / OIL


def fraction(s):
    water = s * s / WATER
    return water * inverted(water + (1.0 - s) * (1.0 - s) / OIL)


def coefficient(scaling):
    def fn(ka, kb, ma, mb):
        return (scaling * ka * kb) * inverted(jnp.maximum(ka + kb, 1e-20)) * (ma + mb)

    return fn


NEXT = (z_next, x_next, y_next)
PREV = (z_prev, x_prev, y_prev)


def build(fn, count):
    side = fn(None)
    blocks = [fn(i) for i in range(count)]
    return [Field([b[n] for b in blocks], side[n]) for n in range(len(side))]


def add(*terms):
    total = terms[0]
    for t in terms[1:]:
        total = total + t
    return total


def packed(own):
    depth, rows, lanes = own.shape
    width = 2 * HALO
    edge = jnp.where(iota(own.shape, 2) < HALO, own, lane_roll(own, width))
    block = iota((rows, lanes), 1) // width
    out = edge[0]
    for z in range(1, depth):
        out = jnp.where(block == z, lane_roll(edge[z], width * z), out)
    return out


def kernel(nx, ny, k_in, s_in, x_in, q_in, p_out, s_out, main_ref, pack_ref, side_ref, slots,
           late_send, late_recv, early_send, early_recv, load_sem, xsend, xrecv, psend, precv, rsend, rrecv, ready, lsem, lrecv, esem, erecv):
    gx, gy = lax.axis_index("gx"), lax.axis_index("gy")
    ins = (k_in, s_in, x_in, q_in)
    rows = k_in.shape[1]
    wide = rows + 2 * HALO

    def has(dx, dy):
        ok = None
        for d, at, n in ((dx, gx, nx), (dy, gy, ny)):
            if d:
                one = at + d >= 0 if d < 0 else at + d < n
                ok = one if ok is None else ok & one
        return ok

    def at(dx, dy):
        return {"gx": gx + dx, "gy": gy + dy}

    diagonals = [(dx, dy) for dx in (-1, 1) for dy in (-1, 1)]

    loads = [pltpu.make_async_copy(ref, main_ref.at[i, :, pl.ds(0, rows)], load_sem.at[i]) for i, ref in enumerate(ins)]
    for copy in loads:
        copy.start()

    barrier = pltpu.get_barrier_semaphore()
    expected = jnp.int32(nx - 1 + ny - 1)
    for off in range(1, nx):
        pl.semaphore_signal(barrier, inc=1, device_id={"gx": lax.rem(gx + off, nx), "gy": gy}, device_id_type=MESH)
    for off in range(1, ny):
        pl.semaphore_signal(barrier, inc=1, device_id={"gx": gx, "gy": lax.rem(gy + off, ny)}, device_id_type=MESH)
    for dx, dy in diagonals:
        @pl.when(has(dx, dy))
        def _():
            pl.semaphore_signal(barrier, inc=1, device_id=at(dx, dy), device_id_type=MESH)

        expected = expected + has(dx, dy).astype(jnp.int32)

    reach = (2, 2, 2, 1)

    def edge_rows(dx, width):
        return pl.ds(0, width) if dx < 0 else pl.ds(rows - width, width)

    def halo_rows(dx, width):
        return pl.ds(rows, width) if dx < 0 else pl.ds(wide - width, width)

    def x_copies(dx, halves=(0, 1)):
        d = (dx + 1) // 2
        return [
            pltpu.make_async_remote_copy(
                src_ref=ref.at[:, edge_rows(dx, reach[i])],
                dst_ref=main_ref.at[i, :, halo_rows(dx, reach[i])],
                send_sem=xsend.at[d * len(ins) + i],
                recv_sem=xrecv.at[d * len(ins) + i],
                device_id=at(dx, 0),
                device_id_type=MESH,
            )
            for i, ref in enumerate(ins)
            if i // 2 in halves
        ]

    def y_copy(dx, dy):
        number = (dx + 1) * 2 + (dy + 1) // 2
        from_rows = to_rows = pl.ds(0, rows)
        if dx:
            from_rows, to_rows = edge_rows(dx, reach[0]), halo_rows(dx, reach[0])
        return pltpu.make_async_remote_copy(
            src_ref=pack_ref.at[:, from_rows],
            dst_ref=side_ref.at[(1 - dy) // 2, :, to_rows],
            send_sem=psend.at[number],
            recv_sem=precv.at[number],
            device_id=at(dx, dy),
            device_id_type=MESH,
        )

    def line_copy(dx, src, dst, send, recv):
        line = pl.ds(1, 1) if dx < 0 else pl.ds(rows - 2, 1)
        d = (dx + 1) // 2
        return pltpu.make_async_remote_copy(
            src_ref=src.at[:, line],
            dst_ref=dst.at[:, line],
            send_sem=send.at[d],
            recv_sem=recv.at[d],
            device_id=at(dx, 0),
            device_id_type=MESH,
        )

    def early_copy(dx):
        return line_copy(dx, early_send, early_recv, esem, erecv)

    def late_copy(dx):
        return line_copy(dx, late_send, late_recv, lsem, lrecv)

    y_moves = [(0, 1), (0, -1)] + diagonals

    for i in range(len(ins)):
        loads[i].wait()
        pack_ref[i] = packed(main_ref[i, :, 0:rows, :])

    pl.semaphore_wait(barrier, expected)
    for dx, dy in y_moves:
        @pl.when(has(dx, dy))
        def _():
            y_copy(dx, dy).start()

    for half in range(2):
        for dx in (-1, 1):
            @pl.when(has(dx, 0))
            def _():
                for copy in x_copies(dx, (half,)):
                    copy.start()

    for off in range(1, nx):
        pl.semaphore_signal(ready, inc=1, device_id={"gx": lax.rem(gx + off, nx), "gy": gy}, device_id_type=MESH)

    def arrive_y(moves):
        for dx, dy in moves:
            @pl.when(has(-dx, -dy))
            def _():
                y_copy(dx, dy).wait_recv()

    def arrive_x(half):
        for dx in (-1, 1):
            @pl.when(has(-dx, 0))
            def _():
                for copy in x_copies(dx, (half,)):
                    copy.wait_recv()

    lanes = k_in.shape[2]
    depth = k_in.shape[0]
    row = iota((wide, lanes), 0)
    lane = iota((wide, lanes), 1)
    right = lane % (2 * HALO) < HALO

    nb = depth // BLOCK

    def field(i, high):
        at_row, at_right = row[:high], right[:high]
        inside = (
            (at_row < rows)
            | ((at_row < rows + reach[i]) & (gx + 1 < nx))
            | ((at_row >= wide - reach[i]) & (gx > 0))
        )
        inside_right = at_right & inside & (gy + 1 < ny)
        inside_left = jnp.logical_not(at_right) & inside & (gy > 0)
        blocks = [main_ref[i, n * BLOCK : (n + 1) * BLOCK, 0:high] for n in range(nb)]
        if high > rows:
            blocks = [jnp.where(inside[None], b, 0.0) for b in blocks]
        side = jnp.where(
            inside_right, side_ref[1, i, 0:high], jnp.where(inside_left, side_ref[0, i, 0:high], 0.0)
        )
        return Field(blocks, side)

    def own(f):
        return jnp.concatenate([b[:, :rows] for b in f.blocks], axis=0)

    def stencil(k, s):
        (mob,) = build(lambda i: [mobility(s.at(i))], nb)
        scalings = (VERTICAL, 1.0, 1.0)
        coefs = [Field([], None) for _ in NEXT]
        before = [Field([], None) for _ in NEXT]
        diag, inverse = Field([], None), Field([], None)

        def face(i):
            return [
                coefficient(sc)(k.at(i), nxt(k, i), mob.at(i), nxt(mob, i)) for nxt, sc in zip(NEXT, scalings)
            ]

        def centre(i):
            sides = [prv(c, i) for prv, c in zip(PREV, coefs)]
            d = add(STORAGE, *[c.at(i) for c in coefs], *sides)
            return sides, d, inverted(d)

        for c, value in zip(coefs, face(None)):
            c.side = value
        for i in range(nb):
            for c, value in zip(coefs, face(i)):
                c.blocks.append(value)
            sides, d, r = centre(i)
            for c, value in zip(before, sides):
                c.blocks.append(value)
            diag.blocks.append(d)
            inverse.blocks.append(r)
        sides, diag.side, inverse.side = centre(None)
        for c, value in zip(before, sides):
            c.side = value
        return coefs, before, diag, inverse

    def around_in(coefs, before):
        def around(v, i):
            return add(*[
                c.at(i) * nxt(v, i) + b.at(i) * prv(v, i)
                for nxt, prv, c, b in zip(NEXT, PREV, coefs, before)
            ])

        return around

    def start_field(x0, q, around, diag, inverse):
        return build(
            lambda i: [(q.at(i) + STORAGE * x0.at(i) - (diag.at(i) * x0.at(i) - around(x0, i))) * inverse.at(i)],
            nb,
        )[0]

    arrive_y(y_moves[:2])
    coefs, before, diag, inverse = stencil(field(0, rows), field(1, rows))
    u0 = start_field(field(2, rows), field(3, rows), around_in(coefs, before), diag, inverse)
    for i, b in enumerate(u0.blocks):
        early_send[i * BLOCK : (i + 1) * BLOCK] = b
    early_send[depth] = u0.side
    for dx in (-1, 1):
        @pl.when(has(dx, 0))
        def _():
            early_copy(dx).start()

    line_row = iota((rows, lanes), 0)
    taken = ((line_row == 1) & (gx + 1 < nx)) | ((line_row == rows - 2) & (gx > 0))

    def patched(value, ref, planes):
        cut = value[..., :rows, :], value[..., rows:, :]
        return jnp.concatenate([cut[0], jnp.where(taken, ref[planes], cut[1])], axis=-2)

    def patch(f, ref):
        f.blocks = [patched(b, ref, slice(i * BLOCK, (i + 1) * BLOCK)) for i, b in enumerate(f.blocks)]

    arrive_y(y_moves[2:])
    arrive_x(0)
    k, s = field(0, wide), field(1, wide)
    coefs, before, diag, inverse = stencil(k, s)
    around = around_in(coefs, before)
    arrive_x(1)
    x0, q = field(2, wide), field(3, wide)
    u0 = start_field(x0, q, around, diag, inverse)
    for dx in (-1, 1):
        @pl.when(has(-dx, 0))
        def _():
            early_copy(dx).wait_recv()

    patch(u0, early_recv)
    u0.side = patched(u0.side, early_recv, depth)
    (u1,) = build(lambda i: [u0.at(i) - around(u0, i) * inverse.at(i)], nb)
    sums = [0.0] * 4
    for i in range(nb):
        d, a, b = [f.blocks[i][:, :rows] for f in (diag, u0, u1)]
        da, db = d * a, d * b
        image = db - around(u1, i)[:, :rows]
        for n, value in enumerate((da * a, da * b, db * b, b * image)):
            sums[n] = sums[n] + jnp.sum(value, axis=0)

    tile_row = iota((rows, lanes), 0)
    part = jnp.zeros((rows, lanes), jnp.float32)
    for i, value in enumerate(sums):
        part = jnp.where(tile_row == i, jnp.sum(value, axis=0, keepdims=True), part)

    late_send[...] = own(u1)

    count = nx * ny
    group = lanes // 4
    folded = part + lane_roll(part, lanes // 2)
    folded = folded + lane_roll(folded, lanes // 4)
    mine = iota((rows, lanes), 1) // group == iota((rows, lanes), 0)
    slots[0:1, :] = jnp.sum(jnp.where(mine, folded, 0.0), axis=0, keepdims=True)
    me = gx * ny + gy

    def share_copy(off, first, size):
        target = lax.rem(me + off, count)
        return pltpu.make_async_remote_copy(
            src_ref=slots.at[pl.ds(0 if size == 1 else first, size)],
            dst_ref=slots.at[pl.ds(first, size)],
            send_sem=rsend,
            recv_sem=rrecv,
            device_id={"gx": target // ny, "gy": target % ny},
            device_id_type=MESH,
        )

    pl.semaphore_wait(ready, nx - 1)
    for off in range(1, count):
        share_copy(off, off, 1).start()

    def gained(i, frac):
        return jnp.maximum(q.at(i), 0.0) + jnp.minimum(q.at(i), 0.0) * frac

    for dx in (-1, 1):
        @pl.when(has(dx, 0))
        def _():
            late_copy(dx).start()

    (frac,) = build(lambda i: [fraction(s.at(i))], nb)
    (gain,) = build(lambda i: [gained(i, frac.at(i))], nb)
    after = build(lambda i: [nxt(frac, i) for nxt in NEXT], nb)
    for dx in (-1, 1):
        @pl.when(has(-dx, 0))
        def _():
            late_copy(dx).wait_recv()

    patch(u1, late_recv)
    share_copy(1, 1, count - 1).wait_recv()
    total = jnp.sum(slots[...], axis=0, keepdims=True)
    sums = jnp.sum(jnp.where(mine, total, 0.0), axis=1, keepdims=True)
    sa, sb, sc, sd = (sums[i : i + 1, :] for i in range(4))
    step0 = sa / sb
    next_energy = step0 * step0 * sc - sa
    conjugacy = next_energy / sa
    curvature = sb - 2.0 * step0 * sc + step0 * step0 * sd
    step1 = next_energy / (curvature - conjugacy * next_energy / step0)
    weight0 = step0 + step1 * (1.0 + conjugacy)
    weight1 = -step1 * step0

    (pressure,) = build(lambda i: [x0.at(i) + weight0 * u0.at(i) + weight1 * u1.at(i)], nb)
    flows = [Field([], None) for _ in NEXT]

    def flux(i):
        return [c.at(i) * (pressure.at(i) - nxt(pressure, i)) for nxt, c in zip(NEXT, coefs)]

    def water_at(i, frac, nexts):
        return [
            f.at(i) * jnp.where(f.at(i) > 0.0, frac.at(i), n) for f, n in zip(flows, nexts)
        ]

    def moved(i, current, gain, water):
        return current + STEP * add(gain, *[prv(w, i) - w.at(i) for prv, w in zip(PREV, water)])

    water = [Field([], None) for _ in NEXT]
    first = Field([], None)
    for f, value in zip(flows, flux(None)):
        f.side = value
    for w, value in zip(water, water_at(None, frac, [n.side for n in after])):
        w.side = value
    for i in range(nb):
        p_out[i * BLOCK : (i + 1) * BLOCK] = pressure.blocks[i][:, :rows]
        for f, value in zip(flows, flux(i)):
            f.blocks.append(value)
        for w, value in zip(water, water_at(i, frac, [n.blocks[i] for n in after])):
            w.blocks.append(value)
        first.blocks.append(moved(i, s.blocks[i], gain.blocks[i], water))
    first.side = moved(None, s.side, gain.side, water)

    (frac,) = build(lambda i: [fraction(first.at(i))], nb)
    water = [Field([], None) for _ in NEXT]
    for w, value in zip(water, water_at(None, frac, [nxt(frac, None) for nxt in NEXT])):
        w.side = value
    for i in range(nb):
        for w, value in zip(water, water_at(i, frac, [nxt(frac, i) for nxt in NEXT])):
            w.blocks.append(value)
        second = moved(i, first.blocks[i], gained(i, frac.blocks[i]), water)
        s_out[i * BLOCK : (i + 1) * BLOCK] = second[:, :rows]

    for dx in (-1, 1):
        @pl.when(has(dx, 0))
        def _():
            for copy in x_copies(dx):
                copy.wait_send()
            early_copy(dx).wait_send()
            late_copy(dx).wait_send()

    for dx, dy in y_moves:
        @pl.when(has(dx, dy))
        def _():
            y_copy(dx, dy).wait_send()

    share_copy(1, 1, count - 1).wait_send()


def local(nx, ny, permeability, saturation, pressure_old, source):
    shape = source.shape
    depth, rows, lanes = shape
    assert permeability.shape[0] == 1 and depth % BLOCK == 0 and depth * 2 * HALO == lanes and rows == 2 * HALO
    wide = rows + 2 * HALO
    f32 = jnp.float32
    dma = pltpu.SemaphoreType.DMA
    outs = pl.pallas_call(
        functools.partial(kernel, nx, ny),
        out_shape=[jax.ShapeDtypeStruct(shape, f32)] * 2,
        in_specs=[pl.BlockSpec(memory_space=pltpu.HBM)] * 4,
        out_specs=[pl.BlockSpec(memory_space=pltpu.VMEM)] * 2,
        scratch_shapes=[
            pltpu.VMEM((4, depth, wide, lanes), f32),
            pltpu.VMEM((4, rows, lanes), f32),
            pltpu.VMEM((2, 4, wide, lanes), f32),
            pltpu.VMEM((nx * ny, lanes), f32),
            pltpu.VMEM(shape, f32),
            pltpu.VMEM(shape, f32),
            pltpu.VMEM((depth + 1, rows, lanes), f32),
            pltpu.VMEM((depth + 1, rows, lanes), f32),
            dma((4,)),
            dma((8,)),
            dma((8,)),
            dma((6,)),
            dma((6,)),
            dma,
            dma,
            pltpu.SemaphoreType.REGULAR,
            dma((2,)),
            dma((2,)),
            dma((2,)),
            dma((2,)),
        ],
        compiler_params=pltpu.CompilerParams(
            collective_id=0, has_side_effects=True, vmem_limit_bytes=32 * 1024 * 1024
        ),
    )(*[pltpu.with_memory_space_constraint(v, pltpu.HBM) for v in (permeability[0], saturation[0], pressure_old[0], source)])
    return outs[0][None], outs[1][None]


def solution(mesh):
    wide = P(None, None, "gx", "gy")
    return jax.shard_map(
        functools.partial(local, mesh.shape["gx"], mesh.shape["gy"]),
        mesh=mesh,
        in_specs=(wide, wide, wide, P(None, "gx", "gy")),
        out_specs=(wide, wide),
        check_vma=False,
    )
```

```python
import functools

import jax
import jax.numpy as jnp
from jax import lax
from jax.experimental import pallas as pl
from jax.experimental.pallas import tpu as pltpu
from jax.sharding import PartitionSpec as P

HALO = 4
BLOCK = 4
STORAGE = 0.5
VERTICAL = 0.1
STEP = 0.05
WATER = 1.0
OIL = 2.0
MESH = pl.DeviceIdType.MESH


def iota(shape, dim):
    return lax.broadcasted_iota(jnp.int32, shape, dim)


class Field:
    def __init__(self, blocks, side):
        self.blocks, self.side = blocks, side

    def at(self, i):
        return self.side if i is None else self.blocks[i]


def row_roll(v, shift):
    axis = v.ndim - 2
    return pltpu.roll(v, shift % v.shape[axis], axis)


def lane_roll(v, shift):
    axis = v.ndim - 1
    shift = shift % v.shape[axis]
    return v if shift == 0 else pltpu.roll(v, shift, axis)


def x_next(f, i):
    return row_roll(f.at(i), -1)


def x_prev(f, i):
    return row_roll(f.at(i), 1)


def z_next(f, i):
    width = 2 * HALO
    if i is None:
        lanes = f.side.shape[1]
        return jnp.where(iota(f.side.shape, 1) < lanes - width, lane_roll(f.side, -width), 0.0)
    b = f.blocks[i]
    last = f.blocks[i + 1][:1] if i + 1 < len(f.blocks) else jnp.zeros_like(b[:1])
    return jnp.concatenate([b[1:], last], axis=0)


def z_prev(f, i):
    width = 2 * HALO
    if i is None:
        return jnp.where(iota(f.side.shape, 1) >= width, lane_roll(f.side, width), 0.0)
    b = f.blocks[i]
    first = f.blocks[i - 1][-1:] if i else jnp.zeros_like(b[:1])
    return jnp.concatenate([first, b[:-1]], axis=0)


def inserted(side, i, lane_from, lane_to):
    planes = range(i * BLOCK, (i + 1) * BLOCK)
    return jnp.stack([lane_roll(side, lane_to - (2 * HALO * z + lane_from)) for z in planes], axis=0)


def gathered(blocks, lane_from, lane_to, base):
    width = 2 * HALO
    lane = iota(base.shape, 1)
    for i, b in enumerate(blocks):
        for j in range(BLOCK):
            to = width * (i * BLOCK + j) + lane_to
            base = jnp.where(lane == to, lane_roll(b[j], to - lane_from), base)
    return base


def y_next(f, i):
    if i is None:
        return gathered(f.blocks, 0, 2 * HALO - 1, lane_roll(f.side, -1))
    b = f.blocks[i]
    lanes = b.shape[2]
    return jnp.where(iota(b.shape, 2) == lanes - 1, inserted(f.side, i, 0, lanes - 1), lane_roll(b, -1))


def y_prev(f, i):
    if i is None:
        return gathered(f.blocks, f.blocks[0].shape[2] - 1, 0, lane_roll(f.side, 1))
    b = f.blocks[i]
    return jnp.where(iota(b.shape, 2) == 0, inserted(f.side, i, 2 * HALO - 1, 0), lane_roll(b, 1))


def inverted(v):
    r = pl.reciprocal(v, approx=True)
    r = r * (2.0 - v * r)
    return r * (2.0 - v * r)


def y_both(f):
    width = 2 * HALO
    side = f.side
    lane = iota(side.shape, 1)
    column = lane % width
    edges = jnp.where(column == 0, lane_roll(side, 1 - width), lane_roll(side, -1))
    ends = jnp.zeros_like(side)
    nexts, prevs = [], []
    for i, b in enumerate(f.blocks):
        put = jnp.stack([lane_roll(edges, -width * (i * BLOCK + j)) for j in range(BLOCK)], axis=0)
        at_lane = iota(b.shape, 2)
        up = lane_roll(b, 1)
        nexts.append(jnp.where(at_lane == b.shape[2] - 1, put, lane_roll(b, -1)))
        prevs.append(jnp.where(at_lane == 0, put, up))
        for j in range(BLOCK):
            z = i * BLOCK + j
            ends = jnp.where(lane // width == z, lane_roll(up[j], width * z), ends)
    side_next = jnp.where(column == width - 1, lane_roll(ends, width - 2), lane_roll(side, -1))
    side_prev = jnp.where(column == 0, ends, lane_roll(side, 1))
    return Field(nexts, side_next), Field(prevs, side_prev)


def mobility(s):
    return s * s / WATER + (1.0 - s) * (1.0 - s) / OIL


def fraction(s):
    water = s * s / WATER
    return water * inverted(water + (1.0 - s) * (1.0 - s) / OIL)


def coefficient(scaling):
    def fn(ka, kb, ma, mb):
        return (scaling * ka * kb) * inverted(jnp.maximum(ka + kb, 1e-20)) * (ma + mb)

    return fn


NEXT = (z_next, x_next, y_next)
PREV = (z_prev, x_prev, y_prev)


def build(fn, count):
    side = fn(None)
    blocks = [fn(i) for i in range(count)]
    return [Field([b[n] for b in blocks], side[n]) for n in range(len(side))]


def add(*terms):
    total = terms[0]
    for t in terms[1:]:
        total = total + t
    return total


def packed(own):
    depth, rows, lanes = own.shape
    width = 2 * HALO
    edge = jnp.where(iota(own.shape, 2) < HALO, own, lane_roll(own, width))
    block = iota((rows, lanes), 1) // width
    out = edge[0]
    for z in range(1, depth):
        out = jnp.where(block == z, lane_roll(edge[z], width * z), out)
    return out


def kernel(nx, ny, k_in, s_in, x_in, q_in, out_ref, main_ref, pack_ref, side_ref, slots,
           late_send, late_recv, early_send, early_recv, load_sem, xsend, xrecv, psend, precv, rsend, rrecv, ready, lsem, lrecv, esem, erecv):
    gx, gy = lax.axis_index("gx"), lax.axis_index("gy")
    ins = (k_in, s_in, x_in, q_in)
    rows = k_in.shape[1]
    wide = rows + 2 * HALO

    def has(dx, dy):
        ok = None
        for d, at, n in ((dx, gx, nx), (dy, gy, ny)):
            if d:
                one = at + d >= 0 if d < 0 else at + d < n
                ok = one if ok is None else ok & one
        return ok

    def at(dx, dy):
        return {"gx": gx + dx, "gy": gy + dy}

    diagonals = [(dx, dy) for dx in (-1, 1) for dy in (-1, 1)]

    loads = [pltpu.make_async_copy(ref, main_ref.at[i, :, pl.ds(0, rows)], load_sem.at[i]) for i, ref in enumerate(ins)]
    for copy in loads:
        copy.start()

    barrier = pltpu.get_barrier_semaphore()
    expected = jnp.int32(nx - 1 + ny - 1)
    for off in range(1, nx):
        pl.semaphore_signal(barrier, inc=1, device_id={"gx": lax.rem(gx + off, nx), "gy": gy}, device_id_type=MESH)
    for off in range(1, ny):
        pl.semaphore_signal(barrier, inc=1, device_id={"gx": gx, "gy": lax.rem(gy + off, ny)}, device_id_type=MESH)
    for dx, dy in diagonals:
        @pl.when(has(dx, dy))
        def _():
            pl.semaphore_signal(barrier, inc=1, device_id=at(dx, dy), device_id_type=MESH)

        expected = expected + has(dx, dy).astype(jnp.int32)

    reach = (2, 2, 2, 1)

    def edge_rows(dx, width):
        return pl.ds(0, width) if dx < 0 else pl.ds(rows - width, width)

    def halo_rows(dx, width):
        return pl.ds(rows, width) if dx < 0 else pl.ds(wide - width, width)

    def x_copies(dx, halves=(0, 1)):
        d = (dx + 1) // 2
        return [
            pltpu.make_async_remote_copy(
                src_ref=ref.at[:, edge_rows(dx, reach[i])],
                dst_ref=main_ref.at[i, :, halo_rows(dx, reach[i])],
                send_sem=xsend.at[d * len(ins) + i],
                recv_sem=xrecv.at[d * len(ins) + i],
                device_id=at(dx, 0),
                device_id_type=MESH,
            )
            for i, ref in enumerate(ins)
            if i // 2 in halves
        ]

    def y_copy(dx, dy):
        number = (dx + 1) * 2 + (dy + 1) // 2
        from_rows = to_rows = pl.ds(0, rows)
        if dx:
            from_rows, to_rows = edge_rows(dx, reach[0]), halo_rows(dx, reach[0])
        return pltpu.make_async_remote_copy(
            src_ref=pack_ref.at[:, from_rows],
            dst_ref=side_ref.at[(1 - dy) // 2, :, to_rows],
            send_sem=psend.at[number],
            recv_sem=precv.at[number],
            device_id=at(dx, dy),
            device_id_type=MESH,
        )

    def line_copy(dx, src, dst, send, recv):
        line = pl.ds(1, 1) if dx < 0 else pl.ds(rows - 2, 1)
        d = (dx + 1) // 2
        return pltpu.make_async_remote_copy(
            src_ref=src.at[:, line],
            dst_ref=dst.at[:, line],
            send_sem=send.at[d],
            recv_sem=recv.at[d],
            device_id=at(dx, 0),
            device_id_type=MESH,
        )

    def early_copy(dx):
        return line_copy(dx, early_send, early_recv, esem, erecv)

    def late_copy(dx):
        return line_copy(dx, late_send, late_recv, lsem, lrecv)

    y_moves = [(0, 1), (0, -1)] + diagonals

    for i in range(len(ins)):
        loads[i].wait()
        pack_ref[i] = packed(main_ref[i, :, 0:rows, :])

    pl.semaphore_wait(barrier, expected)
    for dx, dy in y_moves:
        @pl.when(has(dx, dy))
        def _():
            y_copy(dx, dy).start()

    for half in range(2):
        for dx in (-1, 1):
            @pl.when(has(dx, 0))
            def _():
                for copy in x_copies(dx, (half,)):
                    copy.start()

    for off in range(1, nx):
        pl.semaphore_signal(ready, inc=1, device_id={"gx": lax.rem(gx + off, nx), "gy": gy}, device_id_type=MESH)

    def arrive_y(moves):
        for dx, dy in moves:
            @pl.when(has(-dx, -dy))
            def _():
                y_copy(dx, dy).wait_recv()

    def arrive_x(half):
        for dx in (-1, 1):
            @pl.when(has(-dx, 0))
            def _():
                for copy in x_copies(dx, (half,)):
                    copy.wait_recv()

    lanes = k_in.shape[2]
    depth = k_in.shape[0]
    row = iota((wide, lanes), 0)
    lane = iota((wide, lanes), 1)
    right = lane % (2 * HALO) < HALO

    nb = depth // BLOCK

    def field(i, high):
        at_row, at_right = row[:high], right[:high]
        inside = (
            (at_row < rows)
            | ((at_row < rows + reach[i]) & (gx + 1 < nx))
            | ((at_row >= wide - reach[i]) & (gx > 0))
        )
        inside_right = at_right & inside & (gy + 1 < ny)
        inside_left = jnp.logical_not(at_right) & inside & (gy > 0)
        blocks = [main_ref[i, n * BLOCK : (n + 1) * BLOCK, 0:high] for n in range(nb)]
        if high > rows:
            blocks = [jnp.where(inside[None], b, 0.0) for b in blocks]
        side = jnp.where(
            inside_right, side_ref[1, i, 0:high], jnp.where(inside_left, side_ref[0, i, 0:high], 0.0)
        )
        return Field(blocks, side)

    def own(f):
        return jnp.concatenate([b[:, :rows] for b in f.blocks], axis=0)

    def zy_faces(k, s):
        (mob,) = build(lambda i: [mobility(s.at(i))], nb)
        coefs = [Field([], None) for _ in range(2)]
        before = [Field([], None) for _ in range(2)]

        def face(i):
            return [
                coefficient(sc)(k.at(i), nxt(k, i), mob.at(i), nxt(mob, i))
                for nxt, sc in ((z_next, VERTICAL), (y_next, 1.0))
            ]

        def behind(i):
            return [prv(c, i) for prv, c in zip((z_prev, y_prev), coefs)]

        for c, value in zip(coefs, face(None)):
            c.side = value
        for i in range(nb):
            for c, value in zip(coefs, face(i)):
                c.blocks.append(value)
            for c, value in zip(before, behind(i)):
                c.blocks.append(value)
        for c, value in zip(before, behind(None)):
            c.side = value
        return mob, coefs, before

    def x_faces(k, mob):
        (c,) = build(
            lambda i: [coefficient(1.0)(k.at(i), x_next(k, i), mob.at(i), x_next(mob, i))], nb
        )
        (b,) = build(lambda i: [x_prev(c, i)], nb)
        return c, b

    def zy_diag(coefs, before):
        return build(lambda i: [add(STORAGE, *[f.at(i) for f in coefs + before])], nb)[0]

    def zy_around(v, coefs, before):
        ahead, back = y_both(v)
        return build(
            lambda i: [
                coefs[0].at(i) * z_next(v, i)
                + before[0].at(i) * z_prev(v, i)
                + coefs[1].at(i) * ahead.at(i)
                + before[1].at(i) * back.at(i)
            ],
            nb,
        )[0]

    def x_around(v, c, b, i):
        return c.at(i) * x_next(v, i) + b.at(i) * x_prev(v, i)

    def whole_diag(partial, c, b):
        return build(lambda i: (lambda d: [d, inverted(d)])(partial.at(i) + c.at(i) + b.at(i)), nb)

    def start_field(x0, q, partial, c, b, diag, inverse):
        return build(
            lambda i: [
                (q.at(i) + STORAGE * x0.at(i) - (diag.at(i) * x0.at(i) - (partial.at(i) + x_around(x0, c, b, i))))
                * inverse.at(i)
            ],
            nb,
        )[0]

    def lower(f):
        return Field([b[:, rows:] for b in f.blocks], f.side[rows:])

    def join(f, g):
        return Field(
            [jnp.concatenate([a, b], axis=1) for a, b in zip(f.blocks, g.blocks)],
            jnp.concatenate([f.side, g.side], axis=0),
        )

    arrive_y(y_moves[:2])
    k, s = field(0, rows), field(1, rows)
    own_mob, own_coefs, own_before = zy_faces(k, s)
    own_diag = zy_diag(own_coefs, own_before)
    x_coef, x_before = x_faces(k, own_mob)
    diag, inverse = whole_diag(own_diag, x_coef, x_before)
    x0 = field(2, rows)
    own_around = zy_around(x0, own_coefs, own_before)
    u0 = start_field(x0, field(3, rows), own_around, x_coef, x_before, diag, inverse)
    for i, b in enumerate(u0.blocks):
        early_send[i * BLOCK : (i + 1) * BLOCK] = b
    early_send[depth] = u0.side
    for dx in (-1, 1):
        @pl.when(has(dx, 0))
        def _():
            early_copy(dx).start()

    line_row = iota((rows, lanes), 0)
    taken = ((line_row == 1) & (gx + 1 < nx)) | ((line_row == rows - 2) & (gx > 0))

    def patched(value, ref, planes):
        cut = value[..., :rows, :], value[..., rows:, :]
        return jnp.concatenate([cut[0], jnp.where(taken, ref[planes], cut[1])], axis=-2)

    def patch(f, ref):
        f.blocks = [patched(b, ref, slice(i * BLOCK, (i + 1) * BLOCK)) for i, b in enumerate(f.blocks)]

    arrive_y(y_moves[2:])
    arrive_x(0)
    k, s = field(0, wide), field(1, wide)
    halo_mob, halo_coefs, halo_before = zy_faces(lower(k), lower(s))
    halo_diag = zy_diag(halo_coefs, halo_before)
    x_coef, x_before = x_faces(k, join(own_mob, halo_mob))
    diag, inverse = whole_diag(join(own_diag, halo_diag), x_coef, x_before)
    z_coef, y_coef = [join(f, g) for f, g in zip(own_coefs, halo_coefs)]
    z_before, y_before = [join(f, g) for f, g in zip(own_before, halo_before)]
    coefs = (z_coef, x_coef, y_coef)
    arrive_x(1)
    x0, q = field(2, wide), field(3, wide)
    partial = join(own_around, zy_around(lower(x0), halo_coefs, halo_before))
    u0 = start_field(x0, q, partial, x_coef, x_before, diag, inverse)
    for dx in (-1, 1):
        @pl.when(has(-dx, 0))
        def _():
            early_copy(dx).wait_recv()

    patch(u0, early_recv)
    u0.side = patched(u0.side, early_recv, depth)
    def around(v):
        partial = zy_around(v, (z_coef, y_coef), (z_before, y_before))
        return lambda i: partial.at(i) + x_around(v, x_coef, x_before, i)

    near = around(u0)
    (u1,) = build(lambda i: [u0.at(i) - near(i) * inverse.at(i)], nb)
    near = around(u1)
    sums = [0.0] * 4
    for i in range(nb):
        d, a, b = [f.blocks[i][:, :rows] for f in (diag, u0, u1)]
        da, db = d * a, d * b
        image = db - near(i)[:, :rows]
        for n, value in enumerate((da * a, da * b, db * b, b * image)):
            sums[n] = sums[n] + jnp.sum(value, axis=0)

    tile_row = iota((rows, lanes), 0)
    part = jnp.zeros((rows, lanes), jnp.float32)
    for i, value in enumerate(sums):
        part = jnp.where(tile_row == i, jnp.sum(value, axis=0, keepdims=True), part)

    late_send[...] = own(u1)

    count = nx * ny
    group = lanes // 4
    folded = part + lane_roll(part, lanes // 2)
    folded = folded + lane_roll(folded, lanes // 4)
    mine = iota((rows, lanes), 1) // group == iota((rows, lanes), 0)
    slots[0:1, :] = jnp.sum(jnp.where(mine, folded, 0.0), axis=0, keepdims=True)
    me = gx * ny + gy

    def share_copy(off, first, size):
        target = lax.rem(me + off, count)
        return pltpu.make_async_remote_copy(
            src_ref=slots.at[pl.ds(0 if size == 1 else first, size)],
            dst_ref=slots.at[pl.ds(first, size)],
            send_sem=rsend,
            recv_sem=rrecv,
            device_id={"gx": target // ny, "gy": target % ny},
            device_id_type=MESH,
        )

    pl.semaphore_wait(ready, nx - 1)
    for off in range(1, count):
        share_copy(off, off, 1).start()

    def gained(i, frac):
        return jnp.maximum(q.at(i), 0.0) + jnp.minimum(q.at(i), 0.0) * frac

    for dx in (-1, 1):
        @pl.when(has(dx, 0))
        def _():
            late_copy(dx).start()

    (frac,) = build(lambda i: [fraction(s.at(i))], nb)
    (gain,) = build(lambda i: [gained(i, frac.at(i))], nb)
    after = build(lambda i: [nxt(frac, i) for nxt in NEXT], nb)
    for dx in (-1, 1):
        @pl.when(has(-dx, 0))
        def _():
            late_copy(dx).wait_recv()

    patch(u1, late_recv)
    share_copy(1, 1, count - 1).wait_recv()
    total = jnp.sum(slots[...], axis=0, keepdims=True)
    sums = jnp.sum(jnp.where(mine, total, 0.0), axis=1, keepdims=True)
    sa, sb, sc, sd = (sums[i : i + 1, :] for i in range(4))
    step0 = sa / sb
    next_energy = step0 * step0 * sc - sa
    conjugacy = next_energy / sa
    curvature = sb - 2.0 * step0 * sc + step0 * step0 * sd
    step1 = next_energy / (curvature - conjugacy * next_energy / step0)
    weight0 = step0 + step1 * (1.0 + conjugacy)
    weight1 = -step1 * step0

    (pressure,) = build(lambda i: [x0.at(i) + weight0 * u0.at(i) + weight1 * u1.at(i)], nb)
    flows = [Field([], None) for _ in NEXT]

    def flux(i):
        return [c.at(i) * (pressure.at(i) - nxt(pressure, i)) for nxt, c in zip(NEXT, coefs)]

    def water_at(i, frac, nexts):
        return [
            f.at(i) * jnp.where(f.at(i) > 0.0, frac.at(i), n) for f, n in zip(flows, nexts)
        ]

    def moved(i, current, gain, water):
        return current + STEP * add(gain, *[prv(w, i) - w.at(i) for prv, w in zip(PREV, water)])

    water = [Field([], None) for _ in NEXT]
    first = Field([], None)
    for f, value in zip(flows, flux(None)):
        f.side = value
    for w, value in zip(water, water_at(None, frac, [n.side for n in after])):
        w.side = value
    for i in range(nb):
        out_ref[0, i * BLOCK : (i + 1) * BLOCK] = pressure.blocks[i][:, :rows]
        for f, value in zip(flows, flux(i)):
            f.blocks.append(value)
        for w, value in zip(water, water_at(i, frac, [n.blocks[i] for n in after])):
            w.blocks.append(value)
        first.blocks.append(moved(i, s.blocks[i], gain.blocks[i], water))
    first.side = moved(None, s.side, gain.side, water)

    (frac,) = build(lambda i: [fraction(first.at(i))], nb)
    water = [Field([], None) for _ in NEXT]
    for w, value in zip(water, water_at(None, frac, [nxt(frac, None) for nxt in NEXT])):
        w.side = value
    for i in range(nb):
        for w, value in zip(water, water_at(i, frac, [nxt(frac, i) for nxt in NEXT])):
            w.blocks.append(value)
        second = moved(i, first.blocks[i], gained(i, frac.blocks[i]), water)
        out_ref[1, i * BLOCK : (i + 1) * BLOCK] = second[:, :rows]

    for dx in (-1, 1):
        @pl.when(has(dx, 0))
        def _():
            for copy in x_copies(dx):
                copy.wait_send()
            early_copy(dx).wait_send()
            late_copy(dx).wait_send()

    for dx, dy in y_moves:
        @pl.when(has(dx, dy))
        def _():
            y_copy(dx, dy).wait_send()

    share_copy(1, 1, count - 1).wait_send()


def local(nx, ny, permeability, saturation, pressure_old, source):
    shape = source.shape
    depth, rows, lanes = shape
    assert permeability.shape[0] == 1 and depth % BLOCK == 0 and depth * 2 * HALO == lanes and rows == 2 * HALO
    wide = rows + 2 * HALO
    f32 = jnp.float32
    dma = pltpu.SemaphoreType.DMA
    outs = pl.pallas_call(
        functools.partial(kernel, nx, ny),
        out_shape=jax.ShapeDtypeStruct((2,) + shape, f32),
        in_specs=[pl.BlockSpec(memory_space=pltpu.HBM)] * 4,
        out_specs=pl.BlockSpec(memory_space=pltpu.VMEM),
        scratch_shapes=[
            pltpu.VMEM((4, depth, wide, lanes), f32),
            pltpu.VMEM((4, rows, lanes), f32),
            pltpu.VMEM((2, 4, wide, lanes), f32),
            pltpu.VMEM((nx * ny, lanes), f32),
            pltpu.VMEM(shape, f32),
            pltpu.VMEM(shape, f32),
            pltpu.VMEM((depth + 1, rows, lanes), f32),
            pltpu.VMEM((depth + 1, rows, lanes), f32),
            dma((4,)),
            dma((8,)),
            dma((8,)),
            dma((6,)),
            dma((6,)),
            dma,
            dma,
            pltpu.SemaphoreType.REGULAR,
            dma((2,)),
            dma((2,)),
            dma((2,)),
            dma((2,)),
        ],
        compiler_params=pltpu.CompilerParams(
            collective_id=0, has_side_effects=True, vmem_limit_bytes=32 * 1024 * 1024
        ),
    )(*[pltpu.with_memory_space_constraint(v, pltpu.HBM) for v in (permeability[0], saturation[0], pressure_old[0], source)])
    return outs[:1], outs[1:]


def solution(mesh):
    wide = P(None, None, "gx", "gy")
    return jax.shard_map(
        functools.partial(local, mesh.shape["gx"], mesh.shape["gy"]),
        mesh=mesh,
        in_specs=(wide, wide, wide, P(None, "gx", "gy")),
        out_specs=(wide, wide),
        check_vma=False,
    )
```

```python
import functools

import jax
import jax.numpy as jnp
from jax import lax
from jax.experimental import pallas as pl
from jax.experimental.pallas import tpu as pltpu
from jax.sharding import PartitionSpec as P

HALO = 4
BLOCK = 4
STORAGE = 0.5
VERTICAL = 0.1
STEP = 0.05
WATER = 1.0
OIL = 2.0
MESH = pl.DeviceIdType.MESH


def iota(shape, dim):
    return lax.broadcasted_iota(jnp.int32, shape, dim)


class Field:
    def __init__(self, blocks, side):
        self.blocks, self.side = blocks, side

    def at(self, i):
        return self.side if i is None else self.blocks[i]


def row_roll(v, shift):
    axis = v.ndim - 2
    return pltpu.roll(v, shift % v.shape[axis], axis)


def lane_roll(v, shift):
    axis = v.ndim - 1
    shift = shift % v.shape[axis]
    return v if shift == 0 else pltpu.roll(v, shift, axis)


def x_next(f, i):
    return row_roll(f.at(i), -1)


def x_prev(f, i):
    return row_roll(f.at(i), 1)


def z_next(f, i):
    width = 2 * HALO
    if i is None:
        lanes = f.side.shape[1]
        return jnp.where(iota(f.side.shape, 1) < lanes - width, lane_roll(f.side, -width), 0.0)
    b = f.blocks[i]
    last = f.blocks[i + 1][:1] if i + 1 < len(f.blocks) else jnp.zeros_like(b[:1])
    return jnp.concatenate([b[1:], last], axis=0)


def z_prev(f, i):
    width = 2 * HALO
    if i is None:
        return jnp.where(iota(f.side.shape, 1) >= width, lane_roll(f.side, width), 0.0)
    b = f.blocks[i]
    first = f.blocks[i - 1][-1:] if i else jnp.zeros_like(b[:1])
    return jnp.concatenate([first, b[:-1]], axis=0)


def inserted(side, i, lane_from, lane_to):
    planes = range(i * BLOCK, (i + 1) * BLOCK)
    return jnp.stack([lane_roll(side, lane_to - (2 * HALO * z + lane_from)) for z in planes], axis=0)


def gathered(blocks, lane_from, lane_to, base):
    width = 2 * HALO
    lane = iota(base.shape, 1)
    for i, b in enumerate(blocks):
        for j in range(BLOCK):
            to = width * (i * BLOCK + j) + lane_to
            base = jnp.where(lane == to, lane_roll(b[j], to - lane_from), base)
    return base


def y_next(f, i):
    if i is None:
        return gathered(f.blocks, 0, 2 * HALO - 1, lane_roll(f.side, -1))
    b = f.blocks[i]
    lanes = b.shape[2]
    return jnp.where(iota(b.shape, 2) == lanes - 1, inserted(f.side, i, 0, lanes - 1), lane_roll(b, -1))


def y_prev(f, i):
    if i is None:
        return gathered(f.blocks, f.blocks[0].shape[2] - 1, 0, lane_roll(f.side, 1))
    b = f.blocks[i]
    return jnp.where(iota(b.shape, 2) == 0, inserted(f.side, i, 2 * HALO - 1, 0), lane_roll(b, 1))


def inverted(v):
    r = pl.reciprocal(v, approx=True)
    r = r * (2.0 - v * r)
    return r * (2.0 - v * r)


def y_both(f):
    width = 2 * HALO
    side = f.side
    lane = iota(side.shape, 1)
    column = lane % width
    edges = jnp.where(column == 0, lane_roll(side, 1 - width), lane_roll(side, -1))
    ends = jnp.zeros_like(side)
    nexts, prevs = [], []
    for i, b in enumerate(f.blocks):
        put = jnp.stack([lane_roll(edges, -width * (i * BLOCK + j)) for j in range(BLOCK)], axis=0)
        at_lane = iota(b.shape, 2)
        up = lane_roll(b, 1)
        nexts.append(jnp.where(at_lane == b.shape[2] - 1, put, lane_roll(b, -1)))
        prevs.append(jnp.where(at_lane == 0, put, up))
        for j in range(BLOCK):
            z = i * BLOCK + j
            ends = jnp.where(lane // width == z, lane_roll(up[j], width * z), ends)
    side_next = jnp.where(column == width - 1, lane_roll(ends, width - 2), lane_roll(side, -1))
    side_prev = jnp.where(column == 0, ends, lane_roll(side, 1))
    return Field(nexts, side_next), Field(prevs, side_prev)


def mobility(s):
    return s * s / WATER + (1.0 - s) * (1.0 - s) / OIL


def fraction(s):
    water = s * s / WATER
    return water * inverted(water + (1.0 - s) * (1.0 - s) / OIL)


def coefficient(scaling):
    def fn(ka, kb, ma, mb):
        return (scaling * ka * kb) * inverted(jnp.maximum(ka + kb, 1e-20)) * (ma + mb)

    return fn


NEXT = (z_next, x_next, y_next)
PREV = (z_prev, x_prev, y_prev)


def build(fn, count):
    side = fn(None)
    blocks = [fn(i) for i in range(count)]
    return [Field([b[n] for b in blocks], side[n]) for n in range(len(side))]


def add(*terms):
    total = terms[0]
    for t in terms[1:]:
        total = total + t
    return total


def packed(own):
    depth, rows, lanes = own.shape
    width = 2 * HALO
    edge = jnp.where(iota(own.shape, 2) < HALO, own, lane_roll(own, width))
    block = iota((rows, lanes), 1) // width
    out = edge[0]
    for z in range(1, depth):
        out = jnp.where(block == z, lane_roll(edge[z], width * z), out)
    return out


def kernel(nx, ny, k_in, s_in, x_in, q_in, out_ref, main_ref, pack_ref, side_ref, slots,
           late_send, late_recv, early_send, early_recv, load_sem, xsend, xrecv, psend, precv, rsend, rrecv, ready, lsem, lrecv, esem, erecv):
    gx, gy = lax.axis_index("gx"), lax.axis_index("gy")
    ins = (k_in, s_in, x_in, q_in)
    rows = k_in.shape[1]
    wide = rows + 2 * HALO

    def has(dx, dy):
        ok = None
        for d, at, n in ((dx, gx, nx), (dy, gy, ny)):
            if d:
                one = at + d >= 0 if d < 0 else at + d < n
                ok = one if ok is None else ok & one
        return ok

    def at(dx, dy):
        return {"gx": gx + dx, "gy": gy + dy}

    diagonals = [(dx, dy) for dx in (-1, 1) for dy in (-1, 1)]

    loads = [pltpu.make_async_copy(ref, main_ref.at[i, :, pl.ds(0, rows)], load_sem.at[i]) for i, ref in enumerate(ins)]
    for copy in loads:
        copy.start()

    barrier = pltpu.get_barrier_semaphore()
    expected = jnp.int32(nx - 1 + ny - 1)
    for off in range(1, nx):
        pl.semaphore_signal(barrier, inc=1, device_id={"gx": lax.rem(gx + off, nx), "gy": gy}, device_id_type=MESH)
    for off in range(1, ny):
        pl.semaphore_signal(barrier, inc=1, device_id={"gx": gx, "gy": lax.rem(gy + off, ny)}, device_id_type=MESH)
    for dx, dy in diagonals:
        @pl.when(has(dx, dy))
        def _():
            pl.semaphore_signal(barrier, inc=1, device_id=at(dx, dy), device_id_type=MESH)

        expected = expected + has(dx, dy).astype(jnp.int32)

    reach = (2, 2, 2, 1)

    def edge_rows(dx, width):
        return pl.ds(0, width) if dx < 0 else pl.ds(rows - width, width)

    def halo_rows(dx, width):
        return pl.ds(rows, width) if dx < 0 else pl.ds(wide - width, width)

    def x_copies(dx, halves=(0, 1)):
        d = (dx + 1) // 2
        return [
            pltpu.make_async_remote_copy(
                src_ref=ref.at[:, edge_rows(dx, reach[i])],
                dst_ref=main_ref.at[i, :, halo_rows(dx, reach[i])],
                send_sem=xsend.at[d * len(ins) + i],
                recv_sem=xrecv.at[d * len(ins) + i],
                device_id=at(dx, 0),
                device_id_type=MESH,
            )
            for i, ref in enumerate(ins)
            if i // 2 in halves
        ]

    def y_copy(dx, dy):
        number = (dx + 1) * 2 + (dy + 1) // 2
        from_rows = to_rows = pl.ds(0, rows)
        if dx:
            from_rows, to_rows = edge_rows(dx, reach[0]), halo_rows(dx, reach[0])
        return pltpu.make_async_remote_copy(
            src_ref=pack_ref.at[:, from_rows],
            dst_ref=side_ref.at[(1 - dy) // 2, :, to_rows],
            send_sem=psend.at[number],
            recv_sem=precv.at[number],
            device_id=at(dx, dy),
            device_id_type=MESH,
        )

    def line_copy(dx, src, dst, send, recv):
        line = pl.ds(1, 1) if dx < 0 else pl.ds(rows - 2, 1)
        d = (dx + 1) // 2
        return pltpu.make_async_remote_copy(
            src_ref=src.at[:, line],
            dst_ref=dst.at[:, line],
            send_sem=send.at[d],
            recv_sem=recv.at[d],
            device_id=at(dx, 0),
            device_id_type=MESH,
        )

    def early_copy(dx):
        return line_copy(dx, early_send, early_recv, esem, erecv)

    def late_copy(dx):
        return line_copy(dx, late_send, late_recv, lsem, lrecv)

    y_moves = [(0, 1), (0, -1)] + diagonals

    for i in range(len(ins)):
        loads[i].wait()
        pack_ref[i] = packed(main_ref[i, :, 0:rows, :])

    pl.semaphore_wait(barrier, expected)
    for dx, dy in y_moves:
        @pl.when(has(dx, dy))
        def _():
            y_copy(dx, dy).start()

    for half in range(2):
        for dx in (-1, 1):
            @pl.when(has(dx, 0))
            def _():
                for copy in x_copies(dx, (half,)):
                    copy.start()

    for off in range(1, nx):
        pl.semaphore_signal(ready, inc=1, device_id={"gx": lax.rem(gx + off, nx), "gy": gy}, device_id_type=MESH)

    def arrive_y(moves):
        for dx, dy in moves:
            @pl.when(has(-dx, -dy))
            def _():
                y_copy(dx, dy).wait_recv()

    def arrive_x(half):
        for dx in (-1, 1):
            @pl.when(has(-dx, 0))
            def _():
                for copy in x_copies(dx, (half,)):
                    copy.wait_recv()

    lanes = k_in.shape[2]
    depth = k_in.shape[0]
    row = iota((wide, lanes), 0)
    lane = iota((wide, lanes), 1)
    right = lane % (2 * HALO) < HALO

    nb = depth // BLOCK

    def inside(i, high):
        at_row = row[:high]
        return (
            (at_row < rows)
            | ((at_row < rows + reach[i]) & (gx + 1 < nx))
            | ((at_row >= wide - reach[i]) & (gx > 0))
        )

    def side_field(i, high):
        here, at_right = inside(i, high), right[:high]
        inside_right = at_right & here & (gy + 1 < ny)
        inside_left = jnp.logical_not(at_right) & here & (gy > 0)
        return jnp.where(
            inside_right, side_ref[1, i, 0:high], jnp.where(inside_left, side_ref[0, i, 0:high], 0.0)
        )

    def field(i):
        here = inside(i, wide)[None]
        blocks = [jnp.where(here, main_ref[i, n * BLOCK : (n + 1) * BLOCK], 0.0) for n in range(nb)]
        return Field(blocks, side_field(i, wide))

    def own(f):
        return jnp.concatenate([b[:, :rows] for b in f.blocks], axis=0)

    def zy_faces(k, s):
        (mob,) = build(lambda i: [mobility(s.at(i))], nb)
        coefs = [Field([], None) for _ in range(2)]
        before = [Field([], None) for _ in range(2)]

        def face(i):
            return [
                coefficient(sc)(k.at(i), nxt(k, i), mob.at(i), nxt(mob, i))
                for nxt, sc in ((z_next, VERTICAL), (y_next, 1.0))
            ]

        def behind(i):
            return [prv(c, i) for prv, c in zip((z_prev, y_prev), coefs)]

        for c, value in zip(coefs, face(None)):
            c.side = value
        for i in range(nb):
            for c, value in zip(coefs, face(i)):
                c.blocks.append(value)
            for c, value in zip(before, behind(i)):
                c.blocks.append(value)
        for c, value in zip(before, behind(None)):
            c.side = value
        return mob, coefs, before

    def x_faces(k, mob):
        (c,) = build(
            lambda i: [coefficient(1.0)(k.at(i), x_next(k, i), mob.at(i), x_next(mob, i))], nb
        )
        (b,) = build(lambda i: [x_prev(c, i)], nb)
        return c, b

    def zy_diag(coefs, before):
        return build(lambda i: [add(STORAGE, *[f.at(i) for f in coefs + before])], nb)[0]

    def zy_around(v, coefs, before):
        ahead, back = y_both(v)
        return build(
            lambda i: [
                coefs[0].at(i) * z_next(v, i)
                + before[0].at(i) * z_prev(v, i)
                + coefs[1].at(i) * ahead.at(i)
                + before[1].at(i) * back.at(i)
            ],
            nb,
        )[0]

    def x_around(v, c, b, i):
        return c.at(i) * x_next(v, i) + b.at(i) * x_prev(v, i)

    def whole_diag(partial, c, b):
        return build(lambda i: (lambda d: [d, inverted(d)])(partial.at(i) + c.at(i) + b.at(i)), nb)

    def start_field(x0, q, partial, c, b, diag, inverse):
        return build(
            lambda i: [
                (q.at(i) + STORAGE * x0.at(i) - (diag.at(i) * x0.at(i) - (partial.at(i) + x_around(x0, c, b, i))))
                * inverse.at(i)
            ],
            nb,
        )[0]

    def lower(f):
        return Field([b[:, rows:] for b in f.blocks], f.side[rows:])

    def join(f, g):
        return Field(
            [jnp.concatenate([a, b], axis=1) for a, b in zip(f.blocks, g.blocks)],
            jnp.concatenate([f.side, g.side], axis=0),
        )

    each = range(nb)
    k, s, x0, q = (Field([main_ref[i, n * BLOCK : (n + 1) * BLOCK, 0:rows] for n in each], None) for i in range(4))
    own_mob = Field([mobility(b) for b in s.blocks], None)

    def face_at(nxt, scaling, i):
        return coefficient(scaling)(k.at(i), nxt(k, i), own_mob.at(i), nxt(own_mob, i))

    z_coef = Field([face_at(z_next, VERTICAL, i) for i in each], None)
    z_before = Field([z_prev(z_coef, i) for i in each], None)
    x_coef = Field([face_at(x_next, 1.0, i) for i in each], None)
    x_before = Field([x_prev(x_coef, i) for i in each], None)

    def z_around(i):
        return z_coef.at(i) * z_next(x0, i) + z_before.at(i) * z_prev(x0, i)

    def z_diag(i):
        return STORAGE + z_coef.at(i) + z_before.at(i)

    z_part = Field([z_around(i) for i in each], None)
    x_part = Field([x_around(x0, x_coef, x_before, i) for i in each], None)
    own_diag = Field([z_diag(i) for i in each], None)

    arrive_y(y_moves[:2])
    for i, f in enumerate((k, s, x0, q)):
        f.side = side_field(i, rows)
    own_mob.side = mobility(s.side)
    z_coef.side = face_at(z_next, VERTICAL, None)
    z_before.side = z_prev(z_coef, None)
    x_coef.side = face_at(x_next, 1.0, None)
    x_before.side = x_prev(x_coef, None)
    z_part.side = z_around(None)
    x_part.side = x_around(x0, x_coef, x_before, None)
    own_diag.side = z_diag(None)
    (y_coef,) = build(lambda i: [face_at(y_next, 1.0, i)], nb)
    (y_before,) = build(lambda i: [y_prev(y_coef, i)], nb)
    (own_diag,) = build(lambda i: [own_diag.at(i) + y_coef.at(i) + y_before.at(i)], nb)
    diag, inverse = whole_diag(own_diag, x_coef, x_before)
    ahead, back = y_both(x0)
    (own_around,) = build(
        lambda i: [z_part.at(i) + y_coef.at(i) * ahead.at(i) + y_before.at(i) * back.at(i)], nb
    )
    own_coefs, own_before = (z_coef, y_coef), (z_before, y_before)
    (u0,) = build(
        lambda i: [
            (q.at(i) + STORAGE * x0.at(i) - (diag.at(i) * x0.at(i) - (own_around.at(i) + x_part.at(i))))
            * inverse.at(i)
        ],
        nb,
    )
    for i, b in enumerate(u0.blocks):
        early_send[i * BLOCK : (i + 1) * BLOCK] = b
    early_send[depth] = u0.side
    for dx in (-1, 1):
        @pl.when(has(dx, 0))
        def _():
            early_copy(dx).start()

    line_row = iota((rows, lanes), 0)
    taken = ((line_row == 1) & (gx + 1 < nx)) | ((line_row == rows - 2) & (gx > 0))

    def patched(value, ref, planes):
        cut = value[..., :rows, :], value[..., rows:, :]
        return jnp.concatenate([cut[0], jnp.where(taken, ref[planes], cut[1])], axis=-2)

    def patch(f, ref):
        f.blocks = [patched(b, ref, slice(i * BLOCK, (i + 1) * BLOCK)) for i, b in enumerate(f.blocks)]

    arrive_y(y_moves[2:])
    arrive_x(0)
    k, s = field(0), field(1)
    halo_mob, halo_coefs, halo_before = zy_faces(lower(k), lower(s))
    halo_diag = zy_diag(halo_coefs, halo_before)
    x_coef, x_before = x_faces(k, join(own_mob, halo_mob))
    diag, inverse = whole_diag(join(own_diag, halo_diag), x_coef, x_before)
    z_coef, y_coef = [join(f, g) for f, g in zip(own_coefs, halo_coefs)]
    z_before, y_before = [join(f, g) for f, g in zip(own_before, halo_before)]
    coefs = (z_coef, x_coef, y_coef)
    arrive_x(1)
    x0, q = field(2), field(3)
    partial = join(own_around, zy_around(lower(x0), halo_coefs, halo_before))
    u0 = start_field(x0, q, partial, x_coef, x_before, diag, inverse)
    for dx in (-1, 1):
        @pl.when(has(-dx, 0))
        def _():
            early_copy(dx).wait_recv()

    patch(u0, early_recv)
    u0.side = patched(u0.side, early_recv, depth)
    def around(v):
        partial = zy_around(v, (z_coef, y_coef), (z_before, y_before))
        return lambda i: partial.at(i) + x_around(v, x_coef, x_before, i)

    near = around(u0)
    (u1,) = build(lambda i: [u0.at(i) - near(i) * inverse.at(i)], nb)
    near = around(u1)
    sums = [0.0] * 4
    for i in range(nb):
        d, a, b = [f.blocks[i][:, :rows] for f in (diag, u0, u1)]
        da, db = d * a, d * b
        image = db - near(i)[:, :rows]
        for n, value in enumerate((da * a, da * b, db * b, b * image)):
            sums[n] = sums[n] + jnp.sum(value, axis=0)

    tile_row = iota((rows, lanes), 0)
    part = jnp.zeros((rows, lanes), jnp.float32)
    for i, value in enumerate(sums):
        part = jnp.where(tile_row == i, jnp.sum(value, axis=0, keepdims=True), part)

    late_send[...] = own(u1)

    count = nx * ny
    group = lanes // 4
    folded = part + lane_roll(part, lanes // 2)
    folded = folded + lane_roll(folded, lanes // 4)
    mine = iota((rows, lanes), 1) // group == iota((rows, lanes), 0)
    slots[0:1, :] = jnp.sum(jnp.where(mine, folded, 0.0), axis=0, keepdims=True)
    me = gx * ny + gy

    def share_copy(off, first, size):
        target = lax.rem(me + off, count)
        return pltpu.make_async_remote_copy(
            src_ref=slots.at[pl.ds(0 if size == 1 else first, size)],
            dst_ref=slots.at[pl.ds(first, size)],
            send_sem=rsend,
            recv_sem=rrecv,
            device_id={"gx": target // ny, "gy": target % ny},
            device_id_type=MESH,
        )

    pl.semaphore_wait(ready, nx - 1)
    for off in range(1, count):
        share_copy(off, off, 1).start()

    def gained(i, frac):
        return jnp.maximum(q.at(i), 0.0) + jnp.minimum(q.at(i), 0.0) * frac

    for dx in (-1, 1):
        @pl.when(has(dx, 0))
        def _():
            late_copy(dx).start()

    (frac,) = build(lambda i: [fraction(s.at(i))], nb)
    (gain,) = build(lambda i: [gained(i, frac.at(i))], nb)
    after = build(lambda i: [nxt(frac, i) for nxt in NEXT], nb)
    for dx in (-1, 1):
        @pl.when(has(-dx, 0))
        def _():
            late_copy(dx).wait_recv()

    patch(u1, late_recv)
    bases = [
        build(lambda i: [c.at(i) * (v.at(i) - nxt(v, i)) for nxt, c in zip(NEXT, coefs)], nb) for v in (x0, u0, u1)
    ]
    for dx in (-1, 1):
        @pl.when(has(dx, 0))
        def _():
            for copy in x_copies(dx):
                copy.wait_send()
            early_copy(dx).wait_send()
            late_copy(dx).wait_send()

    for dx, dy in y_moves:
        @pl.when(has(dx, dy))
        def _():
            y_copy(dx, dy).wait_send()

    share_copy(1, 1, count - 1).wait_send()
    share_copy(1, 1, count - 1).wait_recv()
    total = jnp.sum(slots[...], axis=0, keepdims=True)
    sums = jnp.sum(jnp.where(mine, total, 0.0), axis=1, keepdims=True)
    sa, sb, sc, sd = (sums[i : i + 1, :] for i in range(4))
    step0 = sa / sb
    next_energy = step0 * step0 * sc - sa
    conjugacy = next_energy / sa
    curvature = sb - 2.0 * step0 * sc + step0 * step0 * sd
    step1 = next_energy / (curvature - conjugacy * next_energy / step0)
    weight0 = step0 + step1 * (1.0 + conjugacy)
    weight1 = -step1 * step0

    flows = [Field([], None) for _ in NEXT]

    def flux(i):
        return [x.at(i) + weight0 * a.at(i) + weight1 * b.at(i) for x, a, b in zip(*bases)]

    def water_at(i, frac, nexts):
        return [
            f.at(i) * jnp.where(f.at(i) > 0.0, frac.at(i), n) for f, n in zip(flows, nexts)
        ]

    def moved(i, current, gain, water):
        return current + STEP * add(gain, *[prv(w, i) - w.at(i) for prv, w in zip(PREV, water)])

    water = [Field([], None) for _ in NEXT]
    first = Field([], None)
    for f, value in zip(flows, flux(None)):
        f.side = value
    for w, value in zip(water, water_at(None, frac, [n.side for n in after])):
        w.side = value
    for i in range(nb):
        pressure = x0.blocks[i] + weight0 * u0.blocks[i] + weight1 * u1.blocks[i]
        out_ref[0, i * BLOCK : (i + 1) * BLOCK] = pressure[:, :rows]
        for f, value in zip(flows, flux(i)):
            f.blocks.append(value)
        for w, value in zip(water, water_at(i, frac, [n.blocks[i] for n in after])):
            w.blocks.append(value)
        first.blocks.append(moved(i, s.blocks[i], gain.blocks[i], water))
    first.side = moved(None, s.side, gain.side, water)

    (frac,) = build(lambda i: [fraction(first.at(i))], nb)
    water = [Field([], None) for _ in NEXT]
    for w, value in zip(water, water_at(None, frac, [nxt(frac, None) for nxt in NEXT])):
        w.side = value
    for i in range(nb):
        for w, value in zip(water, water_at(i, frac, [nxt(frac, i) for nxt in NEXT])):
            w.blocks.append(value)
        second = moved(i, first.blocks[i], gained(i, frac.blocks[i]), water)
        out_ref[1, i * BLOCK : (i + 1) * BLOCK] = second[:, :rows]


def local(nx, ny, permeability, saturation, pressure_old, source):
    shape = source.shape
    depth, rows, lanes = shape
    assert permeability.shape[0] == 1 and depth % BLOCK == 0 and depth * 2 * HALO == lanes and rows == 2 * HALO
    wide = rows + 2 * HALO
    f32 = jnp.float32
    dma = pltpu.SemaphoreType.DMA
    outs = pl.pallas_call(
        functools.partial(kernel, nx, ny),
        out_shape=jax.ShapeDtypeStruct((2,) + shape, f32),
        in_specs=[pl.BlockSpec(memory_space=pltpu.HBM)] * 4,
        out_specs=pl.BlockSpec(memory_space=pltpu.VMEM),
        scratch_shapes=[
            pltpu.VMEM((4, depth, wide, lanes), f32),
            pltpu.VMEM((4, rows, lanes), f32),
            pltpu.VMEM((2, 4, wide, lanes), f32),
            pltpu.VMEM((nx * ny, lanes), f32),
            pltpu.VMEM(shape, f32),
            pltpu.VMEM(shape, f32),
            pltpu.VMEM((depth + 1, rows, lanes), f32),
            pltpu.VMEM((depth + 1, rows, lanes), f32),
            dma((4,)),
            dma((8,)),
            dma((8,)),
            dma((6,)),
            dma((6,)),
            dma,
            dma,
            pltpu.SemaphoreType.REGULAR,
            dma((2,)),
            dma((2,)),
            dma((2,)),
            dma((2,)),
        ],
        compiler_params=pltpu.CompilerParams(
            collective_id=0, has_side_effects=True, vmem_limit_bytes=32 * 1024 * 1024
        ),
    )(*[pltpu.with_memory_space_constraint(v, pltpu.HBM) for v in (permeability[0], saturation[0], pressure_old[0], source)])
    return outs[:1], outs[1:]


def solution(mesh):
    wide = P(None, None, "gx", "gy")
    return jax.shard_map(
        functools.partial(local, mesh.shape["gx"], mesh.shape["gy"]),
        mesh=mesh,
        in_specs=(wide, wide, wide, P(None, "gx", "gy")),
        out_specs=(wide, wide),
        check_vma=False,
    )
```

```python
import functools

import jax
import jax.numpy as jnp
from jax import lax
from jax.experimental import pallas as pl
from jax.experimental.pallas import tpu as pltpu
from jax.sharding import PartitionSpec as P

HALO = 4
BLOCK = 4
STORAGE = 0.5
VERTICAL = 0.1
STEP = 0.05
WATER = 1.0
OIL = 2.0
MESH = pl.DeviceIdType.MESH


def iota(shape, dim):
    return lax.broadcasted_iota(jnp.int32, shape, dim)


class Field:
    def __init__(self, blocks, side):
        self.blocks, self.side = blocks, side

    def at(self, i):
        return self.side if i is None else self.blocks[i]


def row_roll(v, shift):
    axis = v.ndim - 2
    return pltpu.roll(v, shift % v.shape[axis], axis)


def lane_roll(v, shift):
    axis = v.ndim - 1
    shift = shift % v.shape[axis]
    return v if shift == 0 else pltpu.roll(v, shift, axis)


def x_next(f, i):
    return row_roll(f.at(i), -1)


def x_prev(f, i):
    return row_roll(f.at(i), 1)


def z_next(f, i):
    width = 2 * HALO
    if i is None:
        lanes = f.side.shape[1]
        return jnp.where(iota(f.side.shape, 1) < lanes - width, lane_roll(f.side, -width), 0.0)
    b = f.blocks[i]
    last = f.blocks[i + 1][:1] if i + 1 < len(f.blocks) else jnp.zeros_like(b[:1])
    return jnp.concatenate([b[1:], last], axis=0)


def z_prev(f, i):
    width = 2 * HALO
    if i is None:
        return jnp.where(iota(f.side.shape, 1) >= width, lane_roll(f.side, width), 0.0)
    b = f.blocks[i]
    first = f.blocks[i - 1][-1:] if i else jnp.zeros_like(b[:1])
    return jnp.concatenate([first, b[:-1]], axis=0)


def inserted(side, i, lane_from, lane_to):
    planes = range(i * BLOCK, (i + 1) * BLOCK)
    return jnp.stack([lane_roll(side, lane_to - (2 * HALO * z + lane_from)) for z in planes], axis=0)


def gathered(blocks, lane_from, lane_to, base):
    width = 2 * HALO
    lane = iota(base.shape, 1)
    for i, b in enumerate(blocks):
        for j in range(BLOCK):
            to = width * (i * BLOCK + j) + lane_to
            base = jnp.where(lane == to, lane_roll(b[j], to - lane_from), base)
    return base


def y_next(f, i):
    if i is None:
        return gathered(f.blocks, 0, 2 * HALO - 1, lane_roll(f.side, -1))
    b = f.blocks[i]
    lanes = b.shape[2]
    return jnp.where(iota(b.shape, 2) == lanes - 1, inserted(f.side, i, 0, lanes - 1), lane_roll(b, -1))


def y_prev(f, i):
    if i is None:
        return gathered(f.blocks, f.blocks[0].shape[2] - 1, 0, lane_roll(f.side, 1))
    b = f.blocks[i]
    return jnp.where(iota(b.shape, 2) == 0, inserted(f.side, i, 2 * HALO - 1, 0), lane_roll(b, 1))


def inverted(v):
    r = pl.reciprocal(v, approx=True)
    r = r * (2.0 - v * r)
    return r * (2.0 - v * r)


def y_both(f):
    width = 2 * HALO
    side = f.side
    lane = iota(side.shape, 1)
    column = lane % width
    edges = jnp.where(column == 0, lane_roll(side, 1 - width), lane_roll(side, -1))
    ends = jnp.zeros_like(side)
    nexts, prevs = [], []
    for i, b in enumerate(f.blocks):
        put = jnp.stack([lane_roll(edges, -width * (i * BLOCK + j)) for j in range(BLOCK)], axis=0)
        at_lane = iota(b.shape, 2)
        up = lane_roll(b, 1)
        nexts.append(jnp.where(at_lane == b.shape[2] - 1, put, lane_roll(b, -1)))
        prevs.append(jnp.where(at_lane == 0, put, up))
        for j in range(BLOCK):
            z = i * BLOCK + j
            ends = jnp.where(lane // width == z, lane_roll(up[j], width * z), ends)
    side_next = jnp.where(column == width - 1, lane_roll(ends, width - 2), lane_roll(side, -1))
    side_prev = jnp.where(column == 0, ends, lane_roll(side, 1))
    return Field(nexts, side_next), Field(prevs, side_prev)


def mobility(s):
    return s * s / WATER + (1.0 - s) * (1.0 - s) / OIL


def fraction(s):
    water = s * s / WATER
    return water * inverted(water + (1.0 - s) * (1.0 - s) / OIL)


def coefficient(scaling):
    def fn(ka, kb, ma, mb):
        return (scaling * ka * kb) * inverted(jnp.maximum(ka + kb, 1e-20)) * (ma + mb)

    return fn


NEXT = (z_next, x_next, y_next)
PREV = (z_prev, x_prev, y_prev)


def build(fn, count):
    side = fn(None)
    blocks = [fn(i) for i in range(count)]
    return [Field([b[n] for b in blocks], side[n]) for n in range(len(side))]


def add(*terms):
    total = terms[0]
    for t in terms[1:]:
        total = total + t
    return total


def packed(own):
    depth, rows, lanes = own.shape
    width = 2 * HALO
    edge = jnp.where(iota(own.shape, 2) < HALO, own, lane_roll(own, width))
    block = iota((rows, lanes), 1) // width
    out = edge[0]
    for z in range(1, depth):
        out = jnp.where(block == z, lane_roll(edge[z], width * z), out)
    return out


def kernel(nx, ny, k_in, s_in, x_in, q_in, out_ref, main_ref, pack_ref, side_ref, slots,
           late_send, late_recv, early_send, early_recv, load_sem, xsend, xrecv, psend, precv, rsend, rrecv, ready, lsem, lrecv, esem, erecv):
    gx, gy = lax.axis_index("gx"), lax.axis_index("gy")
    ins = (k_in, s_in, x_in, q_in)
    rows = k_in.shape[1]
    wide = rows + 2 * HALO

    def has(dx, dy):
        ok = None
        for d, at, n in ((dx, gx, nx), (dy, gy, ny)):
            if d:
                one = at + d >= 0 if d < 0 else at + d < n
                ok = one if ok is None else ok & one
        return ok

    def at(dx, dy):
        return {"gx": gx + dx, "gy": gy + dy}

    diagonals = [(dx, dy) for dx in (-1, 1) for dy in (-1, 1)]

    loads = [pltpu.make_async_copy(ref, main_ref.at[i, :, pl.ds(0, rows)], load_sem.at[i]) for i, ref in enumerate(ins)]
    for copy in loads:
        copy.start()

    barrier = pltpu.get_barrier_semaphore()
    expected = jnp.int32(nx - 1 + ny - 1)
    for off in range(1, nx):
        pl.semaphore_signal(barrier, inc=1, device_id={"gx": lax.rem(gx + off, nx), "gy": gy}, device_id_type=MESH)
    for off in range(1, ny):
        pl.semaphore_signal(barrier, inc=1, device_id={"gx": gx, "gy": lax.rem(gy + off, ny)}, device_id_type=MESH)
    for dx, dy in diagonals:
        @pl.when(has(dx, dy))
        def _():
            pl.semaphore_signal(barrier, inc=1, device_id=at(dx, dy), device_id_type=MESH)

        expected = expected + has(dx, dy).astype(jnp.int32)

    reach = (2, 2, 2, 1)

    def edge_rows(dx, width):
        return pl.ds(0, width) if dx < 0 else pl.ds(rows - width, width)

    def halo_rows(dx, width):
        return pl.ds(rows, width) if dx < 0 else pl.ds(wide - width, width)

    def x_copies(dx, halves=(0, 1)):
        d = (dx + 1) // 2
        return [
            pltpu.make_async_remote_copy(
                src_ref=main_ref.at[i, :, edge_rows(dx, reach[i])],
                dst_ref=main_ref.at[i, :, halo_rows(dx, reach[i])],
                send_sem=xsend.at[d * len(ins) + i],
                recv_sem=xrecv.at[d * len(ins) + i],
                device_id=at(dx, 0),
                device_id_type=MESH,
            )
            for i in range(len(ins))
            if i // 2 in halves
        ]

    def y_copy(dx, dy):
        number = (dx + 1) * 2 + (dy + 1) // 2
        from_rows = to_rows = pl.ds(0, rows)
        if dx:
            from_rows, to_rows = edge_rows(dx, reach[0]), halo_rows(dx, reach[0])
        return pltpu.make_async_remote_copy(
            src_ref=pack_ref.at[:, from_rows],
            dst_ref=side_ref.at[(1 - dy) // 2, :, to_rows],
            send_sem=psend.at[number],
            recv_sem=precv.at[number],
            device_id=at(dx, dy),
            device_id_type=MESH,
        )

    def line_copy(dx, src, dst, send, recv):
        line = pl.ds(1, 1) if dx < 0 else pl.ds(rows - 2, 1)
        d = (dx + 1) // 2
        return pltpu.make_async_remote_copy(
            src_ref=src.at[:, line],
            dst_ref=dst.at[:, line],
            send_sem=send.at[d],
            recv_sem=recv.at[d],
            device_id=at(dx, 0),
            device_id_type=MESH,
        )

    def early_copy(dx):
        return line_copy(dx, early_send, early_recv, esem, erecv)

    def late_copy(dx):
        return line_copy(dx, late_send, late_recv, lsem, lrecv)

    y_moves = [(0, 1), (0, -1)] + diagonals

    for i in range(len(ins)):
        loads[i].wait()
        pack_ref[i] = packed(main_ref[i, :, 0:rows, :])

    pl.semaphore_wait(barrier, expected)
    for half, moves in enumerate((y_moves[:2], y_moves[2:])):
        for dx, dy in moves:
            @pl.when(has(dx, dy))
            def _():
                y_copy(dx, dy).start()

        for dx in (-1, 1):
            @pl.when(has(dx, 0))
            def _():
                for copy in x_copies(dx, (half,)):
                    copy.start()

    for off in range(1, nx):
        pl.semaphore_signal(ready, inc=1, device_id={"gx": lax.rem(gx + off, nx), "gy": gy}, device_id_type=MESH)

    def arrive_y(moves):
        for dx, dy in moves:
            @pl.when(has(-dx, -dy))
            def _():
                y_copy(dx, dy).wait_recv()

    def arrive_x(half):
        for dx in (-1, 1):
            @pl.when(has(-dx, 0))
            def _():
                for copy in x_copies(dx, (half,)):
                    copy.wait_recv()

    lanes = k_in.shape[2]
    depth = k_in.shape[0]
    row = iota((wide, lanes), 0)
    lane = iota((wide, lanes), 1)
    right = lane % (2 * HALO) < HALO

    nb = depth // BLOCK

    def inside(i, high):
        at_row = row[:high]
        return (
            (at_row < rows)
            | ((at_row < rows + reach[i]) & (gx + 1 < nx))
            | ((at_row >= wide - reach[i]) & (gx > 0))
        )

    def side_field(i, high):
        here, at_right = inside(i, high), right[:high]
        inside_right = at_right & here & (gy + 1 < ny)
        inside_left = jnp.logical_not(at_right) & here & (gy > 0)
        return jnp.where(
            inside_right, side_ref[1, i, 0:high], jnp.where(inside_left, side_ref[0, i, 0:high], 0.0)
        )

    def field(i):
        here = inside(i, wide)[None]
        blocks = [jnp.where(here, main_ref[i, n * BLOCK : (n + 1) * BLOCK], 0.0) for n in range(nb)]
        return Field(blocks, side_field(i, wide))

    def own(f):
        return jnp.concatenate([b[:, :rows] for b in f.blocks], axis=0)

    def zy_faces(k, s):
        (mob,) = build(lambda i: [mobility(s.at(i))], nb)
        coefs = [Field([], None) for _ in range(2)]
        before = [Field([], None) for _ in range(2)]

        def face(i):
            return [
                coefficient(sc)(k.at(i), nxt(k, i), mob.at(i), nxt(mob, i))
                for nxt, sc in ((z_next, VERTICAL), (y_next, 1.0))
            ]

        def behind(i):
            return [prv(c, i) for prv, c in zip((z_prev, y_prev), coefs)]

        for c, value in zip(coefs, face(None)):
            c.side = value
        for i in range(nb):
            for c, value in zip(coefs, face(i)):
                c.blocks.append(value)
            for c, value in zip(before, behind(i)):
                c.blocks.append(value)
        for c, value in zip(before, behind(None)):
            c.side = value
        return mob, coefs, before

    def x_faces(k, mob):
        (c,) = build(
            lambda i: [coefficient(1.0)(k.at(i), x_next(k, i), mob.at(i), x_next(mob, i))], nb
        )
        (b,) = build(lambda i: [x_prev(c, i)], nb)
        return c, b

    def zy_diag(coefs, before):
        return build(lambda i: [add(STORAGE, *[f.at(i) for f in coefs + before])], nb)[0]

    def zy_around(v, coefs, before):
        ahead, back = y_both(v)
        return build(
            lambda i: [
                coefs[0].at(i) * z_next(v, i)
                + before[0].at(i) * z_prev(v, i)
                + coefs[1].at(i) * ahead.at(i)
                + before[1].at(i) * back.at(i)
            ],
            nb,
        )[0]

    def x_around(v, c, b, i):
        return c.at(i) * x_next(v, i) + b.at(i) * x_prev(v, i)

    def whole_diag(partial, c, b):
        return build(lambda i: (lambda d: [d, inverted(d)])(partial.at(i) + c.at(i) + b.at(i)), nb)

    def start_field(x0, q, partial, c, b, diag, inverse):
        return build(
            lambda i: [
                (q.at(i) + STORAGE * x0.at(i) - (diag.at(i) * x0.at(i) - (partial.at(i) + x_around(x0, c, b, i))))
                * inverse.at(i)
            ],
            nb,
        )[0]

    def lower(f):
        return Field([b[:, rows:] for b in f.blocks], f.side[rows:])

    def join(f, g):
        return Field(
            [jnp.concatenate([a, b], axis=1) for a, b in zip(f.blocks, g.blocks)],
            jnp.concatenate([f.side, g.side], axis=0),
        )

    each = range(nb)
    k, s, x0, q = (Field([main_ref[i, n * BLOCK : (n + 1) * BLOCK, 0:rows] for n in each], None) for i in range(4))
    own_mob = Field([mobility(b) for b in s.blocks], None)

    def face_at(nxt, scaling, i):
        return coefficient(scaling)(k.at(i), nxt(k, i), own_mob.at(i), nxt(own_mob, i))

    z_coef = Field([face_at(z_next, VERTICAL, i) for i in each], None)
    z_before = Field([z_prev(z_coef, i) for i in each], None)
    x_coef = Field([face_at(x_next, 1.0, i) for i in each], None)
    x_before = Field([x_prev(x_coef, i) for i in each], None)

    def z_around(i):
        return z_coef.at(i) * z_next(x0, i) + z_before.at(i) * z_prev(x0, i)

    def z_diag(i):
        return STORAGE + z_coef.at(i) + z_before.at(i)

    z_part = Field([z_around(i) for i in each], None)
    x_part = Field([x_around(x0, x_coef, x_before, i) for i in each], None)
    own_diag = Field([z_diag(i) for i in each], None)

    arrive_y(y_moves[:2])
    for i, f in enumerate((k, s, x0, q)):
        f.side = side_field(i, rows)
    own_mob.side = mobility(s.side)
    z_coef.side = face_at(z_next, VERTICAL, None)
    z_before.side = z_prev(z_coef, None)
    x_coef.side = face_at(x_next, 1.0, None)
    x_before.side = x_prev(x_coef, None)
    z_part.side = z_around(None)
    x_part.side = x_around(x0, x_coef, x_before, None)
    own_diag.side = z_diag(None)
    (y_coef,) = build(lambda i: [face_at(y_next, 1.0, i)], nb)
    (y_before,) = build(lambda i: [y_prev(y_coef, i)], nb)
    (own_diag,) = build(lambda i: [own_diag.at(i) + y_coef.at(i) + y_before.at(i)], nb)
    diag, inverse = whole_diag(own_diag, x_coef, x_before)
    ahead, back = y_both(x0)
    (own_around,) = build(
        lambda i: [z_part.at(i) + y_coef.at(i) * ahead.at(i) + y_before.at(i) * back.at(i)], nb
    )
    own_coefs, own_before = (z_coef, y_coef), (z_before, y_before)
    (u0,) = build(
        lambda i: [
            (q.at(i) + STORAGE * x0.at(i) - (diag.at(i) * x0.at(i) - (own_around.at(i) + x_part.at(i))))
            * inverse.at(i)
        ],
        nb,
    )
    for i, b in enumerate(u0.blocks):
        early_send[i * BLOCK : (i + 1) * BLOCK] = b
    early_send[depth] = u0.side
    for dx in (-1, 1):
        @pl.when(has(dx, 0))
        def _():
            early_copy(dx).start()

    line_row = iota((rows, lanes), 0)
    taken = ((line_row == 1) & (gx + 1 < nx)) | ((line_row == rows - 2) & (gx > 0))

    def patched(value, ref, planes):
        cut = value[..., :rows, :], value[..., rows:, :]
        return jnp.concatenate([cut[0], jnp.where(taken, ref[planes], cut[1])], axis=-2)

    def patch(f, ref):
        f.blocks = [patched(b, ref, slice(i * BLOCK, (i + 1) * BLOCK)) for i, b in enumerate(f.blocks)]

    arrive_y(y_moves[2:])
    arrive_x(0)
    k, s = field(0), field(1)
    halo_mob, halo_coefs, halo_before = zy_faces(lower(k), lower(s))
    halo_diag = zy_diag(halo_coefs, halo_before)
    x_coef, x_before = x_faces(k, join(own_mob, halo_mob))
    diag, inverse = whole_diag(join(own_diag, halo_diag), x_coef, x_before)
    z_coef, y_coef = [join(f, g) for f, g in zip(own_coefs, halo_coefs)]
    z_before, y_before = [join(f, g) for f, g in zip(own_before, halo_before)]
    coefs = (z_coef, x_coef, y_coef)
    arrive_x(1)
    x0, q = field(2), field(3)
    partial = join(own_around, zy_around(lower(x0), halo_coefs, halo_before))
    u0 = start_field(x0, q, partial, x_coef, x_before, diag, inverse)
    for dx in (-1, 1):
        @pl.when(has(-dx, 0))
        def _():
            early_copy(dx).wait_recv()

    patch(u0, early_recv)
    u0.side = patched(u0.side, early_recv, depth)
    def around(v):
        partial = zy_around(v, (z_coef, y_coef), (z_before, y_before))
        return lambda i: partial.at(i) + x_around(v, x_coef, x_before, i)

    near = around(u0)
    (u1,) = build(lambda i: [u0.at(i) - near(i) * inverse.at(i)], nb)
    near = around(u1)
    sums = [0.0] * 4
    for i in range(nb):
        d, a, b = [f.blocks[i][:, :rows] for f in (diag, u0, u1)]
        da, db = d * a, d * b
        image = db - near(i)[:, :rows]
        for n, value in enumerate((da * a, da * b, db * b, b * image)):
            sums[n] = sums[n] + jnp.sum(value, axis=0)

    tile_row = iota((rows, lanes), 0)
    part = jnp.zeros((rows, lanes), jnp.float32)
    for i, value in enumerate(sums):
        part = jnp.where(tile_row == i, jnp.sum(value, axis=0, keepdims=True), part)

    late_send[...] = own(u1)

    count = nx * ny
    group = lanes // 4
    folded = part + lane_roll(part, lanes // 2)
    folded = folded + lane_roll(folded, lanes // 4)
    mine = iota((rows, lanes), 1) // group == iota((rows, lanes), 0)
    slots[0:1, :] = jnp.sum(jnp.where(mine, folded, 0.0), axis=0, keepdims=True)
    me = gx * ny + gy

    def share_copy(off, first, size):
        target = lax.rem(me + off, count)
        return pltpu.make_async_remote_copy(
            src_ref=slots.at[pl.ds(0 if size == 1 else first, size)],
            dst_ref=slots.at[pl.ds(first, size)],
            send_sem=rsend,
            recv_sem=rrecv,
            device_id={"gx": target // ny, "gy": target % ny},
            device_id_type=MESH,
        )

    pl.semaphore_wait(ready, nx - 1)
    for off in range(1, count):
        share_copy(off, off, 1).start()

    def gained(i, frac):
        return jnp.maximum(q.at(i), 0.0) + jnp.minimum(q.at(i), 0.0) * frac

    for dx in (-1, 1):
        @pl.when(has(dx, 0))
        def _():
            late_copy(dx).start()

    (frac,) = build(lambda i: [fraction(s.at(i))], nb)
    (gain,) = build(lambda i: [gained(i, frac.at(i))], nb)
    after = build(lambda i: [nxt(frac, i) for nxt in NEXT], nb)
    for dx in (-1, 1):
        @pl.when(has(-dx, 0))
        def _():
            late_copy(dx).wait_recv()

    patch(u1, late_recv)
    bases = [
        build(lambda i: [c.at(i) * (v.at(i) - nxt(v, i)) for nxt, c in zip(NEXT, coefs)], nb) for v in (x0, u0, u1)
    ]
    for dx in (-1, 1):
        @pl.when(has(dx, 0))
        def _():
            for copy in x_copies(dx):
                copy.wait_send()
            early_copy(dx).wait_send()
            late_copy(dx).wait_send()

    for dx, dy in y_moves:
        @pl.when(has(dx, dy))
        def _():
            y_copy(dx, dy).wait_send()

    share_copy(1, 1, count - 1).wait_send()
    share_copy(1, 1, count - 1).wait_recv()
    total = jnp.sum(slots[...], axis=0, keepdims=True)
    sums = jnp.sum(jnp.where(mine, total, 0.0), axis=1, keepdims=True)
    sa, sb, sc, sd = (sums[i : i + 1, :] for i in range(4))
    step0 = sa / sb
    next_energy = step0 * step0 * sc - sa
    conjugacy = next_energy / sa
    curvature = sb - 2.0 * step0 * sc + step0 * step0 * sd
    step1 = next_energy / (curvature - conjugacy * next_energy / step0)
    weight0 = step0 + step1 * (1.0 + conjugacy)
    weight1 = -step1 * step0

    flows = [Field([], None) for _ in NEXT]

    def flux(i):
        return [x.at(i) + weight0 * a.at(i) + weight1 * b.at(i) for x, a, b in zip(*bases)]

    def water_at(i, frac, nexts):
        return [
            f.at(i) * jnp.where(f.at(i) > 0.0, frac.at(i), n) for f, n in zip(flows, nexts)
        ]

    def moved(i, current, gain, water):
        return current + STEP * add(gain, *[prv(w, i) - w.at(i) for prv, w in zip(PREV, water)])

    water = [Field([], None) for _ in NEXT]
    first = Field([], None)
    for f, value in zip(flows, flux(None)):
        f.side = value
    for w, value in zip(water, water_at(None, frac, [n.side for n in after])):
        w.side = value
    for i in range(nb):
        pressure = x0.blocks[i] + weight0 * u0.blocks[i] + weight1 * u1.blocks[i]
        out_ref[0, i * BLOCK : (i + 1) * BLOCK] = pressure[:, :rows]
        for f, value in zip(flows, flux(i)):
            f.blocks.append(value)
        for w, value in zip(water, water_at(i, frac, [n.blocks[i] for n in after])):
            w.blocks.append(value)
        first.blocks.append(moved(i, s.blocks[i], gain.blocks[i], water))
    first.side = moved(None, s.side, gain.side, water)

    (frac,) = build(lambda i: [fraction(first.at(i))], nb)
    water = [Field([], None) for _ in NEXT]
    for w, value in zip(water, water_at(None, frac, [nxt(frac, None) for nxt in NEXT])):
        w.side = value
    for i in range(nb):
        for w, value in zip(water, water_at(i, frac, [nxt(frac, i) for nxt in NEXT])):
            w.blocks.append(value)
        second = moved(i, first.blocks[i], gained(i, frac.blocks[i]), water)
        out_ref[1, i * BLOCK : (i + 1) * BLOCK] = second[:, :rows]


def local(nx, ny, permeability, saturation, pressure_old, source):
    shape = source.shape
    depth, rows, lanes = shape
    assert permeability.shape[0] == 1 and depth % BLOCK == 0 and depth * 2 * HALO == lanes and rows == 2 * HALO
    wide = rows + 2 * HALO
    f32 = jnp.float32
    dma = pltpu.SemaphoreType.DMA
    outs = pl.pallas_call(
        functools.partial(kernel, nx, ny),
        out_shape=jax.ShapeDtypeStruct((2,) + shape, f32),
        in_specs=[pl.BlockSpec(memory_space=pltpu.HBM)] * 4,
        out_specs=pl.BlockSpec(memory_space=pltpu.VMEM),
        scratch_shapes=[
            pltpu.VMEM((4, depth, wide, lanes), f32),
            pltpu.VMEM((4, rows, lanes), f32),
            pltpu.VMEM((2, 4, wide, lanes), f32),
            pltpu.VMEM((nx * ny, lanes), f32),
            pltpu.VMEM(shape, f32),
            pltpu.VMEM(shape, f32),
            pltpu.VMEM((depth + 1, rows, lanes), f32),
            pltpu.VMEM((depth + 1, rows, lanes), f32),
            dma((4,)),
            dma((8,)),
            dma((8,)),
            dma((6,)),
            dma((6,)),
            dma,
            dma,
            pltpu.SemaphoreType.REGULAR,
            dma((2,)),
            dma((2,)),
            dma((2,)),
            dma((2,)),
        ],
        compiler_params=pltpu.CompilerParams(
            collective_id=0, has_side_effects=True, vmem_limit_bytes=32 * 1024 * 1024
        ),
    )(*[pltpu.with_memory_space_constraint(v, pltpu.HBM) for v in (permeability[0], saturation[0], pressure_old[0], source)])
    return outs[:1], outs[1:]


def solution(mesh):
    wide = P(None, None, "gx", "gy")
    return jax.shard_map(
        functools.partial(local, mesh.shape["gx"], mesh.shape["gy"]),
        mesh=mesh,
        in_specs=(wide, wide, wide, P(None, "gx", "gy")),
        out_specs=(wide, wide),
        check_vma=False,
    )
```

```python
import functools

import jax
import jax.numpy as jnp
from jax import lax
from jax.experimental import pallas as pl
from jax.experimental.pallas import tpu as pltpu
from jax.sharding import PartitionSpec as P

HALO = 4
BLOCK = 2
STORAGE = 0.5
VERTICAL = 0.1
STEP = 0.05
WATER = 1.0
OIL = 2.0
MESH = pl.DeviceIdType.MESH


def iota(shape, dim):
    return lax.broadcasted_iota(jnp.int32, shape, dim)


class Field:
    def __init__(self, blocks, side):
        self.blocks, self.side = blocks, side

    def at(self, i):
        return self.side if i is None else self.blocks[i]


def row_roll(v, shift):
    axis = v.ndim - 2
    return pltpu.roll(v, shift % v.shape[axis], axis)


def lane_roll(v, shift):
    axis = v.ndim - 1
    shift = shift % v.shape[axis]
    return v if shift == 0 else pltpu.roll(v, shift, axis)


def x_next(f, i):
    return row_roll(f.at(i), -1)


def x_prev(f, i):
    return row_roll(f.at(i), 1)


def z_next(f, i):
    width = 2 * HALO
    if i is None:
        lanes = f.side.shape[1]
        return jnp.where(iota(f.side.shape, 1) < lanes - width, lane_roll(f.side, -width), 0.0)
    b = f.blocks[i]
    last = f.blocks[i + 1][:1] if i + 1 < len(f.blocks) else jnp.zeros_like(b[:1])
    return jnp.concatenate([b[1:], last], axis=0)


def z_prev(f, i):
    width = 2 * HALO
    if i is None:
        return jnp.where(iota(f.side.shape, 1) >= width, lane_roll(f.side, width), 0.0)
    b = f.blocks[i]
    first = f.blocks[i - 1][-1:] if i else jnp.zeros_like(b[:1])
    return jnp.concatenate([first, b[:-1]], axis=0)


def inserted(side, i, lane_from, lane_to):
    planes = range(i * BLOCK, (i + 1) * BLOCK)
    return jnp.stack([lane_roll(side, lane_to - (2 * HALO * z + lane_from)) for z in planes], axis=0)


def gathered(blocks, lane_from, lane_to, base):
    width = 2 * HALO
    lane = iota(base.shape, 1)
    for i, b in enumerate(blocks):
        for j in range(BLOCK):
            to = width * (i * BLOCK + j) + lane_to
            base = jnp.where(lane == to, lane_roll(b[j], to - lane_from), base)
    return base


def y_next(f, i):
    if i is None:
        return gathered(f.blocks, 0, 2 * HALO - 1, lane_roll(f.side, -1))
    b = f.blocks[i]
    lanes = b.shape[2]
    return jnp.where(iota(b.shape, 2) == lanes - 1, inserted(f.side, i, 0, lanes - 1), lane_roll(b, -1))


def y_prev(f, i):
    if i is None:
        return gathered(f.blocks, f.blocks[0].shape[2] - 1, 0, lane_roll(f.side, 1))
    b = f.blocks[i]
    return jnp.where(iota(b.shape, 2) == 0, inserted(f.side, i, 2 * HALO - 1, 0), lane_roll(b, 1))


def inverted(v):
    r = pl.reciprocal(v, approx=True)
    r = r * (2.0 - v * r)
    return r * (2.0 - v * r)


def y_both(f):
    width = 2 * HALO
    side = f.side
    lane = iota(side.shape, 1)
    column = lane % width
    edges = jnp.where(column == 0, lane_roll(side, 1 - width), lane_roll(side, -1))
    ends = jnp.zeros_like(side)
    nexts, prevs = [], []
    for i, b in enumerate(f.blocks):
        put = jnp.stack([lane_roll(edges, -width * (i * BLOCK + j)) for j in range(BLOCK)], axis=0)
        at_lane = iota(b.shape, 2)
        up = lane_roll(b, 1)
        nexts.append(jnp.where(at_lane == b.shape[2] - 1, put, lane_roll(b, -1)))
        prevs.append(jnp.where(at_lane == 0, put, up))
        for j in range(BLOCK):
            z = i * BLOCK + j
            ends = jnp.where(lane // width == z, lane_roll(up[j], width * z), ends)
    side_next = jnp.where(column == width - 1, lane_roll(ends, width - 2), lane_roll(side, -1))
    side_prev = jnp.where(column == 0, ends, lane_roll(side, 1))
    return Field(nexts, side_next), Field(prevs, side_prev)


def mobility(s):
    return s * s / WATER + (1.0 - s) * (1.0 - s) / OIL


def fraction(s):
    water = s * s / WATER
    return water * inverted(water + (1.0 - s) * (1.0 - s) / OIL)


def coefficient(scaling):
    def fn(ka, kb, ma, mb):
        return (scaling * ka * kb) * inverted(jnp.maximum(ka + kb, 1e-20)) * (ma + mb)

    return fn


NEXT = (z_next, x_next, y_next)
PREV = (z_prev, x_prev, y_prev)


def build(fn, count):
    side = fn(None)
    blocks = [fn(i) for i in range(count)]
    return [Field([b[n] for b in blocks], side[n]) for n in range(len(side))]


def add(*terms):
    total = terms[0]
    for t in terms[1:]:
        total = total + t
    return total


def packed(own):
    depth, rows, lanes = own.shape
    width = 2 * HALO
    edge = jnp.where(iota(own.shape, 2) < HALO, own, lane_roll(own, width))
    block = iota((rows, lanes), 1) // width
    out = edge[0]
    for z in range(1, depth):
        out = jnp.where(block == z, lane_roll(edge[z], width * z), out)
    return out


def kernel(nx, ny, k_in, s_in, x_in, q_in, out_ref, main_ref, pack_ref, side_ref, slots,
           late_send, late_recv, early_send, early_recv, load_sem, xsend, xrecv, psend, precv, rsend, rrecv, ready, lsem, lrecv, esem, erecv):
    gx, gy = lax.axis_index("gx"), lax.axis_index("gy")
    ins = (k_in, s_in, x_in, q_in)
    rows = k_in.shape[1]
    wide = rows + 2 * HALO

    def has(dx, dy):
        ok = None
        for d, at, n in ((dx, gx, nx), (dy, gy, ny)):
            if d:
                one = at + d >= 0 if d < 0 else at + d < n
                ok = one if ok is None else ok & one
        return ok

    def at(dx, dy):
        return {"gx": gx + dx, "gy": gy + dy}

    diagonals = [(dx, dy) for dx in (-1, 1) for dy in (-1, 1)]

    loads = [pltpu.make_async_copy(ref, main_ref.at[i, :, pl.ds(0, rows)], load_sem.at[i]) for i, ref in enumerate(ins)]
    for copy in loads:
        copy.start()

    barrier = pltpu.get_barrier_semaphore()
    expected = jnp.int32(nx - 1 + ny - 1)
    for off in range(1, nx):
        pl.semaphore_signal(barrier, inc=1, device_id={"gx": lax.rem(gx + off, nx), "gy": gy}, device_id_type=MESH)
    for off in range(1, ny):
        pl.semaphore_signal(barrier, inc=1, device_id={"gx": gx, "gy": lax.rem(gy + off, ny)}, device_id_type=MESH)
    for dx, dy in diagonals:
        @pl.when(has(dx, dy))
        def _():
            pl.semaphore_signal(barrier, inc=1, device_id=at(dx, dy), device_id_type=MESH)

        expected = expected + has(dx, dy).astype(jnp.int32)

    reach = (2, 2, 2, 1)

    def edge_rows(dx, width):
        return pl.ds(0, width) if dx < 0 else pl.ds(rows - width, width)

    def halo_rows(dx, width):
        return pl.ds(rows, width) if dx < 0 else pl.ds(wide - width, width)

    def x_copies(dx, halves=(0, 1)):
        d = (dx + 1) // 2
        return [
            pltpu.make_async_remote_copy(
                src_ref=main_ref.at[i, :, edge_rows(dx, reach[i])],
                dst_ref=main_ref.at[i, :, halo_rows(dx, reach[i])],
                send_sem=xsend.at[d * len(ins) + i],
                recv_sem=xrecv.at[d * len(ins) + i],
                device_id=at(dx, 0),
                device_id_type=MESH,
            )
            for i in range(len(ins))
            if i // 2 in halves
        ]

    def y_copy(dx, dy):
        number = (dx + 1) * 2 + (dy + 1) // 2
        from_rows = to_rows = pl.ds(0, rows)
        if dx:
            from_rows, to_rows = edge_rows(dx, reach[0]), halo_rows(dx, reach[0])
        return pltpu.make_async_remote_copy(
            src_ref=pack_ref.at[:, from_rows],
            dst_ref=side_ref.at[(1 - dy) // 2, :, to_rows],
            send_sem=psend.at[number],
            recv_sem=precv.at[number],
            device_id=at(dx, dy),
            device_id_type=MESH,
        )

    def line_copy(dx, src, dst, send, recv):
        line = pl.ds(1, 1) if dx < 0 else pl.ds(rows - 2, 1)
        d = (dx + 1) // 2
        return pltpu.make_async_remote_copy(
            src_ref=src.at[:, line],
            dst_ref=dst.at[:, line],
            send_sem=send.at[d],
            recv_sem=recv.at[d],
            device_id=at(dx, 0),
            device_id_type=MESH,
        )

    def early_copy(dx):
        return line_copy(dx, early_send, early_recv, esem, erecv)

    def late_copy(dx):
        return line_copy(dx, late_send, late_recv, lsem, lrecv)

    y_moves = [(0, 1), (0, -1)] + diagonals

    for i in range(len(ins)):
        loads[i].wait()
        pack_ref[i] = packed(main_ref[i, :, 0:rows, :])

    pl.semaphore_wait(barrier, expected)
    for half, moves in enumerate((y_moves[:2], y_moves[2:])):
        for dx, dy in moves:
            @pl.when(has(dx, dy))
            def _():
                y_copy(dx, dy).start()

        for dx in (-1, 1):
            @pl.when(has(dx, 0))
            def _():
                for copy in x_copies(dx, (half,)):
                    copy.start()

    for off in range(1, nx):
        pl.semaphore_signal(ready, inc=1, device_id={"gx": lax.rem(gx + off, nx), "gy": gy}, device_id_type=MESH)

    def arrive_y(moves):
        for dx, dy in moves:
            @pl.when(has(-dx, -dy))
            def _():
                y_copy(dx, dy).wait_recv()

    def arrive_x(half):
        for dx in (-1, 1):
            @pl.when(has(-dx, 0))
            def _():
                for copy in x_copies(dx, (half,)):
                    copy.wait_recv()

    lanes = k_in.shape[2]
    depth = k_in.shape[0]
    row = iota((wide, lanes), 0)
    lane = iota((wide, lanes), 1)
    right = lane % (2 * HALO) < HALO

    nb = depth // BLOCK

    def inside(i, high):
        at_row = row[:high]
        return (
            (at_row < rows)
            | ((at_row < rows + reach[i]) & (gx + 1 < nx))
            | ((at_row >= wide - reach[i]) & (gx > 0))
        )

    def side_field(i, high):
        here, at_right = inside(i, high), right[:high]
        inside_right = at_right & here & (gy + 1 < ny)
        inside_left = jnp.logical_not(at_right) & here & (gy > 0)
        return jnp.where(
            inside_right, side_ref[1, i, 0:high], jnp.where(inside_left, side_ref[0, i, 0:high], 0.0)
        )

    def field(i):
        here = inside(i, wide)[None]
        blocks = [jnp.where(here, main_ref[i, n * BLOCK : (n + 1) * BLOCK], 0.0) for n in range(nb)]
        return Field(blocks, side_field(i, wide))

    def own(f):
        return jnp.concatenate([b[:, :rows] for b in f.blocks], axis=0)

    def zy_faces(k, s):
        (mob,) = build(lambda i: [mobility(s.at(i))], nb)
        coefs = [Field([], None) for _ in range(2)]
        before = [Field([], None) for _ in range(2)]

        def face(i):
            return [
                coefficient(sc)(k.at(i), nxt(k, i), mob.at(i), nxt(mob, i))
                for nxt, sc in ((z_next, VERTICAL), (y_next, 1.0))
            ]

        def behind(i):
            return [prv(c, i) for prv, c in zip((z_prev, y_prev), coefs)]

        for c, value in zip(coefs, face(None)):
            c.side = value
        for i in range(nb):
            for c, value in zip(coefs, face(i)):
                c.blocks.append(value)
            for c, value in zip(before, behind(i)):
                c.blocks.append(value)
        for c, value in zip(before, behind(None)):
            c.side = value
        return mob, coefs, before

    def x_faces(k, mob):
        (c,) = build(
            lambda i: [coefficient(1.0)(k.at(i), x_next(k, i), mob.at(i), x_next(mob, i))], nb
        )
        (b,) = build(lambda i: [x_prev(c, i)], nb)
        return c, b

    def zy_diag(coefs, before):
        return build(lambda i: [add(STORAGE, *[f.at(i) for f in coefs + before])], nb)[0]

    def zy_around(v, coefs, before):
        ahead, back = y_both(v)
        return build(
            lambda i: [
                coefs[0].at(i) * z_next(v, i)
                + before[0].at(i) * z_prev(v, i)
                + coefs[1].at(i) * ahead.at(i)
                + before[1].at(i) * back.at(i)
            ],
            nb,
        )[0]

    def x_around(v, c, b, i):
        return c.at(i) * x_next(v, i) + b.at(i) * x_prev(v, i)

    def whole_diag(partial, c, b):
        return build(lambda i: (lambda d: [d, inverted(d)])(partial.at(i) + c.at(i) + b.at(i)), nb)

    def start_field(x0, q, partial, c, b, diag, inverse):
        return build(
            lambda i: [
                (q.at(i) + STORAGE * x0.at(i) - (diag.at(i) * x0.at(i) - (partial.at(i) + x_around(x0, c, b, i))))
                * inverse.at(i)
            ],
            nb,
        )[0]

    def lower(f):
        return Field([b[:, rows:] for b in f.blocks], f.side[rows:])

    def join(f, g):
        return Field(
            [jnp.concatenate([a, b], axis=1) for a, b in zip(f.blocks, g.blocks)],
            jnp.concatenate([f.side, g.side], axis=0),
        )

    each = range(nb)
    k, s, x0, q = (Field([main_ref[i, n * BLOCK : (n + 1) * BLOCK, 0:rows] for n in each], None) for i in range(4))
    own_mob = Field([mobility(b) for b in s.blocks], None)

    def face_at(nxt, scaling, i):
        return coefficient(scaling)(k.at(i), nxt(k, i), own_mob.at(i), nxt(own_mob, i))

    z_coef = Field([face_at(z_next, VERTICAL, i) for i in each], None)
    z_before = Field([z_prev(z_coef, i) for i in each], None)
    x_coef = Field([face_at(x_next, 1.0, i) for i in each], None)
    x_before = Field([x_prev(x_coef, i) for i in each], None)

    def z_around(i):
        return z_coef.at(i) * z_next(x0, i) + z_before.at(i) * z_prev(x0, i)

    def z_diag(i):
        return STORAGE + z_coef.at(i) + z_before.at(i)

    z_part = Field([z_around(i) for i in each], None)
    x_part = Field([x_around(x0, x_coef, x_before, i) for i in each], None)
    own_diag = Field([z_diag(i) for i in each], None)

    arrive_y(y_moves[:2])
    for i, f in enumerate((k, s, x0, q)):
        f.side = side_field(i, rows)
    own_mob.side = mobility(s.side)
    z_coef.side = face_at(z_next, VERTICAL, None)
    z_before.side = z_prev(z_coef, None)
    x_coef.side = face_at(x_next, 1.0, None)
    x_before.side = x_prev(x_coef, None)
    z_part.side = z_around(None)
    x_part.side = x_around(x0, x_coef, x_before, None)
    own_diag.side = z_diag(None)
    (y_coef,) = build(lambda i: [face_at(y_next, 1.0, i)], nb)
    (y_before,) = build(lambda i: [y_prev(y_coef, i)], nb)
    (own_diag,) = build(lambda i: [own_diag.at(i) + y_coef.at(i) + y_before.at(i)], nb)
    diag, inverse = whole_diag(own_diag, x_coef, x_before)
    ahead, back = y_both(x0)
    (own_around,) = build(
        lambda i: [z_part.at(i) + y_coef.at(i) * ahead.at(i) + y_before.at(i) * back.at(i)], nb
    )
    own_coefs, own_before = (z_coef, y_coef), (z_before, y_before)
    (u0,) = build(
        lambda i: [
            (q.at(i) + STORAGE * x0.at(i) - (diag.at(i) * x0.at(i) - (own_around.at(i) + x_part.at(i))))
            * inverse.at(i)
        ],
        nb,
    )
    for i, b in enumerate(u0.blocks):
        early_send[i * BLOCK : (i + 1) * BLOCK] = b
    early_send[depth] = u0.side
    for dx in (-1, 1):
        @pl.when(has(dx, 0))
        def _():
            early_copy(dx).start()

    line_row = iota((rows, lanes), 0)
    taken = ((line_row == 1) & (gx + 1 < nx)) | ((line_row == rows - 2) & (gx > 0))

    def patched(value, ref, planes):
        cut = value[..., :rows, :], value[..., rows:, :]
        return jnp.concatenate([cut[0], jnp.where(taken, ref[planes], cut[1])], axis=-2)

    def patch(f, ref):
        f.blocks = [patched(b, ref, slice(i * BLOCK, (i + 1) * BLOCK)) for i, b in enumerate(f.blocks)]

    arrive_y(y_moves[2:])
    arrive_x(0)
    k, s = field(0), field(1)
    halo_mob, halo_coefs, halo_before = zy_faces(lower(k), lower(s))
    halo_diag = zy_diag(halo_coefs, halo_before)
    x_coef, x_before = x_faces(k, join(own_mob, halo_mob))
    diag, inverse = whole_diag(join(own_diag, halo_diag), x_coef, x_before)
    z_coef, y_coef = [join(f, g) for f, g in zip(own_coefs, halo_coefs)]
    z_before, y_before = [join(f, g) for f, g in zip(own_before, halo_before)]
    coefs = (z_coef, x_coef, y_coef)
    arrive_x(1)
    x0, q = field(2), field(3)
    partial = join(own_around, zy_around(lower(x0), halo_coefs, halo_before))
    u0 = start_field(x0, q, partial, x_coef, x_before, diag, inverse)
    for dx in (-1, 1):
        @pl.when(has(-dx, 0))
        def _():
            early_copy(dx).wait_recv()

    patch(u0, early_recv)
    u0.side = patched(u0.side, early_recv, depth)
    def around(v):
        partial = zy_around(v, (z_coef, y_coef), (z_before, y_before))
        return lambda i: partial.at(i) + x_around(v, x_coef, x_before, i)

    near = around(u0)
    (u1,) = build(lambda i: [u0.at(i) - near(i) * inverse.at(i)], nb)
    near = around(u1)
    sums = [0.0] * 4
    for i in range(nb):
        d, a, b = [f.blocks[i][:, :rows] for f in (diag, u0, u1)]
        da, db = d * a, d * b
        image = db - near(i)[:, :rows]
        for n, value in enumerate((da * a, da * b, db * b, b * image)):
            sums[n] = sums[n] + jnp.sum(value, axis=0)

    tile_row = iota((rows, lanes), 0)
    part = jnp.zeros((rows, lanes), jnp.float32)
    for i, value in enumerate(sums):
        part = jnp.where(tile_row == i, jnp.sum(value, axis=0, keepdims=True), part)

    late_send[...] = own(u1)

    count = nx * ny
    group = lanes // 4
    folded = part + lane_roll(part, lanes // 2)
    folded = folded + lane_roll(folded, lanes // 4)
    mine = iota((rows, lanes), 1) // group == iota((rows, lanes), 0)
    slots[0:1, :] = jnp.sum(jnp.where(mine, folded, 0.0), axis=0, keepdims=True)
    me = gx * ny + gy

    def share_copy(off, first, size):
        target = lax.rem(me + off, count)
        return pltpu.make_async_remote_copy(
            src_ref=slots.at[pl.ds(0 if size == 1 else first, size)],
            dst_ref=slots.at[pl.ds(first, size)],
            send_sem=rsend,
            recv_sem=rrecv,
            device_id={"gx": target // ny, "gy": target % ny},
            device_id_type=MESH,
        )

    pl.semaphore_wait(ready, nx - 1)
    for off in range(1, count):
        share_copy(off, off, 1).start()

    def gained(i, frac):
        return jnp.maximum(q.at(i), 0.0) + jnp.minimum(q.at(i), 0.0) * frac

    for dx in (-1, 1):
        @pl.when(has(dx, 0))
        def _():
            late_copy(dx).start()

    (frac,) = build(lambda i: [fraction(s.at(i))], nb)
    (gain,) = build(lambda i: [gained(i, frac.at(i))], nb)
    after = build(lambda i: [nxt(frac, i) for nxt in NEXT], nb)
    for dx in (-1, 1):
        @pl.when(has(-dx, 0))
        def _():
            late_copy(dx).wait_recv()

    patch(u1, late_recv)
    bases = [
        build(lambda i: [c.at(i) * (v.at(i) - nxt(v, i)) for nxt, c in zip(NEXT, coefs)], nb) for v in (x0, u0, u1)
    ]
    for dx in (-1, 1):
        @pl.when(has(dx, 0))
        def _():
            for copy in x_copies(dx):
                copy.wait_send()
            early_copy(dx).wait_send()
            late_copy(dx).wait_send()

    for dx, dy in y_moves:
        @pl.when(has(dx, dy))
        def _():
            y_copy(dx, dy).wait_send()

    share_copy(1, 1, count - 1).wait_send()
    share_copy(1, 1, count - 1).wait_recv()
    total = jnp.sum(slots[...], axis=0, keepdims=True)
    sums = jnp.sum(jnp.where(mine, total, 0.0), axis=1, keepdims=True)
    sa, sb, sc, sd = (sums[i : i + 1, :] for i in range(4))
    over_a, over_b = 1.0 / sa, 1.0 / sb
    step0 = sa * over_b
    next_energy = step0 * step0 * sc - sa
    conjugacy = next_energy * over_a
    curvature = sb - 2.0 * step0 * sc + step0 * step0 * sd
    step1 = next_energy / (curvature - conjugacy * next_energy * sb * over_a)
    weight0 = step0 + step1 * (1.0 + conjugacy)
    weight1 = -step1 * step0

    flows = [Field([], None) for _ in NEXT]

    def flux(i):
        return [x.at(i) + weight0 * a.at(i) + weight1 * b.at(i) for x, a, b in zip(*bases)]

    def water_at(i, frac, nexts):
        return [
            f.at(i) * jnp.where(f.at(i) > 0.0, frac.at(i), n) for f, n in zip(flows, nexts)
        ]

    def moved(i, current, gain, water):
        return current + STEP * add(gain, *[prv(w, i) - w.at(i) for prv, w in zip(PREV, water)])

    water = [Field([], None) for _ in NEXT]
    first = Field([], None)
    for f, value in zip(flows, flux(None)):
        f.side = value
    for w, value in zip(water, water_at(None, frac, [n.side for n in after])):
        w.side = value
    for i in range(nb):
        pressure = x0.blocks[i] + weight0 * u0.blocks[i] + weight1 * u1.blocks[i]
        out_ref[0, i * BLOCK : (i + 1) * BLOCK] = pressure[:, :rows]
        for f, value in zip(flows, flux(i)):
            f.blocks.append(value)
        for w, value in zip(water, water_at(i, frac, [n.blocks[i] for n in after])):
            w.blocks.append(value)
        first.blocks.append(moved(i, s.blocks[i], gain.blocks[i], water))
    first.side = moved(None, s.side, gain.side, water)

    (frac,) = build(lambda i: [fraction(first.at(i))], nb)
    water = [Field([], None) for _ in NEXT]
    for w, value in zip(water, water_at(None, frac, [nxt(frac, None) for nxt in NEXT])):
        w.side = value
    for i in range(nb):
        for w, value in zip(water, water_at(i, frac, [nxt(frac, i) for nxt in NEXT])):
            w.blocks.append(value)
        second = moved(i, first.blocks[i], gained(i, frac.blocks[i]), water)
        out_ref[1, i * BLOCK : (i + 1) * BLOCK] = second[:, :rows]


def local(nx, ny, permeability, saturation, pressure_old, source):
    shape = source.shape
    depth, rows, lanes = shape
    assert permeability.shape[0] == 1 and depth % BLOCK == 0 and depth * 2 * HALO == lanes and rows == 2 * HALO
    wide = rows + 2 * HALO
    f32 = jnp.float32
    dma = pltpu.SemaphoreType.DMA
    outs = pl.pallas_call(
        functools.partial(kernel, nx, ny),
        out_shape=jax.ShapeDtypeStruct((2,) + shape, f32),
        in_specs=[pl.BlockSpec(memory_space=pltpu.HBM)] * 4,
        out_specs=pl.BlockSpec(memory_space=pltpu.VMEM),
        scratch_shapes=[
            pltpu.VMEM((4, depth, wide, lanes), f32),
            pltpu.VMEM((4, rows, lanes), f32),
            pltpu.VMEM((2, 4, wide, lanes), f32),
            pltpu.VMEM((nx * ny, lanes), f32),
            pltpu.VMEM(shape, f32),
            pltpu.VMEM(shape, f32),
            pltpu.VMEM((depth + 1, rows, lanes), f32),
            pltpu.VMEM((depth + 1, rows, lanes), f32),
            dma((4,)),
            dma((8,)),
            dma((8,)),
            dma((6,)),
            dma((6,)),
            dma,
            dma,
            pltpu.SemaphoreType.REGULAR,
            dma((2,)),
            dma((2,)),
            dma((2,)),
            dma((2,)),
        ],
        compiler_params=pltpu.CompilerParams(
            collective_id=0, has_side_effects=True, vmem_limit_bytes=32 * 1024 * 1024
        ),
    )(*[pltpu.with_memory_space_constraint(v, pltpu.HBM) for v in (permeability[0], saturation[0], pressure_old[0], source)])
    return outs[:1], outs[1:]


def solution(mesh):
    wide = P(None, None, "gx", "gy")
    return jax.shard_map(
        functools.partial(local, mesh.shape["gx"], mesh.shape["gy"]),
        mesh=mesh,
        in_specs=(wide, wide, wide, P(None, "gx", "gy")),
        out_specs=(wide, wide),
        check_vma=False,
    )
```

```python
import functools

import jax
import jax.numpy as jnp
from jax import lax
from jax.experimental import pallas as pl
from jax.experimental.pallas import tpu as pltpu
from jax.sharding import PartitionSpec as P

HALO = 4
BLOCK = 2
STORAGE = 0.5
VERTICAL = 0.1
STEP = 0.05
WATER = 1.0
OIL = 2.0
MESH = pl.DeviceIdType.MESH


def iota(shape, dim):
    return lax.broadcasted_iota(jnp.int32, shape, dim)


class Field:
    def __init__(self, blocks, side):
        self.blocks, self.side = blocks, side

    def at(self, i):
        return self.side if i is None else self.blocks[i]


def row_roll(v, shift):
    axis = v.ndim - 2
    return pltpu.roll(v, shift % v.shape[axis], axis)


def lane_roll(v, shift):
    axis = v.ndim - 1
    shift = shift % v.shape[axis]
    return v if shift == 0 else pltpu.roll(v, shift, axis)


def x_next(f, i):
    return row_roll(f.at(i), -1)


def x_prev(f, i):
    return row_roll(f.at(i), 1)


def z_next(f, i):
    width = 2 * HALO
    if i is None:
        lanes = f.side.shape[1]
        return jnp.where(iota(f.side.shape, 1) < lanes - width, lane_roll(f.side, -width), 0.0)
    b = f.blocks[i]
    last = f.blocks[i + 1][:1] if i + 1 < len(f.blocks) else jnp.zeros_like(b[:1])
    return jnp.concatenate([b[1:], last], axis=0)


def z_prev(f, i):
    width = 2 * HALO
    if i is None:
        return jnp.where(iota(f.side.shape, 1) >= width, lane_roll(f.side, width), 0.0)
    b = f.blocks[i]
    first = f.blocks[i - 1][-1:] if i else jnp.zeros_like(b[:1])
    return jnp.concatenate([first, b[:-1]], axis=0)


def inserted(side, i, lane_from, lane_to):
    planes = range(i * BLOCK, (i + 1) * BLOCK)
    return jnp.stack([lane_roll(side, lane_to - (2 * HALO * z + lane_from)) for z in planes], axis=0)


def gathered(blocks, lane_from, lane_to, base):
    width = 2 * HALO
    lane = iota(base.shape, 1)
    for i, b in enumerate(blocks):
        for j in range(BLOCK):
            to = width * (i * BLOCK + j) + lane_to
            base = jnp.where(lane == to, lane_roll(b[j], to - lane_from), base)
    return base


def y_next(f, i):
    if i is None:
        return gathered(f.blocks, 0, 2 * HALO - 1, lane_roll(f.side, -1))
    b = f.blocks[i]
    lanes = b.shape[2]
    return jnp.where(iota(b.shape, 2) == lanes - 1, inserted(f.side, i, 0, lanes - 1), lane_roll(b, -1))


def y_prev(f, i):
    if i is None:
        return gathered(f.blocks, f.blocks[0].shape[2] - 1, 0, lane_roll(f.side, 1))
    b = f.blocks[i]
    return jnp.where(iota(b.shape, 2) == 0, inserted(f.side, i, 2 * HALO - 1, 0), lane_roll(b, 1))


def inverted(v):
    r = pl.reciprocal(v, approx=True)
    r = r * (2.0 - v * r)
    return r * (2.0 - v * r)


def y_both(f):
    width = 2 * HALO
    side = f.side
    lane = iota(side.shape, 1)
    column = lane % width
    edges = jnp.where(column == 0, lane_roll(side, 1 - width), lane_roll(side, -1))
    ends = jnp.zeros_like(side)
    nexts, prevs = [], []
    for i, b in enumerate(f.blocks):
        put = jnp.stack([lane_roll(edges, -width * (i * BLOCK + j)) for j in range(BLOCK)], axis=0)
        at_lane = iota(b.shape, 2)
        up = lane_roll(b, 1)
        nexts.append(jnp.where(at_lane == b.shape[2] - 1, put, lane_roll(b, -1)))
        prevs.append(jnp.where(at_lane == 0, put, up))
        for j in range(BLOCK):
            z = i * BLOCK + j
            ends = jnp.where(lane // width == z, lane_roll(up[j], width * z), ends)
    side_next = jnp.where(column == width - 1, lane_roll(ends, width - 2), lane_roll(side, -1))
    side_prev = jnp.where(column == 0, ends, lane_roll(side, 1))
    return Field(nexts, side_next), Field(prevs, side_prev)


def mobility(s):
    return s * s / WATER + (1.0 - s) * (1.0 - s) / OIL


def fraction(s):
    water = s * s / WATER
    return water * inverted(water + (1.0 - s) * (1.0 - s) / OIL)


def coefficient(scaling):
    def fn(ka, kb, ma, mb):
        return (scaling * ka * kb) * inverted(jnp.maximum(ka + kb, 1e-20)) * (ma + mb)

    return fn


NEXT = (z_next, x_next, y_next)
PREV = (z_prev, x_prev, y_prev)


def build(fn, count):
    side = fn(None)
    blocks = [fn(i) for i in range(count)]
    return [Field([b[n] for b in blocks], side[n]) for n in range(len(side))]


def add(*terms):
    total = terms[0]
    for t in terms[1:]:
        total = total + t
    return total


def packed(own):
    depth, rows, lanes = own.shape
    width = 2 * HALO
    edge = jnp.where(iota(own.shape, 2) < HALO, own, lane_roll(own, width))
    block = iota((rows, lanes), 1) // width
    out = edge[0]
    for z in range(1, depth):
        out = jnp.where(block == z, lane_roll(edge[z], width * z), out)
    return out


def kernel(nx, ny, k_in, s_in, x_in, q_in, out_ref, main_ref, pack_ref, side_ref, slots,
           late_send, late_recv, early_send, early_recv, load_sem, xsend, xrecv, psend, precv, rsend, rrecv, ready, lsem, lrecv, esem, erecv):
    gx, gy = lax.axis_index("gx"), lax.axis_index("gy")
    ins = (k_in, s_in, x_in, q_in)
    rows = k_in.shape[1]
    wide = rows + 2 * HALO

    def has(dx, dy):
        ok = None
        for d, at, n in ((dx, gx, nx), (dy, gy, ny)):
            if d:
                one = at + d >= 0 if d < 0 else at + d < n
                ok = one if ok is None else ok & one
        return ok

    def at(dx, dy):
        return {"gx": gx + dx, "gy": gy + dy}

    diagonals = [(dx, dy) for dx in (-1, 1) for dy in (-1, 1)]

    loads = [pltpu.make_async_copy(ref, main_ref.at[i, :, pl.ds(0, rows)], load_sem.at[i]) for i, ref in enumerate(ins)]
    for copy in loads:
        copy.start()

    barrier = pltpu.get_barrier_semaphore()
    expected = jnp.int32(nx - 1 + ny - 1)
    for off in range(1, nx):
        pl.semaphore_signal(barrier, inc=1, device_id={"gx": lax.rem(gx + off, nx), "gy": gy}, device_id_type=MESH)
    for off in range(1, ny):
        pl.semaphore_signal(barrier, inc=1, device_id={"gx": gx, "gy": lax.rem(gy + off, ny)}, device_id_type=MESH)
    for dx, dy in diagonals:
        @pl.when(has(dx, dy))
        def _():
            pl.semaphore_signal(barrier, inc=1, device_id=at(dx, dy), device_id_type=MESH)

        expected = expected + has(dx, dy).astype(jnp.int32)

    reach = (2, 2, 2, 1)

    def edge_rows(dx, width):
        return pl.ds(0, width) if dx < 0 else pl.ds(rows - width, width)

    def halo_rows(dx, width):
        return pl.ds(rows, width) if dx < 0 else pl.ds(wide - width, width)

    def x_copies(dx, halves=(0, 1)):
        d = (dx + 1) // 2
        groups = (pl.ds(0, 2), None, pl.ds(2, 1), pl.ds(3, 1))
        return [
            pltpu.make_async_remote_copy(
                src_ref=main_ref.at[groups[i], :, edge_rows(dx, reach[i])],
                dst_ref=main_ref.at[groups[i], :, halo_rows(dx, reach[i])],
                send_sem=xsend.at[d * len(ins) + i],
                recv_sem=xrecv.at[d * len(ins) + i],
                device_id=at(dx, 0),
                device_id_type=MESH,
            )
            for i in range(len(ins))
            if i // 2 in halves and groups[i] is not None
        ]

    def y_copy(dx, dy):
        number = (dx + 1) * 2 + (dy + 1) // 2
        from_rows = to_rows = pl.ds(0, rows)
        if dx:
            from_rows, to_rows = edge_rows(dx, reach[0]), halo_rows(dx, reach[0])
        return pltpu.make_async_remote_copy(
            src_ref=pack_ref.at[:, from_rows],
            dst_ref=side_ref.at[(1 - dy) // 2, :, to_rows],
            send_sem=psend.at[number],
            recv_sem=precv.at[number],
            device_id=at(dx, dy),
            device_id_type=MESH,
        )

    def line_copy(dx, src, dst, send, recv):
        line = pl.ds(1, 1) if dx < 0 else pl.ds(rows - 2, 1)
        d = (dx + 1) // 2
        return pltpu.make_async_remote_copy(
            src_ref=src.at[:, line],
            dst_ref=dst.at[:, line],
            send_sem=send.at[d],
            recv_sem=recv.at[d],
            device_id=at(dx, 0),
            device_id_type=MESH,
        )

    def early_copy(dx):
        return line_copy(dx, early_send, early_recv, esem, erecv)

    def late_copy(dx):
        return line_copy(dx, late_send, late_recv, lsem, lrecv)

    y_moves = [(0, 1), (0, -1)] + diagonals

    for i in range(len(ins)):
        loads[i].wait()
        pack_ref[i] = packed(main_ref[i, :, 0:rows, :])

    pl.semaphore_wait(barrier, expected)
    for half, moves in enumerate((y_moves[:2], y_moves[2:])):
        for dx, dy in moves:
            @pl.when(has(dx, dy))
            def _():
                y_copy(dx, dy).start()

        for dx in (-1, 1):
            @pl.when(has(dx, 0))
            def _():
                for copy in x_copies(dx, (half,)):
                    copy.start()

    for off in range(1, nx):
        pl.semaphore_signal(ready, inc=1, device_id={"gx": lax.rem(gx + off, nx), "gy": gy}, device_id_type=MESH)

    def arrive_y(moves):
        for dx, dy in moves:
            @pl.when(has(-dx, -dy))
            def _():
                y_copy(dx, dy).wait_recv()

    def arrive_x(half):
        for dx in (-1, 1):
            @pl.when(has(-dx, 0))
            def _():
                for copy in x_copies(dx, (half,)):
                    copy.wait_recv()

    lanes = k_in.shape[2]
    depth = k_in.shape[0]
    row = iota((wide, lanes), 0)
    lane = iota((wide, lanes), 1)
    right = lane % (2 * HALO) < HALO

    nb = depth // BLOCK

    def inside(i, high):
        at_row = row[:high]
        return (
            (at_row < rows)
            | ((at_row < rows + reach[i]) & (gx + 1 < nx))
            | ((at_row >= wide - reach[i]) & (gx > 0))
        )

    def side_field(i, high):
        here, at_right = inside(i, high), right[:high]
        inside_right = at_right & here & (gy + 1 < ny)
        inside_left = jnp.logical_not(at_right) & here & (gy > 0)
        return jnp.where(
            inside_right, side_ref[1, i, 0:high], jnp.where(inside_left, side_ref[0, i, 0:high], 0.0)
        )

    def field(i):
        here = inside(i, wide)[None]
        blocks = [jnp.where(here, main_ref[i, n * BLOCK : (n + 1) * BLOCK], 0.0) for n in range(nb)]
        return Field(blocks, side_field(i, wide))

    def own(f):
        return jnp.concatenate([b[:, :rows] for b in f.blocks], axis=0)

    def zy_faces(k, s):
        (mob,) = build(lambda i: [mobility(s.at(i))], nb)
        coefs = [Field([], None) for _ in range(2)]
        before = [Field([], None) for _ in range(2)]

        def face(i):
            return [
                coefficient(sc)(k.at(i), nxt(k, i), mob.at(i), nxt(mob, i))
                for nxt, sc in ((z_next, VERTICAL), (y_next, 1.0))
            ]

        def behind(i):
            return [prv(c, i) for prv, c in zip((z_prev, y_prev), coefs)]

        for c, value in zip(coefs, face(None)):
            c.side = value
        for i in range(nb):
            for c, value in zip(coefs, face(i)):
                c.blocks.append(value)
            for c, value in zip(before, behind(i)):
                c.blocks.append(value)
        for c, value in zip(before, behind(None)):
            c.side = value
        return mob, coefs, before

    def x_faces(k, mob):
        (c,) = build(
            lambda i: [coefficient(1.0)(k.at(i), x_next(k, i), mob.at(i), x_next(mob, i))], nb
        )
        (b,) = build(lambda i: [x_prev(c, i)], nb)
        return c, b

    def zy_diag(coefs, before):
        return build(lambda i: [add(STORAGE, *[f.at(i) for f in coefs + before])], nb)[0]

    def zy_around(v, coefs, before):
        ahead, back = y_both(v)
        return build(
            lambda i: [
                coefs[0].at(i) * z_next(v, i)
                + before[0].at(i) * z_prev(v, i)
                + coefs[1].at(i) * ahead.at(i)
                + before[1].at(i) * back.at(i)
            ],
            nb,
        )[0]

    def x_around(v, c, b, i):
        return c.at(i) * x_next(v, i) + b.at(i) * x_prev(v, i)

    def whole_diag(partial, c, b):
        return build(lambda i: (lambda d: [d, inverted(d)])(partial.at(i) + c.at(i) + b.at(i)), nb)

    def start_field(x0, q, partial, c, b, diag, inverse):
        return build(
            lambda i: [
                (q.at(i) + STORAGE * x0.at(i) - (diag.at(i) * x0.at(i) - (partial.at(i) + x_around(x0, c, b, i))))
                * inverse.at(i)
            ],
            nb,
        )[0]

    def lower(f):
        return Field([b[:, rows:] for b in f.blocks], f.side[rows:])

    def join(f, g):
        return Field(
            [jnp.concatenate([a, b], axis=1) for a, b in zip(f.blocks, g.blocks)],
            jnp.concatenate([f.side, g.side], axis=0),
        )

    each = range(nb)
    k, s, x0, q = (Field([main_ref[i, n * BLOCK : (n + 1) * BLOCK, 0:rows] for n in each], None) for i in range(4))
    own_mob = Field([mobility(b) for b in s.blocks], None)

    def face_at(nxt, scaling, i):
        return coefficient(scaling)(k.at(i), nxt(k, i), own_mob.at(i), nxt(own_mob, i))

    z_coef = Field([face_at(z_next, VERTICAL, i) for i in each], None)
    z_before = Field([z_prev(z_coef, i) for i in each], None)
    x_coef = Field([face_at(x_next, 1.0, i) for i in each], None)
    x_before = Field([x_prev(x_coef, i) for i in each], None)

    def z_around(i):
        return z_coef.at(i) * z_next(x0, i) + z_before.at(i) * z_prev(x0, i)

    def z_diag(i):
        return STORAGE + z_coef.at(i) + z_before.at(i)

    z_part = Field([z_around(i) for i in each], None)
    x_part = Field([x_around(x0, x_coef, x_before, i) for i in each], None)
    own_diag = Field([z_diag(i) for i in each], None)

    arrive_y(y_moves[:2])
    for i, f in enumerate((k, s, x0, q)):
        f.side = side_field(i, rows)
    own_mob.side = mobility(s.side)
    z_coef.side = face_at(z_next, VERTICAL, None)
    z_before.side = z_prev(z_coef, None)
    x_coef.side = face_at(x_next, 1.0, None)
    x_before.side = x_prev(x_coef, None)
    z_part.side = z_around(None)
    x_part.side = x_around(x0, x_coef, x_before, None)
    own_diag.side = z_diag(None)
    (y_coef,) = build(lambda i: [face_at(y_next, 1.0, i)], nb)
    (y_before,) = build(lambda i: [y_prev(y_coef, i)], nb)
    (own_diag,) = build(lambda i: [own_diag.at(i) + y_coef.at(i) + y_before.at(i)], nb)
    diag, inverse = whole_diag(own_diag, x_coef, x_before)
    ahead, back = y_both(x0)
    (own_around,) = build(
        lambda i: [z_part.at(i) + y_coef.at(i) * ahead.at(i) + y_before.at(i) * back.at(i)], nb
    )
    own_coefs, own_before = (z_coef, y_coef), (z_before, y_before)
    (u0,) = build(
        lambda i: [
            (q.at(i) + STORAGE * x0.at(i) - (diag.at(i) * x0.at(i) - (own_around.at(i) + x_part.at(i))))
            * inverse.at(i)
        ],
        nb,
    )
    for i, b in enumerate(u0.blocks):
        early_send[i * BLOCK : (i + 1) * BLOCK] = b
    early_send[depth] = u0.side
    for dx in (-1, 1):
        @pl.when(has(dx, 0))
        def _():
            early_copy(dx).start()

    line_row = iota((rows, lanes), 0)
    taken = ((line_row == 1) & (gx + 1 < nx)) | ((line_row == rows - 2) & (gx > 0))

    def patched(value, ref, planes):
        cut = value[..., :rows, :], value[..., rows:, :]
        return jnp.concatenate([cut[0], jnp.where(taken, ref[planes], cut[1])], axis=-2)

    def patch(f, ref):
        f.blocks = [patched(b, ref, slice(i * BLOCK, (i + 1) * BLOCK)) for i, b in enumerate(f.blocks)]

    arrive_y(y_moves[2:])
    arrive_x(0)
    k, s = field(0), field(1)
    halo_mob, halo_coefs, halo_before = zy_faces(lower(k), lower(s))
    halo_diag = zy_diag(halo_coefs, halo_before)
    x_coef, x_before = x_faces(k, join(own_mob, halo_mob))
    diag, inverse = whole_diag(join(own_diag, halo_diag), x_coef, x_before)
    z_coef, y_coef = [join(f, g) for f, g in zip(own_coefs, halo_coefs)]
    z_before, y_before = [join(f, g) for f, g in zip(own_before, halo_before)]
    coefs = (z_coef, x_coef, y_coef)
    arrive_x(1)
    x0, q = field(2), field(3)
    partial = join(own_around, zy_around(lower(x0), halo_coefs, halo_before))
    u0 = start_field(x0, q, partial, x_coef, x_before, diag, inverse)
    for dx in (-1, 1):
        @pl.when(has(-dx, 0))
        def _():
            early_copy(dx).wait_recv()

    patch(u0, early_recv)
    u0.side = patched(u0.side, early_recv, depth)
    def around(v):
        partial = zy_around(v, (z_coef, y_coef), (z_before, y_before))
        return lambda i: partial.at(i) + x_around(v, x_coef, x_before, i)

    near = around(u0)
    (u1,) = build(lambda i: [u0.at(i) - near(i) * inverse.at(i)], nb)
    near = around(u1)
    sums = [0.0] * 4
    for i in range(nb):
        d, a, b = [f.blocks[i][:, :rows] for f in (diag, u0, u1)]
        da, db = d * a, d * b
        image = db - near(i)[:, :rows]
        for n, value in enumerate((da * a, da * b, db * b, b * image)):
            sums[n] = sums[n] + jnp.sum(value, axis=0)

    tile_row = iota((rows, lanes), 0)
    part = jnp.zeros((rows, lanes), jnp.float32)
    for i, value in enumerate(sums):
        part = jnp.where(tile_row == i, jnp.sum(value, axis=0, keepdims=True), part)

    late_send[...] = own(u1)

    count = nx * ny
    group = lanes // 4
    folded = part + lane_roll(part, lanes // 2)
    folded = folded + lane_roll(folded, lanes // 4)
    mine = iota((rows, lanes), 1) // group == iota((rows, lanes), 0)
    slots[0:1, :] = jnp.sum(jnp.where(mine, folded, 0.0), axis=0, keepdims=True)
    me = gx * ny + gy

    def share_copy(off, first, size):
        target = lax.rem(me + off, count)
        return pltpu.make_async_remote_copy(
            src_ref=slots.at[pl.ds(0 if size == 1 else first, size)],
            dst_ref=slots.at[pl.ds(first, size)],
            send_sem=rsend,
            recv_sem=rrecv,
            device_id={"gx": target // ny, "gy": target % ny},
            device_id_type=MESH,
        )

    pl.semaphore_wait(ready, nx - 1)
    for off in range(1, count):
        share_copy(off, off, 1).start()

    def gained(i, frac):
        return jnp.maximum(q.at(i), 0.0) + jnp.minimum(q.at(i), 0.0) * frac

    for dx in (-1, 1):
        @pl.when(has(dx, 0))
        def _():
            late_copy(dx).start()

    (frac,) = build(lambda i: [fraction(s.at(i))], nb)
    (gain,) = build(lambda i: [gained(i, frac.at(i))], nb)
    after = build(lambda i: [nxt(frac, i) for nxt in NEXT], nb)
    for dx in (-1, 1):
        @pl.when(has(-dx, 0))
        def _():
            late_copy(dx).wait_recv()

    patch(u1, late_recv)
    bases = [
        build(lambda i: [c.at(i) * (v.at(i) - nxt(v, i)) for nxt, c in zip(NEXT, coefs)], nb) for v in (x0, u0, u1)
    ]
    for dx in (-1, 1):
        @pl.when(has(dx, 0))
        def _():
            for copy in x_copies(dx):
                copy.wait_send()
            early_copy(dx).wait_send()
            late_copy(dx).wait_send()

    for dx, dy in y_moves:
        @pl.when(has(dx, dy))
        def _():
            y_copy(dx, dy).wait_send()

    share_copy(1, 1, count - 1).wait_send()
    share_copy(1, 1, count - 1).wait_recv()
    total = jnp.sum(slots[...], axis=0, keepdims=True)
    sums = jnp.sum(jnp.where(mine, total, 0.0), axis=1, keepdims=True)
    sa, sb, sc, sd = (sums[i : i + 1, :] for i in range(4))
    over_a, over_b = 1.0 / sa, 1.0 / sb
    step0 = sa * over_b
    next_energy = step0 * step0 * sc - sa
    conjugacy = next_energy * over_a
    curvature = sb - 2.0 * step0 * sc + step0 * step0 * sd
    step1 = next_energy / (curvature - conjugacy * next_energy * sb * over_a)
    weight0 = step0 + step1 * (1.0 + conjugacy)
    weight1 = -step1 * step0

    flows = [Field([], None) for _ in NEXT]

    def flux(i):
        return [x.at(i) + weight0 * a.at(i) + weight1 * b.at(i) for x, a, b in zip(*bases)]

    def water_at(i, frac, nexts):
        return [
            f.at(i) * jnp.where(f.at(i) > 0.0, frac.at(i), n) for f, n in zip(flows, nexts)
        ]

    def moved(i, current, gain, water):
        return current + STEP * add(gain, *[prv(w, i) - w.at(i) for prv, w in zip(PREV, water)])

    water = [Field([], None) for _ in NEXT]
    first = Field([], None)
    for f, value in zip(flows, flux(None)):
        f.side = value
    for w, value in zip(water, water_at(None, frac, [n.side for n in after])):
        w.side = value
    for i in range(nb):
        pressure = x0.blocks[i] + weight0 * u0.blocks[i] + weight1 * u1.blocks[i]
        out_ref[0, i * BLOCK : (i + 1) * BLOCK] = pressure[:, :rows]
        for f, value in zip(flows, flux(i)):
            f.blocks.append(value)
        for w, value in zip(water, water_at(i, frac, [n.blocks[i] for n in after])):
            w.blocks.append(value)
        first.blocks.append(moved(i, s.blocks[i], gain.blocks[i], water))
    first.side = moved(None, s.side, gain.side, water)

    (frac,) = build(lambda i: [fraction(first.at(i))], nb)
    water = [Field([], None) for _ in NEXT]
    for w, value in zip(water, water_at(None, frac, [nxt(frac, None) for nxt in NEXT])):
        w.side = value
    for i in range(nb):
        for w, value in zip(water, water_at(i, frac, [nxt(frac, i) for nxt in NEXT])):
            w.blocks.append(value)
        second = moved(i, first.blocks[i], gained(i, frac.blocks[i]), water)
        out_ref[1, i * BLOCK : (i + 1) * BLOCK] = second[:, :rows]


def local(nx, ny, permeability, saturation, pressure_old, source):
    shape = source.shape
    depth, rows, lanes = shape
    assert permeability.shape[0] == 1 and depth % BLOCK == 0 and depth * 2 * HALO == lanes and rows == 2 * HALO
    wide = rows + 2 * HALO
    f32 = jnp.float32
    dma = pltpu.SemaphoreType.DMA
    outs = pl.pallas_call(
        functools.partial(kernel, nx, ny),
        out_shape=jax.ShapeDtypeStruct((2,) + shape, f32),
        in_specs=[pl.BlockSpec(memory_space=pltpu.HBM)] * 4,
        out_specs=pl.BlockSpec(memory_space=pltpu.VMEM),
        scratch_shapes=[
            pltpu.VMEM((4, depth, wide, lanes), f32),
            pltpu.VMEM((4, rows, lanes), f32),
            pltpu.VMEM((2, 4, wide, lanes), f32),
            pltpu.VMEM((nx * ny, lanes), f32),
            pltpu.VMEM(shape, f32),
            pltpu.VMEM(shape, f32),
            pltpu.VMEM((depth + 1, rows, lanes), f32),
            pltpu.VMEM((depth + 1, rows, lanes), f32),
            dma((4,)),
            dma((8,)),
            dma((8,)),
            dma((6,)),
            dma((6,)),
            dma,
            dma,
            pltpu.SemaphoreType.REGULAR,
            dma((2,)),
            dma((2,)),
            dma((2,)),
            dma((2,)),
        ],
        compiler_params=pltpu.CompilerParams(
            collective_id=0, has_side_effects=True, vmem_limit_bytes=32 * 1024 * 1024
        ),
    )(*[pltpu.with_memory_space_constraint(v, pltpu.HBM) for v in (permeability[0], saturation[0], pressure_old[0], source)])
    return outs[:1], outs[1:]


def solution(mesh):
    wide = P(None, None, "gx", "gy")
    return jax.shard_map(
        functools.partial(local, mesh.shape["gx"], mesh.shape["gy"]),
        mesh=mesh,
        in_specs=(wide, wide, wide, P(None, "gx", "gy")),
        out_specs=(wide, wide),
        check_vma=False,
    )
```
